256 devices in a mesh: tile: 64 (over y, z, core), band: 4 (over x).
Axes of the slice: x: 4, y: 4, z: 8, core: 2. Of those that a mesh axis runs over, the one named last changes fastest.
Arguments:
- params: float32 [2048, 44], P(('tile', 'band')), may hold values from -4 to 4
- offsets: int32 [2048, 2], P(('tile', 'band')), may hold values from -32 to 351
- counts: int32 [256], P(('tile', 'band')), may hold values from 1 to 8, 1153 in all
- image: float32 [64, 5, 384, 384], P('tile'), may hold values from 0.25 to 4
- background: float32 [64, 5], P('tile'), may hold values from 0.5 to 2
- psf_y: float32 [5, 25], replicated, may hold values from 0.02 to 0.1
- psf_x: float32 [5, 25], replicated, may hold values from 0.02 to 0.1
Outputs:
- gradient: float32 [2048, 44], P(('tile', 'band'))
The draws below stay inside these ranges and needn't reach their ends.
All inputs are finite; a program needn't handle non-finite values. No bound on the sum of `counts` on one device may be relied on, other than what follows from the above.
Results may differ from the reference program's by a relative error of at most 0.0001.
Values sent between devices are 32-bit elements; how exact they have to be, the bound alone decides.
A program may use at most 192 MiB of HBM per device.

```python
import math
import jax
import jax.numpy as jnp
import numpy as np
from jax import lax

BANDS = 5
COMPONENTS = 12
PARAMS = 44
PATCH = 64
PSF_TAPS = 25
TILE_COLS = 8
TILE_SIDE = 384
SRC_DEV = 8
TILES = 64
SOURCES = 2048
LIVE_TOTAL = 1153
N_BAND = 4
DEVICES = 256


def set_ends(values, own_key, smallest, top_value):
    longest = values.shape.index(max(values.shape))
    spots = []
    for shift in (0, 1):
        where = [jax.random.randint(jax.random.fold_in(own_key, axis), (), 0, length) for axis, length in enumerate(values.shape)]
        where[longest] = (where[longest] + shift) % values.shape[longest]
        spots.append(tuple(where))
    return values.at[spots[0]].set(smallest).at[spots[1]].set(top_value)


def level_of(rng, shape, pieces, least, top_value):
    def one(dim, parts):
        heights = jax.random.uniform(jax.random.fold_in(jax.random.fold_in(rng, 6), dim), (parts,), jnp.float32, least / len(pieces), top_value / len(pieces))
        return jnp.repeat(jnp.exp(heights), shape[dim] // parts).reshape((-1,) + (1,) * (len(shape) - dim - 1))

    loudness = one(*pieces[0])
    for cut in pieces[1:]:
        loudness = loudness * one(*cut)
    return loudness


def split_up(count, total, limit, skew):
    loads = [(1 << 20) // math.isqrt(grade ** skew) + 1 for grade in range(2, count + 1)]
    spare, given = total - limit - (count - 1), [1] * (count - 1)
    while spare > 0:
        free = [i for i in range(count - 1) if given[i] < limit]
        whole, left = sum([loads[i] for i in free]), spare
        for i in free:
            extra = min(limit - given[i], max(1, left * loads[i] // whole), spare)
            given[i] = given[i] + extra
            spare = spare - extra
    return np.array([limit] + given)


def uneven_parts(key, amount, total, reach, skew):
    if amount == 2:
        one = jax.random.randint(key, (), max(1, total - reach), min(reach, total - 1) + 1)
        return jnp.stack([one, total - one])
    tallies = jnp.asarray(split_up(amount, total, reach, skew), jnp.int32)
    couples = (amount - 1) // 2
    giver, taker = tallies[1:1 + 2 * couples:2], tallies[2:2 + 2 * couples:2]
    slack = jnp.minimum(giver - 1, reach - taker)
    passed = jax.random.randint(jax.random.fold_in(key, 1), (couples,), 0, 1 << 20) % (slack + 1)
    tallies = tallies.at[1:1 + 2 * couples:2].set(giver - passed).at[2:2 + 2 * couples:2].set(taker + passed)
    return tallies[jax.random.permutation(jax.random.fold_in(key, 2), amount)]


def gaussian(stream_key, shape, scale, reach, shards=(), kind=jnp.bfloat16):
    gain = level_of(stream_key, shape, shards, -0.22, 0.18) if shards else 1.0
    values = jax.random.normal(stream_key, shape, jnp.float32) * scale * gain
    return jnp.minimum(jnp.maximum(values, -reach), reach).astype(kind)


def setup_inputs(seed: int = 0) -> dict:
    splits = jax.random.split(jax.random.key(seed), 8)
    return {
        "params": gaussian(splits[0], (SOURCES, PARAMS), 1.0, 4.0, ((0, 256),), jnp.float32),
        "offsets": set_ends(jax.random.randint(splits[1], (SOURCES, 2), 0 - PATCH // 2, TILE_SIDE - PATCH // 2), jax.random.fold_in(splits[1], 1), 0 - PATCH // 2, (TILE_SIDE - PATCH // 2) - 1).astype(jnp.int32),
        "counts": uneven_parts(splits[2], DEVICES, LIVE_TOTAL, SRC_DEV, 2).astype(jnp.int32),
        "image": jnp.clip(jnp.exp(math.log(4.0) - 2.7725887 * jax.random.uniform(splits[3], (TILES, BANDS, TILE_SIDE, TILE_SIDE), jnp.float32) ** level_of(splits[3], (TILES, BANDS, TILE_SIDE, TILE_SIDE), ((0, 64),), -0.2, 0.2)), 0.25, 4.0),
        "background": jnp.clip(jnp.exp(math.log(2.0) - 1.3862944 * jax.random.uniform(splits[4], (TILES, BANDS), jnp.float32) ** level_of(splits[4], (TILES, BANDS), ((0, 64),), -0.2, 0.2)), 0.5, 2.0),
        "psf_y": jnp.clip(jnp.exp(jax.random.uniform(splits[5], (BANDS, PSF_TAPS), jnp.float32, math.log(0.02), math.log(0.1))), 0.02, 0.1),
        "psf_x": jnp.clip(jnp.exp(jax.random.uniform(splits[6], (BANDS, PSF_TAPS), jnp.float32, math.log(0.02), math.log(0.1))), 0.02, 0.1),
    }


flux_scale = 2.0
prior_weight = 0.1
highest = lax.Precision.HIGHEST

def toeplitz_table(psf_taps):
    taps = psf_taps.shape[1]
    half = taps // 2
    places = jnp.arange(PATCH, dtype=jnp.int32)
    lag_grid = places[None, :] - places[:, None] + half
    onehot = (lag_grid[:, :, None] == jnp.arange(taps, dtype=jnp.int32)[None, None, :]).astype(jnp.float32)
    return jnp.einsum('bt,pit->bpi', psf_taps, onehot, precision=highest)

def render_factors(params, live, psf_y, psf_x):
    count = params.shape[0]
    centre = jnp.arange(PATCH, dtype=jnp.float32) + 0.5 - PATCH / 2.0
    softness = jnp.exp(0.25 * params[:, PARAMS - 1])
    comps = params[:, BANDS + 2:BANDS + 2 + 3 * COMPONENTS].reshape(count, COMPONENTS, 3)
    weights = jax.nn.softmax(comps[:, :, 0], axis=-1)
    factors = []
    for column in range(2):
        offset_pos = PATCH / 16.0 * jnp.tanh(params[:, BANDS + column])
        spread = (0.5 + jax.nn.softplus(comps[:, :, 1 + column])) * (PATCH / 32.0) * softness[:, None]
        profile = jnp.exp(-jnp.square(centre[None, None, :] - offset_pos[:, None, None]) / (2.0 * jnp.square(spread))[:, :, None])
        table = toeplitz_table(psf_y if column == 0 else psf_x)
        factors.append(jnp.einsum('bpi,ski->sbkp', table, profile, precision=highest))
    flux = jax.nn.softplus(params[:, :BANDS]) * flux_scale * live[:, None]
    coef = flux[:, :, None] * weights[:, None, :]
    return (factors[0], factors[1], coef)

def reference(params, offsets, counts, image, background, psf_y, psf_x):
    count = params.shape[0]
    numbers = jnp.arange(count, dtype=jnp.int32)
    device = numbers // SRC_DEV
    tile = (device // N_BAND + TILES // 2) % TILES
    live = (numbers % SRC_DEV < counts[device]).astype(jnp.float32)
    tile_rows = TILES // TILE_COLS
    height = tile_rows * TILE_SIDE
    width = TILE_COLS * TILE_SIDE
    top = (tile // TILE_COLS * TILE_SIDE + offsets[:, 0] + PATCH).astype(jnp.int32)
    left = (tile % TILE_COLS * TILE_SIDE + offsets[:, 1] + PATCH).astype(jnp.int32)
    factor_y, factor_x, coef = render_factors(params, live, psf_y, psf_x)
    zero = jnp.zeros((), jnp.int32)

    def place(number, canvas):
        patch = jnp.einsum('bk,bkp,bkq->bpq', coef[number], factor_y[number], factor_x[number], precision=highest)
        start = (zero, top[number], left[number])
        current = lax.dynamic_slice(canvas, start, (BANDS, PATCH, PATCH))
        return lax.dynamic_update_slice(canvas, current + patch, start)
    canvas = jnp.zeros((BANDS, height + 2 * PATCH, width + 2 * PATCH), jnp.float32)
    canvas = lax.fori_loop(0, count, place, canvas)
    sky = canvas[:, PATCH:PATCH + height, PATCH:PATCH + width]
    observed = image.reshape(tile_rows, TILE_COLS, BANDS, TILE_SIDE, TILE_SIDE).transpose(2, 0, 3, 1, 4).reshape(BANDS, height, width)
    floor_sky = background.reshape(tile_rows, TILE_COLS, BANDS).transpose(2, 0, 1)
    floor_full = jnp.repeat(jnp.repeat(floor_sky, TILE_SIDE, axis=1), TILE_SIDE, axis=2)
    model = floor_full + sky
    residual = (observed / model - 1.0) / (PATCH * PATCH)
    padded = jnp.pad(residual, ((0, 0), (PATCH, PATCH), (PATCH, PATCH)))

    def pull(number):
        window = lax.dynamic_slice(padded, (zero, top[number], left[number]), (BANDS, PATCH, PATCH))
        along_y = jnp.einsum('bpq,bkq->bkp', window, factor_x[number], precision=highest)
        along_x = jnp.einsum('bpq,bkp->bkq', window, factor_y[number], precision=highest)
        d_coef = lax.optimization_barrier(jnp.sum(along_y * factor_y[number], axis=-1))
        return (coef[number][:, :, None] * along_y, coef[number][:, :, None] * along_x, d_coef)
    d_y, d_x, d_coef = lax.map(pull, numbers)
    _, pullback = jax.vjp(lambda theta: render_factors(theta, live, psf_y, psf_x), params)
    grad, = pullback((d_y, d_x, d_coef))
    return grad - prior_weight * params * live[:, None]
```

```python
import functools

import jax
import jax.numpy as jnp
from jax import lax
from jax.experimental import pallas as pl
from jax.experimental.pallas import tpu as pltpu
from jax.sharding import PartitionSpec as P

BANDS = 5
COMPONENTS = 12
PARAMS = 44
PATCH = 64
TAPS = 25
HALF = TAPS // 2
TILE_COLS = 8
TILE_SIDE = 384
QUAD = TILE_SIDE // 2
SRC = 8
TILES = 64
N_BAND = 4
PARTNERS = 16
SLOTS = PARTNERS * SRC
LANES = 128

TOP, LEFT, LIVE = 8, 9, 10
WEIGHT, SPREAD_Y, SPREAD_X = 16, 32, 48

PER_CHUNK = 21
COLS = 256
CHUNKS = -(-SLOTS // PER_CHUNK)
SPAN = 224

flux_scale = 2.0
prior_weight = 0.1
highest = lax.Precision.HIGHEST
f32 = jnp.float32
bf16 = jnp.bfloat16
MESH = pl.DeviceIdType.MESH


def iota(shape, axis):
    return lax.broadcasted_iota(jnp.int32, shape, axis)


def dot(a, b, dims=((1,), (0,)), precision=None):
    return lax.dot_general(a, b, (dims, ((), ())), precision=precision, preferred_element_type=f32)


def halves(x):
    high = x.astype(bf16)
    return high, (x - high.astype(f32)).astype(bf16)


def dot3(a, b, dims=((1,), (0,))):
    return dot(a[0], b[0], dims) + (dot(a[0], b[1], dims) + dot(a[1], b[0], dims))


def wrapped_tile(row, col):
    return lax.rem(row + TILE_COLS, TILE_COLS) * TILE_COLS + lax.rem(col + TILE_COLS, TILE_COLS)


def viewers(tile, band):
    home = lax.rem(tile + TILES // 2, TILES)
    row, col = home // TILE_COLS, lax.rem(home, TILE_COLS)
    found = []
    for step_y, half_y in ((0, 0), (0, 1), (1, 0), (-1, 1)):
        for step_x, half_x in ((0, 0), (0, 1), (1, 0), (-1, 1)):
            far = 2 * abs(step_y) + abs(step_x)
            answer = (2 * abs(step_y) + half_y) * 4 + 2 * abs(step_x) + half_x
            found.append(
                (wrapped_tile(row + step_y, col + step_x), 2 * half_y + half_x, far * N_BAND + band, answer)
            )
    return found


def owners(tile, band):
    row, col = tile // TILE_COLS, lax.rem(tile, TILE_COLS)
    half_y, half_x = band // 2, lax.rem(band, 2)
    found = []
    for far_y in range(2):
        for far_x in range(2):
            home = wrapped_tile(row + far_y * (2 * half_y - 1), col + far_x * (2 * half_x - 1))
            holder = lax.rem(home + TILES // 2, TILES)
            answer = (2 * far_y + half_y) * 4 + 2 * far_x + half_x
            for other in range(N_BAND):
                found.append((holder, other, (2 * far_y + far_x) * N_BAND + other, answer))
    return found


def parameter_lanes():
    lane = iota((1, LANES), 1)
    source = jnp.where(lane < BANDS + 2, lane, -1)
    source = jnp.where(lane == BANDS + 2, PARAMS - 1, source)
    for j, base in enumerate((WEIGHT, SPREAD_Y, SPREAD_X)):
        here = (lane >= base) & (lane < base + COMPONENTS)
        source = jnp.where(here, BANDS + 2 + 3 * (lane - base) + j, source)
    return (iota((PARAMS, LANES), 0) == source).astype(f32)


def derived(params, lanes):
    raw = dot(params, lanes, precision=highest)
    lane = iota(raw.shape, 1)
    is_flux = lane < BANDS
    is_shift = (lane >= BANDS) & (lane < BANDS + 2)
    is_weight = (lane >= WEIGHT) & (lane < WEIGHT + COMPONENTS)
    is_spread = ((lane >= SPREAD_Y) & (lane < SPREAD_Y + COMPONENTS)) | (
        (lane >= SPREAD_X) & (lane < SPREAD_X + COMPONENTS)
    )
    most = jnp.max(jnp.where(is_weight, raw, -jnp.inf), axis=1, keepdims=True)
    power = jnp.where(is_weight, jnp.exp(jnp.where(is_weight, raw - most, 0.0)), 0.0)
    weight = power / jnp.sum(power, axis=1, keepdims=True)
    decay = jnp.exp(-jnp.abs(raw))
    soft = jnp.maximum(raw, 0.0) + jnp.log1p(decay)
    sigmoid = jnp.where(raw >= 0.0, 1.0, decay) / (1.0 + decay)
    curve = jnp.tanh(raw)
    softness = jnp.exp(0.25 * raw[:, BANDS + 2 : BANDS + 3])
    scale = (PATCH / 32.0) * softness
    spread = (0.5 + soft) * scale
    return is_flux, is_shift, is_weight, is_spread, weight, soft, sigmoid, curve, scale, spread


def send_kernel(params, offsets, counts, out, mine, landed, send_sem, recv_sem):
    tile, band = lax.axis_index("tile"), lax.axis_index("band")
    barrier = pltpu.get_barrier_semaphore()
    for other_tile, other_band, _, _ in owners(tile, band):
        pl.semaphore_signal(barrier, inc=1, device_id=(other_tile, other_band), device_id_type=MESH)
    is_flux, is_shift, is_weight, is_spread, weight, soft, _, curve, _, spread = derived(
        params[...], parameter_lanes()
    )
    lane = iota((SRC, LANES), 1)
    live = (iota((SRC, LANES), 0) < counts[0]).astype(f32)
    place = offsets[...].astype(f32)
    row = jnp.where(is_flux, flux_scale * soft * live, 0.0)
    row = jnp.where(is_shift, (PATCH / 16.0) * curve, row)
    row = jnp.where(is_weight, weight, row)
    row = jnp.where(is_spread, spread, row)
    row = jnp.where(lane == TOP, place[:, 0:1], row)
    row = jnp.where(lane == LEFT, place[:, 1:2], row)
    mine[...] = jnp.where(lane == LIVE, live, row)
    pl.semaphore_wait(barrier, PARTNERS)
    copies = []
    for i, (other_tile, other_band, block, _) in enumerate(viewers(tile, band)):
        copy = pltpu.make_async_remote_copy(
            src_ref=mine,
            dst_ref=landed.at[block],
            send_sem=send_sem.at[i],
            recv_sem=recv_sem.at[block],
            device_id=(other_tile, other_band),
            device_id_type=MESH,
        )
        copy.start()
        copies.append(copy)
    for i, (other_tile, other_band, _, _) in enumerate(owners(tile, band)):
        pltpu.make_async_remote_copy(
            src_ref=mine,
            dst_ref=landed.at[i],
            send_sem=send_sem.at[i],
            recv_sem=recv_sem.at[i],
            device_id=(other_tile, other_band),
            device_id_type=MESH,
        ).wait_recv()
        out[i * SRC : (i + 1) * SRC, :] = landed[i]
    for copy in copies:
        copy.wait_send()


def return_kernel(params, counts, parts, out, landed, send_sem, recv_sem):
    tile, band = lax.axis_index("tile"), lax.axis_index("band")
    barrier = pltpu.get_barrier_semaphore()
    for other_tile, other_band, _, _ in viewers(tile, band):
        pl.semaphore_signal(barrier, inc=1, device_id=(other_tile, other_band), device_id_type=MESH)
    pl.semaphore_wait(barrier, PARTNERS)
    copies = []
    for i, (other_tile, other_band, block, answer) in enumerate(owners(tile, band)):
        copy = pltpu.make_async_remote_copy(
            src_ref=parts.at[block * SRC : (block + 1) * SRC, :],
            dst_ref=landed.at[answer],
            send_sem=send_sem.at[i],
            recv_sem=recv_sem.at[answer],
            device_id=(other_tile, other_band),
            device_id_type=MESH,
        )
        copy.start()
        copies.append(copy)
    theta = params[...]
    lanes = parameter_lanes()
    is_flux, is_shift, is_weight, is_spread, weight, soft, sigmoid, curve, scale, spread = derived(
        theta, lanes
    )
    lane = iota((SRC, LANES), 1)
    slope = jnp.where(is_flux, sigmoid / soft, 0.0)
    slope = jnp.where(is_shift, (PATCH / 16.0) * (1.0 - curve * curve), slope)
    slope = jnp.where(is_weight, 1.0, slope)
    slope = jnp.where(is_spread, scale * sigmoid, slope)
    live = (iota((SRC, PARAMS), 0) < counts[0]).astype(f32)
    prior = prior_weight * theta * live
    total = jnp.zeros((SRC, LANES), f32)
    for i, (other_tile, other_band, _, _) in enumerate(viewers(tile, band)):
        pltpu.make_async_remote_copy(
            src_ref=parts.at[0:SRC, :],
            dst_ref=landed.at[i],
            send_sem=send_sem.at[i],
            recv_sem=recv_sem.at[i],
            device_id=(other_tile, other_band),
            device_id_type=MESH,
        ).wait_recv()
        total = total + landed[i]
    pulled = total * slope
    all_weights = jnp.sum(jnp.where(is_weight, total, 0.0), axis=1, keepdims=True)
    pulled = pulled - jnp.where(is_weight, weight * all_weights, 0.0)
    all_spreads = jnp.sum(jnp.where(is_spread, total * spread, 0.0), axis=1, keepdims=True)
    pulled = jnp.where(lane == BANDS + 2, 0.25 * all_spreads, pulled)
    out[...] = dot(pulled, lanes, ((1,), (1,)), highest) - prior
    for copy in copies:
        copy.wait_send()


def quadrant_kernel(
    slots,
    background,
    psf_y,
    psf_x,
    image,
    out,
    pixels,
    conv_high,
    conv_low,
    back_high,
    back_low,
    profiles,
    y_high,
    y_low,
    x_high,
    x_low,
    model,
    r_high,
    r_low,
    image_sem,
):
    tile, band = lax.axis_index("tile"), lax.axis_index("band")
    row, col = tile // TILE_COLS, lax.rem(tile, TILE_COLS)
    half_y, half_x = band // 2, lax.rem(band, 2)
    load = pltpu.make_async_copy(
        image.at[
            0,
            :,
            pl.ds(pl.multiple_of(half_y * QUAD, QUAD), QUAD),
            pl.ds(pl.multiple_of(half_x * 128, 128), COLS),
        ],
        pixels,
        image_sem,
    )
    load.start()

    slot = iota((SLOTS, LANES), 0)
    lane = iota((SLOTS, LANES), 1)
    far_y, far_x = slot // (SLOTS // 2), lax.rem(slot // (SLOTS // 4), 2)

    def moved(far, half, place):
        origin = jnp.where(far == 0, 0, TILE_SIDE * (2 * half - 1)) - QUAD * half
        beyond = place + 2 * half - 1
        there = (far == 0) | ((beyond >= 0) & (beyond < TILE_COLS))
        return origin.astype(f32), there

    origin_y, there_y = moved(far_y, half_y, row)
    origin_x, there_x = moved(far_x, half_x, col)
    data = slots[...]
    data = jnp.where(lane == TOP, data + origin_y, jnp.where(lane == LEFT, data + origin_x, data))
    top, left, live = data[:, TOP : TOP + 1], data[:, LEFT : LEFT + 1], data[:, LIVE : LIVE + 1]
    reach = (live > 0.0) & (top > -PATCH) & (top < QUAD) & (left > -PATCH) & (left < QUAD)
    active = jnp.where(there_y & there_x & reach, 1.0, 0.0)
    before = jnp.where(lane < slot, 1.0, 0.0).astype(bf16)
    order = dot(before, active.astype(bf16))
    count = jnp.sum(active[:, 0:1]).astype(jnp.int32)
    chunks = (count + PER_CHUNK - 1) // PER_CHUNK
    order = jnp.where(active > 0.0, order, -1.0)[:, 0:1].astype(jnp.int32)

    tap, spot = iota((TAPS, COLS), 0), iota((TAPS, COLS), 1)
    forward = (tap == spot).astype(f32)
    backward = (lax.rem(COLS - tap, COLS) == spot).astype(f32)
    for side, psf in enumerate((psf_y, psf_x)):
        ahead = dot(psf[...], forward, precision=highest)
        behind = dot(psf[...], backward, precision=highest)
        for b in range(BANDS):
            wide = jnp.broadcast_to(ahead[b : b + 1, :], (QUAD, COLS))
            high, low = halves(pltpu.roll(wide, 0, 1, stride=1, stride_axis=0))
            conv_high[side, b] = high
            conv_low[side, b] = low
            wide = jnp.broadcast_to(behind[b : b + 1, :], (SPAN, COLS))
            high, low = halves(pltpu.roll(wide, 0, 1, stride=1, stride_axis=0))
            back_high[side, b] = high
            back_low[side, b] = low

    column = iota((1, COLS), 1)
    place = (column * 5462) >> 16
    comp = column - COMPONENTS * place
    used = place < PER_CHUNK
    mine = iota((16, COLS), 0) == comp

    def picked(c):
        return jnp.where(used & (order - c * PER_CHUNK == place), 1.0, 0.0)

    def gathered(c):
        return dot(data, picked(c), ((0,), (0,)), highest)

    def one_of(values, base):
        return jnp.sum(jnp.where(mine, values[base : base + 16], 0.0), axis=0, keepdims=True)

    def geometry(values, side):
        spread = one_of(values, (SPREAD_Y, SPREAD_X)[side])
        inverse = 1.0 / jnp.where(spread > 0.0, spread, 1.0)
        shift = values[BANDS + side : BANDS + side + 1]
        start = values[TOP + side : TOP + side + 1]
        spot = iota((SPAN, COLS), 0).astype(f32) - (start + float(HALF))
        inside = (spot >= 0.0) & (spot < PATCH)
        ratio = (spot + (0.5 - PATCH / 2.0) - shift) * inverse
        spot = iota((QUAD, COLS), 0).astype(f32) - start
        window = ((spot >= 0.0) & (spot < PATCH)).astype(f32)
        return inverse, inside, ratio, window

    model[...] = jnp.zeros_like(model)

    def render(c, carry):
        values = gathered(c)
        weight = one_of(values, WEIGHT)
        for side in range(2):
            _, inside, ratio, window = geometry(values, side)
            profile = jnp.where(inside, jnp.exp(-0.5 * ratio * ratio), 0.0)
            profiles[c, side] = profile
            split = halves(profile)
            for b in range(BANDS):
                factor = dot3(
                    (conv_high[side, b, :, :SPAN], conv_low[side, b, :, :SPAN]), split
                )
                if side == 0:
                    factor = factor * (window * (weight * values[b : b + 1]))
                    y_high[c, b], y_low[c, b] = halves(factor)
                else:
                    factor = factor * window
                    x_high[c, b], x_low[c, b] = halves(factor)
        for b in range(BANDS):
            model[b] += dot3((y_high[c, b], y_low[c, b]), (x_high[c, b], x_low[c, b]), ((1,), (1,)))
        return carry

    lax.fori_loop(0, chunks, render, 0)

    load.wait()
    turn = lax.rem(COLS - half_x * (QUAD - 128), COLS)
    for b in range(BANDS):
        observed = pltpu.roll(pixels[b], turn, 1)[:, :QUAD]
        residual = (observed / (background[0, b] + model[b]) - 1.0) * (1.0 / (PATCH * PATCH))
        r_high[b], r_low[b] = halves(residual)

    out[...] = jnp.zeros_like(out)

    def pull(c, carry):
        values = gathered(c)
        weight = one_of(values, WEIGHT)
        rows = []
        d_y = jnp.zeros((SPAN, COLS), f32)
        d_x = jnp.zeros((SPAN, COLS), f32)
        inverse_y, _, ratio_y, window_y = geometry(values, 0)
        inverse_x, _, ratio_x, window_x = geometry(values, 1)
        for b in range(BANDS):
            r = (r_high[b], r_low[b])
            along_y = dot3(r, (x_high[c, b], x_low[c, b]))
            along_x = dot3(r, (y_high[c, b], y_low[c, b]), ((0,), (0,)))
            factor = y_high[c, b].astype(f32) + y_low[c, b].astype(f32)
            rows.append(jnp.sum(along_y * factor, axis=0, keepdims=True))
            along_y = along_y * (window_y * (weight * values[b : b + 1]))
            along_x = along_x * window_x
            d_y = d_y + dot3((back_high[0, b, :, :QUAD], back_low[0, b, :, :QUAD]), halves(along_y))
            d_x = d_x + dot3((back_high[1, b, :, :QUAD], back_low[1, b, :, :QUAD]), halves(along_x))
        by_comp = rows[0] + rows[1] + rows[2] + rows[3] + rows[4]
        spreads = []
        for side, (d, inverse, ratio) in enumerate(
            ((d_y, inverse_y, ratio_y), (d_x, inverse_x, ratio_x))
        ):
            first = d * profiles[c, side] * ratio
            rows.append(inverse * jnp.sum(first, axis=0, keepdims=True))
            spreads.append(inverse * jnp.sum(first * ratio, axis=0, keepdims=True))
        pieces = rows + [jnp.zeros((16 - len(rows), COLS), f32)]
        for by in (by_comp, spreads[0], spreads[1]):
            pieces.append(jnp.where(mine, by, 0.0))
        pieces.append(jnp.zeros((LANES - 64, COLS), f32))
        out[...] += dot(picked(c), jnp.concatenate(pieces, axis=0), ((1,), (1,)), highest)
        return carry

    lax.fori_loop(0, chunks, pull, 0)


def vmem(count):
    return [pl.BlockSpec(memory_space=pltpu.VMEM)] * count


def body(params, offsets, counts, image, background, psf_y, psf_x):
    smem = pl.BlockSpec(memory_space=pltpu.SMEM)
    slots = pl.pallas_call(
        send_kernel,
        out_shape=jax.ShapeDtypeStruct((SLOTS, LANES), f32),
        in_specs=vmem(2) + [smem],
        out_specs=vmem(1)[0],
        scratch_shapes=[
            pltpu.VMEM((SRC, LANES), f32),
            pltpu.VMEM((PARTNERS, SRC, LANES), f32),
            pltpu.SemaphoreType.DMA((PARTNERS,)),
            pltpu.SemaphoreType.DMA((PARTNERS,)),
        ],
        compiler_params=pltpu.CompilerParams(collective_id=0, has_side_effects=True),
        name="send_slots",
    )(params, offsets, counts)
    parts = pl.pallas_call(
        quadrant_kernel,
        out_shape=jax.ShapeDtypeStruct((SLOTS, LANES), f32),
        in_specs=[vmem(1)[0], smem] + vmem(2) + [pl.BlockSpec(memory_space=pl.ANY)],
        out_specs=vmem(1)[0],
        scratch_shapes=[
            pltpu.VMEM((BANDS, QUAD, COLS), f32),
            pltpu.VMEM((2, BANDS, QUAD, COLS), bf16),
            pltpu.VMEM((2, BANDS, QUAD, COLS), bf16),
            pltpu.VMEM((2, BANDS, SPAN, COLS), bf16),
            pltpu.VMEM((2, BANDS, SPAN, COLS), bf16),
            pltpu.VMEM((CHUNKS, 2, SPAN, COLS), f32),
            pltpu.VMEM((CHUNKS, BANDS, QUAD, COLS), bf16),
            pltpu.VMEM((CHUNKS, BANDS, QUAD, COLS), bf16),
            pltpu.VMEM((CHUNKS, BANDS, QUAD, COLS), bf16),
            pltpu.VMEM((CHUNKS, BANDS, QUAD, COLS), bf16),
            pltpu.VMEM((BANDS, QUAD, QUAD), f32),
            pltpu.VMEM((BANDS, QUAD, QUAD), bf16),
            pltpu.VMEM((BANDS, QUAD, QUAD), bf16),
            pltpu.SemaphoreType.DMA,
        ],
        compiler_params=pltpu.CompilerParams(vmem_limit_bytes=48 * 1024 * 1024),
        name="quadrant",
    )(slots, background, psf_y, psf_x, image)
    return pl.pallas_call(
        return_kernel,
        out_shape=jax.ShapeDtypeStruct((SRC, PARAMS), f32),
        in_specs=[vmem(1)[0], smem, vmem(1)[0]],
        out_specs=vmem(1)[0],
        scratch_shapes=[
            pltpu.VMEM((PARTNERS, SRC, LANES), f32),
            pltpu.SemaphoreType.DMA((PARTNERS,)),
            pltpu.SemaphoreType.DMA((PARTNERS,)),
        ],
        compiler_params=pltpu.CompilerParams(collective_id=1, has_side_effects=True),
        name="return_parts",
    )(params, counts, parts)


def solution(mesh):
    placed = (
        P(("tile", "band"), None),
        P(("tile", "band"), None),
        P(("tile", "band")),
        P("tile", None, None, None),
        P("tile", None),
        P(),
        P(),
    )
    return jax.shard_map(
        body, mesh=mesh, in_specs=placed, out_specs=P(("tile", "band"), None), check_vma=False
    )
```

```python
import functools

import jax
import jax.numpy as jnp
from jax import lax
from jax.experimental import pallas as pl
from jax.experimental.pallas import tpu as pltpu
from jax.sharding import PartitionSpec as P

BANDS = 5
COMPONENTS = 12
PARAMS = 44
PATCH = 64
TAPS = 25
HALF = TAPS // 2
TILE_COLS = 8
TILE_SIDE = 384
QUAD = TILE_SIDE // 2
SRC = 8
TILES = 64
N_BAND = 4
PARTNERS = 16
SLOTS = PARTNERS * SRC
LANES = 128

TOP, LEFT, LIVE = 8, 9, 10
WEIGHT, SPREAD_Y, SPREAD_X = 16, 32, 48

PER_CHUNK = 21
COLS = 256
CHUNKS = -(-SLOTS // PER_CHUNK)
SPAN = 224

flux_scale = 2.0
prior_weight = 0.1
highest = lax.Precision.HIGHEST
f32 = jnp.float32
bf16 = jnp.bfloat16
MESH = pl.DeviceIdType.MESH


def iota(shape, axis):
    return lax.broadcasted_iota(jnp.int32, shape, axis)


def dot(a, b, dims=((1,), (0,)), precision=None):
    return lax.dot_general(a, b, (dims, ((), ())), precision=precision, preferred_element_type=f32)


def halves(x):
    high = x.astype(bf16)
    return high, (x - high.astype(f32)).astype(bf16)


def dot3(a, b, dims=((1,), (0,))):
    return dot(a[0], b[0], dims) + (dot(a[0], b[1], dims) + dot(a[1], b[0], dims))


def wrapped_tile(row, col):
    return lax.rem(row + TILE_COLS, TILE_COLS) * TILE_COLS + lax.rem(col + TILE_COLS, TILE_COLS)


def viewers(tile, band):
    home = lax.rem(tile + TILES // 2, TILES)
    row, col = home // TILE_COLS, lax.rem(home, TILE_COLS)
    found = []
    for step_y, half_y in ((0, 0), (0, 1), (1, 0), (-1, 1)):
        for step_x, half_x in ((0, 0), (0, 1), (1, 0), (-1, 1)):
            far = 2 * abs(step_y) + abs(step_x)
            answer = (2 * abs(step_y) + half_y) * 4 + 2 * abs(step_x) + half_x
            found.append(
                (wrapped_tile(row + step_y, col + step_x), 2 * half_y + half_x, far * N_BAND + band, answer)
            )
    return found


def owners(tile, band):
    row, col = tile // TILE_COLS, lax.rem(tile, TILE_COLS)
    half_y, half_x = band // 2, lax.rem(band, 2)
    found = []
    for far_y in range(2):
        for far_x in range(2):
            home = wrapped_tile(row + far_y * (2 * half_y - 1), col + far_x * (2 * half_x - 1))
            holder = lax.rem(home + TILES // 2, TILES)
            answer = (2 * far_y + half_y) * 4 + 2 * far_x + half_x
            for other in range(N_BAND):
                found.append((holder, other, (2 * far_y + far_x) * N_BAND + other, answer))
    return found


def parameter_lanes():
    lane = iota((1, LANES), 1)
    source = jnp.where(lane < BANDS + 2, lane, -1)
    source = jnp.where(lane == BANDS + 2, PARAMS - 1, source)
    for j, base in enumerate((WEIGHT, SPREAD_Y, SPREAD_X)):
        here = (lane >= base) & (lane < base + COMPONENTS)
        source = jnp.where(here, BANDS + 2 + 3 * (lane - base) + j, source)
    return (iota((PARAMS, LANES), 0) == source).astype(f32)


def derived(params, lanes):
    raw = dot(params, lanes, precision=highest)
    lane = iota(raw.shape, 1)
    is_flux = lane < BANDS
    is_shift = (lane >= BANDS) & (lane < BANDS + 2)
    is_weight = (lane >= WEIGHT) & (lane < WEIGHT + COMPONENTS)
    is_spread = ((lane >= SPREAD_Y) & (lane < SPREAD_Y + COMPONENTS)) | (
        (lane >= SPREAD_X) & (lane < SPREAD_X + COMPONENTS)
    )
    most = jnp.max(jnp.where(is_weight, raw, -jnp.inf), axis=1, keepdims=True)
    power = jnp.where(is_weight, jnp.exp(jnp.where(is_weight, raw - most, 0.0)), 0.0)
    weight = power / jnp.sum(power, axis=1, keepdims=True)
    decay = jnp.exp(-jnp.abs(raw))
    soft = jnp.maximum(raw, 0.0) + jnp.log1p(decay)
    sigmoid = jnp.where(raw >= 0.0, 1.0, decay) / (1.0 + decay)
    curve = jnp.tanh(raw)
    softness = jnp.exp(0.25 * raw[:, BANDS + 2 : BANDS + 3])
    scale = (PATCH / 32.0) * softness
    spread = (0.5 + soft) * scale
    return is_flux, is_shift, is_weight, is_spread, weight, soft, sigmoid, curve, scale, spread


def start_copies(pairs, sems):
    copies = [pltpu.make_async_copy(src, dst, sems.at[i]) for i, (src, dst) in enumerate(pairs)]
    for copy in copies:
        copy.start()
    return copies


def send_kernel(
    params,
    offsets,
    counts,
    psf_y,
    psf_x,
    out,
    conv_high,
    conv_low,
    back_high,
    back_low,
    pulls,
    prior,
    theta,
    place,
    taps,
    mine,
    landed,
    load_sem,
    send_sem,
    recv_sem,
):
    tile, band = lax.axis_index("tile"), lax.axis_index("band")
    barrier = pltpu.get_barrier_semaphore()
    for other_tile, other_band, _, _ in owners(tile, band):
        pl.semaphore_signal(barrier, inc=1, device_id=(other_tile, other_band), device_id_type=MESH)
    loads = start_copies(
        ((params, theta), (offsets, place), (psf_y, taps.at[0]), (psf_x, taps.at[1])), load_sem
    )
    for load in loads:
        load.wait()
    is_flux, is_shift, is_weight, is_spread, weight, soft, sigmoid, curve, scale, spread = derived(
        theta[...], parameter_lanes()
    )
    slot, lane = iota((SRC, LANES), 0), iota((SRC, LANES), 1)
    live = (slot < counts[0]).astype(f32)
    row = jnp.where(is_flux, flux_scale * soft * live, 0.0)
    row = jnp.where(is_shift, (PATCH / 16.0) * curve, row)
    row = jnp.where(is_weight, weight, row)
    row = jnp.where(is_spread, spread, row)
    start = place[...].astype(f32)
    diagonal = iota((SRC, SRC), 0) == iota((SRC, SRC), 1)
    for side in range(2):
        start_side = jnp.sum(jnp.where(diagonal, start[side : side + 1, :], 0.0), axis=1, keepdims=True)
        row = jnp.where(lane == TOP + side, start_side, row)
    mine[...] = jnp.where(lane == LIVE, live, row)

    slope = jnp.where(is_flux, sigmoid / soft, 0.0)
    slope = jnp.where(is_shift, (PATCH / 16.0) * (1.0 - curve * curve), slope)
    slope = jnp.where(is_weight, 1.0, slope)
    pulls[0] = jnp.where(is_spread, scale * sigmoid, slope)
    pulls[1] = jnp.where(is_weight, weight, 0.0)
    pulls[2] = jnp.where(is_spread, spread, 0.0)
    prior[...] = prior_weight * theta[...] * live[:, :PARAMS]

    pl.semaphore_wait(barrier, PARTNERS)
    copies = []
    for i, (other_tile, other_band, block, _) in enumerate(viewers(tile, band)):
        copy = pltpu.make_async_remote_copy(
            src_ref=mine,
            dst_ref=landed.at[block],
            send_sem=send_sem.at[i],
            recv_sem=recv_sem.at[block],
            device_id=(other_tile, other_band),
            device_id_type=MESH,
        )
        copy.start()
        copies.append(copy)

    tap, spot = iota((TAPS, COLS), 0), iota((TAPS, COLS), 1)
    forward = (tap == spot).astype(f32)
    backward = (lax.rem(COLS - tap, COLS) == spot).astype(f32)
    for side in range(2):
        psf = taps[side]
        ahead = dot(psf, forward, precision=highest)
        behind = dot(psf, backward, precision=highest)
        for b in range(BANDS):
            wide = jnp.broadcast_to(ahead[b : b + 1, :], (QUAD, COLS))
            conv_high[side, b], conv_low[side, b] = halves(
                pltpu.roll(wide, 0, 1, stride=1, stride_axis=0)
            )
            wide = jnp.broadcast_to(behind[b : b + 1, :], (SPAN, COLS))
            back_high[side, b], back_low[side, b] = halves(
                pltpu.roll(wide, 0, 1, stride=1, stride_axis=0)
            )

    for i, (other_tile, other_band, _, _) in enumerate(owners(tile, band)):
        pltpu.make_async_remote_copy(
            src_ref=mine,
            dst_ref=landed.at[i],
            send_sem=send_sem.at[i],
            recv_sem=recv_sem.at[i],
            device_id=(other_tile, other_band),
            device_id_type=MESH,
        ).wait_recv()
        out[i * SRC : (i + 1) * SRC, :] = landed[i]
    for copy in copies:
        copy.wait_send()


def quadrant_of(image, tile, band):
    half_y, half_x = band // 2, lax.rem(band, 2)
    rows = pl.ds(pl.multiple_of(half_y * QUAD, QUAD), QUAD)
    cols = pl.ds(pl.multiple_of(half_x * (COLS // 2), COLS // 2), COLS)
    return image.at[0, :, rows, cols]


def column_comps():
    column = iota((1, COLS), 1)
    place = (column * 5462) >> 16
    return place, iota((16, COLS), 0) == column - COMPONENTS * place


def one_of(values, base):
    mine = column_comps()[1]
    return jnp.sum(jnp.where(mine, values[base : base + 16], 0.0), axis=0, keepdims=True)


def geometry(values, side):
    spread = one_of(values, (SPREAD_Y, SPREAD_X)[side])
    inverse = 1.0 / jnp.where(spread > 0.0, spread, 1.0)
    shift = values[BANDS + side : BANDS + side + 1]
    start = values[TOP + side : TOP + side + 1]
    spot = iota((SPAN, COLS), 0).astype(f32) - (start + float(HALF))
    inside = (spot >= 0.0) & (spot < PATCH)
    ratio = (spot + (0.5 - PATCH / 2.0) - shift) * inverse
    spot = iota((QUAD, COLS), 0).astype(f32) - start
    window = ((spot >= 0.0) & (spot < PATCH)).astype(f32)
    return inverse, inside, ratio, window


def render(values, conv, profiles, factors, model, c):
    conv_high, conv_low = conv
    y_high, y_low, x_high, x_low = factors
    weight = one_of(values, WEIGHT)
    for side in range(2):
        _, inside, ratio, window = geometry(values, side)
        profile = jnp.where(inside, jnp.exp(-0.5 * ratio * ratio), 0.0)
        profiles[c, side] = profile
        split = halves(profile)
        for b in range(BANDS):
            factor = dot3((conv_high[side, b, :, :SPAN], conv_low[side, b, :, :SPAN]), split)
            if side == 0:
                factor = factor * (window * (weight * values[b : b + 1]))
                y_high[c, b], y_low[c, b] = halves(factor)
            else:
                factor = factor * window
                x_high[c, b], x_low[c, b] = halves(factor)
    for b in range(BANDS):
        model[b] += dot3((y_high[c, b], y_low[c, b]), (x_high[c, b], x_low[c, b]), ((1,), (1,)))


def leave(pixels, background, model, residual, half_x):
    turn = lax.rem(COLS - half_x * (QUAD - COLS // 2), COLS)
    for b in range(BANDS):
        observed = pltpu.roll(pixels[b], turn, 1)[:, :QUAD]
        left = observed / (background[0:1, b : b + 1] + model[b]) - 1.0
        residual[0][b], residual[1][b] = halves(left * (1.0 / (PATCH * PATCH)))


def pull(values, onehot, back, profiles, factors, residual, c):
    back_high, back_low = back
    y_high, y_low, x_high, x_low = factors
    mine = column_comps()[1]
    weight = one_of(values, WEIGHT)
    rows = []
    d_y = jnp.zeros((SPAN, COLS), f32)
    d_x = jnp.zeros((SPAN, COLS), f32)
    inverse_y, _, ratio_y, window_y = geometry(values, 0)
    inverse_x, _, ratio_x, window_x = geometry(values, 1)
    for b in range(BANDS):
        r = (residual[0][b], residual[1][b])
        along_y = dot3(r, (x_high[c, b], x_low[c, b]))
        along_x = dot3(r, (y_high[c, b], y_low[c, b]), ((0,), (0,)))
        factor = y_high[c, b].astype(f32) + y_low[c, b].astype(f32)
        rows.append(jnp.sum(along_y * factor, axis=0, keepdims=True))
        along_y = along_y * (window_y * (weight * values[b : b + 1]))
        along_x = along_x * window_x
        d_y = d_y + dot3((back_high[0, b, :, :QUAD], back_low[0, b, :, :QUAD]), halves(along_y))
        d_x = d_x + dot3((back_high[1, b, :, :QUAD], back_low[1, b, :, :QUAD]), halves(along_x))
    by_comp = rows[0] + rows[1] + rows[2] + rows[3] + rows[4]
    spreads = []
    for side, (d, inverse, ratio) in enumerate(((d_y, inverse_y, ratio_y), (d_x, inverse_x, ratio_x))):
        first = d * profiles[c, side] * ratio
        rows.append(inverse * jnp.sum(first, axis=0, keepdims=True))
        spreads.append(inverse * jnp.sum(first * ratio, axis=0, keepdims=True))
    pieces = rows + [jnp.zeros((16 - len(rows), COLS), f32)]
    for by in (by_comp, spreads[0], spreads[1]):
        pieces.append(jnp.where(mine, by, 0.0))
    pieces.append(jnp.zeros((LANES - 64, COLS), f32))
    return dot(onehot, jnp.concatenate(pieces, axis=0), ((1,), (1,)), highest)


def find_kernel(
    slots,
    background,
    image,
    conv_high,
    conv_low,
    back_high,
    back_low,
    values_out,
    onehot_out,
    rest_model,
    rest_parts,
    sky,
    pixels,
    profiles,
    y_high,
    y_low,
    x_high,
    x_low,
    whole,
    r_high,
    r_low,
    load_sem,
):
    tile, band = lax.axis_index("tile"), lax.axis_index("band")
    row, col = tile // TILE_COLS, lax.rem(tile, TILE_COLS)
    half_y, half_x = band // 2, lax.rem(band, 2)

    slot = iota((SLOTS, LANES), 0)
    lane = iota((SLOTS, LANES), 1)
    far_y, far_x = slot // (SLOTS // 2), lax.rem(slot // (SLOTS // 4), 2)

    def moved(far, half, place):
        origin = jnp.where(far == 0, 0, TILE_SIDE * (2 * half - 1)) - QUAD * half
        beyond = place + 2 * half - 1
        there = (far == 0) | ((beyond >= 0) & (beyond < TILE_COLS))
        return origin.astype(f32), there

    origin_y, there_y = moved(far_y, half_y, row)
    origin_x, there_x = moved(far_x, half_x, col)
    data = slots[...]
    data = jnp.where(lane == TOP, data + origin_y, jnp.where(lane == LEFT, data + origin_x, data))
    top, left, live = data[:, TOP : TOP + 1], data[:, LEFT : LEFT + 1], data[:, LIVE : LIVE + 1]
    reach = (live > 0.0) & (top > -PATCH) & (top < QUAD) & (left > -PATCH) & (left < QUAD)
    active = jnp.where(there_y & there_x & reach, 1.0, 0.0)
    before = jnp.where(lane < slot, 1.0, 0.0).astype(bf16)
    order = dot(before, active.astype(bf16))
    count = jnp.sum(active[:, 0:1]).astype(jnp.int32)
    order = jnp.where(active > 0.0, order, -1.0)[:, 0:1].astype(jnp.int32)
    place = column_comps()[0]

    def picked(c):
        return jnp.where((place < PER_CHUNK) & (order - c * PER_CHUNK == place), 1.0, 0.0)

    def gathered(c):
        return dot(data, picked(c), ((0,), (0,)), highest)

    onehot_out[...] = picked(0)
    values_out[...] = gathered(0)
    rest_model[...] = jnp.zeros_like(rest_model)
    rest_parts[...] = jnp.zeros_like(rest_parts)

    @pl.when(count > PER_CHUNK)
    def _():
        conv, back = (conv_high, conv_low), (back_high, back_low)
        factors, residual = (y_high, y_low, x_high, x_low), (r_high, r_low)
        loads = start_copies(
            ((quadrant_of(image, tile, band), pixels), (background, sky)), load_sem
        )
        chunks = (count + PER_CHUNK - 1) // PER_CHUNK

        def add(c, carry):
            render(gathered(c), conv, profiles, factors, rest_model, c)
            return carry

        lax.fori_loop(1, chunks, add, 0)
        whole[...] = rest_model[...]
        render(gathered(0), conv, profiles, factors, whole, 0)
        for load in loads:
            load.wait()
        leave(pixels, sky, whole, residual, half_x)

        def take(c, carry):
            rest_parts[...] += pull(gathered(c), picked(c), back, profiles, factors, residual, c)
            return carry

        lax.fori_loop(1, chunks, take, 0)


def return_kernel(
    values_in,
    onehot,
    rest_model,
    rest_parts,
    background,
    image,
    conv_high,
    conv_low,
    back_high,
    back_low,
    pulls,
    prior,
    out,
    sky,
    pixels,
    profiles,
    y_high,
    y_low,
    x_high,
    x_low,
    model,
    r_high,
    r_low,
    parts,
    landed,
    load_sem,
    send_sem,
    recv_sem,
):
    tile, band = lax.axis_index("tile"), lax.axis_index("band")
    half_x = lax.rem(band, 2)
    barrier = pltpu.get_barrier_semaphore()
    for other_tile, other_band, _, _ in viewers(tile, band):
        pl.semaphore_signal(barrier, inc=1, device_id=(other_tile, other_band), device_id_type=MESH)
    loads = start_copies(((quadrant_of(image, tile, band), pixels), (background, sky)), load_sem)
    conv, back = (conv_high, conv_low), (back_high, back_low)
    factors, residual = (y_high, y_low, x_high, x_low), (r_high, r_low)
    values = values_in[...]
    model[...] = rest_model[...]
    render(values, conv, profiles, factors, model, 0)
    for load in loads:
        load.wait()
    leave(pixels, sky, model, residual, half_x)
    parts[...] = rest_parts[...] + pull(values, onehot[...], back, profiles, factors, residual, 0)

    pl.semaphore_wait(barrier, PARTNERS)
    copies = []
    for i, (other_tile, other_band, block, answer) in enumerate(owners(tile, band)):
        copy = pltpu.make_async_remote_copy(
            src_ref=parts.at[block * SRC : (block + 1) * SRC, :],
            dst_ref=landed.at[answer],
            send_sem=send_sem.at[i],
            recv_sem=recv_sem.at[answer],
            device_id=(other_tile, other_band),
            device_id_type=MESH,
        )
        copy.start()
        copies.append(copy)
    lanes = parameter_lanes()
    total = jnp.zeros((SRC, LANES), f32)
    for i, (other_tile, other_band, _, _) in enumerate(viewers(tile, band)):
        pltpu.make_async_remote_copy(
            src_ref=parts.at[0:SRC, :],
            dst_ref=landed.at[i],
            send_sem=send_sem.at[i],
            recv_sem=recv_sem.at[i],
            device_id=(other_tile, other_band),
            device_id_type=MESH,
        ).wait_recv()
        total = total + landed[i]
    lane = iota((SRC, LANES), 1)
    is_weight = (lane >= WEIGHT) & (lane < WEIGHT + COMPONENTS)
    all_weights = jnp.sum(jnp.where(is_weight, total, 0.0), axis=1, keepdims=True)
    all_spreads = jnp.sum(total * pulls[2], axis=1, keepdims=True)
    pulled = total * pulls[0] - pulls[1] * all_weights
    pulled = jnp.where(lane == BANDS + 2, 0.25 * all_spreads, pulled)
    out[...] = dot(pulled, lanes, ((1,), (1,)), highest) - prior[...]
    for copy in copies:
        copy.wait_send()


def vmem(count):
    return [pl.BlockSpec(memory_space=pltpu.VMEM)] * count


def hbm(count):
    return [pl.BlockSpec(memory_space=pltpu.HBM)] * count


def work_space(chunks):
    return [
        pltpu.VMEM((1, BANDS), f32),
        pltpu.VMEM((BANDS, QUAD, COLS), f32),
        pltpu.VMEM((chunks, 2, SPAN, COLS), f32),
        pltpu.VMEM((chunks, BANDS, QUAD, COLS), bf16),
        pltpu.VMEM((chunks, BANDS, QUAD, COLS), bf16),
        pltpu.VMEM((chunks, BANDS, QUAD, COLS), bf16),
        pltpu.VMEM((chunks, BANDS, QUAD, COLS), bf16),
        pltpu.VMEM((BANDS, QUAD, QUAD), f32),
        pltpu.VMEM((BANDS, QUAD, QUAD), bf16),
        pltpu.VMEM((BANDS, QUAD, QUAD), bf16),
    ]


def shape(*dims, kind=f32):
    return jax.ShapeDtypeStruct(dims, kind)


def body(params, offsets, counts, image, background, psf_y, psf_x):
    smem = pl.BlockSpec(memory_space=pltpu.SMEM)
    params, offsets, image, background, psf_y, psf_x = (
        pltpu.with_memory_space_constraint(x, pltpu.HBM)
        for x in (params, offsets.T, image, background, psf_y, psf_x)
    )
    partners = [pltpu.SemaphoreType.DMA((PARTNERS,))] * 2
    slots, conv_high, conv_low, back_high, back_low, pulls, prior = pl.pallas_call(
        send_kernel,
        out_shape=[shape(SLOTS, LANES)]
        + [shape(2, BANDS, QUAD, COLS, kind=bf16)] * 2
        + [shape(2, BANDS, SPAN, COLS, kind=bf16)] * 2
        + [shape(3, SRC, LANES), shape(SRC, PARAMS)],
        in_specs=hbm(2) + [smem] + hbm(2),
        out_specs=vmem(7),
        scratch_shapes=[
            pltpu.VMEM((SRC, PARAMS), f32),
            pltpu.VMEM((2, SRC), jnp.int32),
            pltpu.VMEM((2, BANDS, TAPS), f32),
            pltpu.VMEM((SRC, LANES), f32),
            pltpu.VMEM((PARTNERS, SRC, LANES), f32),
            pltpu.SemaphoreType.DMA((4,)),
        ]
        + partners,
        compiler_params=pltpu.CompilerParams(
            collective_id=0, has_side_effects=True, vmem_limit_bytes=16 * 1024 * 1024
        ),
        name="send_slots",
    )(params, offsets, counts, psf_y, psf_x)
    values, onehot, rest_model, rest_parts = pl.pallas_call(
        find_kernel,
        out_shape=[
            shape(LANES, COLS),
            shape(SLOTS, COLS),
            shape(BANDS, QUAD, QUAD),
            shape(SLOTS, LANES),
        ],
        in_specs=vmem(1) + hbm(2) + vmem(4),
        out_specs=vmem(4),
        scratch_shapes=work_space(CHUNKS) + [pltpu.SemaphoreType.DMA((2,))],
        compiler_params=pltpu.CompilerParams(vmem_limit_bytes=40 * 1024 * 1024),
        name="find_sources",
    )(slots, background, image, conv_high, conv_low, back_high, back_low)
    return pl.pallas_call(
        return_kernel,
        out_shape=shape(SRC, PARAMS),
        in_specs=vmem(4) + hbm(2) + vmem(6),
        out_specs=vmem(1)[0],
        scratch_shapes=work_space(1)
        + [
            pltpu.VMEM((SLOTS, LANES), f32),
            pltpu.VMEM((PARTNERS, SRC, LANES), f32),
            pltpu.SemaphoreType.DMA((2,)),
        ]
        + partners,
        compiler_params=pltpu.CompilerParams(
            collective_id=1, has_side_effects=True, vmem_limit_bytes=24 * 1024 * 1024
        ),
        name="return_parts",
    )(
        values, onehot, rest_model, rest_parts, background, image,
        conv_high, conv_low, back_high, back_low, pulls, prior,
    )


def solution(mesh):
    placed = (
        P(("tile", "band"), None),
        P(("tile", "band"), None),
        P(("tile", "band")),
        P("tile", None, None, None),
        P("tile", None),
        P(),
        P(),
    )
    return jax.shard_map(
        body, mesh=mesh, in_specs=placed, out_specs=P(("tile", "band"), None), check_vma=False
    )
```

```python
import functools

import jax
import jax.numpy as jnp
from jax import lax
from jax.experimental import pallas as pl
from jax.experimental.pallas import tpu as pltpu
from jax.sharding import PartitionSpec as P

BANDS = 5
COMPONENTS = 12
PARAMS = 44
PATCH = 64
TAPS = 25
HALF = TAPS // 2
TILE_COLS = 8
TILE_SIDE = 384
QUAD = TILE_SIDE // 2
SRC = 8
TILES = 64
N_BAND = 4
PARTNERS = 16
SLOTS = PARTNERS * SRC
LANES = 128

TOP, LEFT, LIVE = 8, 9, 10
WEIGHT, SPREAD_Y, SPREAD_X = 16, 32, 48

PER_CHUNK = 21
COLS = 256
CHUNKS = -(-SLOTS // PER_CHUNK)
SPAN = 224
GROUP = 48
STEP = 80
HALF_SPAN = SPAN // 2
BACK_START = QUAD - HALF_SPAN

flux_scale = 2.0
prior_weight = 0.1
highest = lax.Precision.HIGHEST
f32 = jnp.float32
bf16 = jnp.bfloat16
MESH = pl.DeviceIdType.MESH


def iota(shape, axis):
    return lax.broadcasted_iota(jnp.int32, shape, axis)


def dot(a, b, dims=((1,), (0,)), precision=None):
    return lax.dot_general(a, b, (dims, ((), ())), precision=precision, preferred_element_type=f32)


def halves(x):
    high = x.astype(bf16)
    return high, (x - high.astype(f32)).astype(bf16)


def dot3(a, b, dims=((1,), (0,))):
    rows = a.shape[0] // 2
    both = dot(a, b[0], dims)
    return both[:rows] + (both[rows:] + dot(a[:rows], b[1], dims))


def wrapped_tile(row, col):
    return lax.rem(row + TILE_COLS, TILE_COLS) * TILE_COLS + lax.rem(col + TILE_COLS, TILE_COLS)


def viewers(tile, band):
    home = lax.rem(tile + TILES // 2, TILES)
    row, col = home // TILE_COLS, lax.rem(home, TILE_COLS)
    found = []
    for step_y, half_y in ((1, 0), (-1, 1), (0, 0), (0, 1)):
        for step_x, half_x in ((1, 0), (-1, 1), (0, 0), (0, 1)):
            far = 2 * abs(step_y) + abs(step_x)
            answer = (2 * abs(step_y) + half_y) * 4 + 2 * abs(step_x) + half_x
            found.append(
                (wrapped_tile(row + step_y, col + step_x), 2 * half_y + half_x, far * N_BAND + band, answer)
            )
    return found


def owners(tile, band):
    row, col = tile // TILE_COLS, lax.rem(tile, TILE_COLS)
    half_y, half_x = band // 2, lax.rem(band, 2)
    found = []
    for far_y in (1, 0):
        for far_x in (1, 0):
            home = wrapped_tile(row + far_y * (2 * half_y - 1), col + far_x * (2 * half_x - 1))
            holder = lax.rem(home + TILES // 2, TILES)
            answer = (2 * far_y + half_y) * 4 + 2 * far_x + half_x
            for other in range(N_BAND):
                found.append((holder, other, (2 * far_y + far_x) * N_BAND + other, answer))
    return found


def parameter_lanes():
    lane = iota((1, LANES), 1)
    source = jnp.where(lane < BANDS + 2, lane, -1)
    source = jnp.where(lane == BANDS + 2, PARAMS - 1, source)
    for j, base in enumerate((WEIGHT, SPREAD_Y, SPREAD_X)):
        here = (lane >= base) & (lane < base + COMPONENTS)
        source = jnp.where(here, BANDS + 2 + 3 * (lane - base) + j, source)
    return (iota((PARAMS, LANES), 0) == source).astype(f32)


def derived(params, lanes):
    raw = dot(params, lanes, precision=highest)
    lane = iota(raw.shape, 1)
    is_flux = lane < BANDS
    is_shift = (lane >= BANDS) & (lane < BANDS + 2)
    is_weight = (lane >= WEIGHT) & (lane < WEIGHT + COMPONENTS)
    is_spread = ((lane >= SPREAD_Y) & (lane < SPREAD_Y + COMPONENTS)) | (
        (lane >= SPREAD_X) & (lane < SPREAD_X + COMPONENTS)
    )
    most = jnp.max(jnp.where(is_weight, raw, -jnp.inf), axis=1, keepdims=True)
    power = jnp.where(is_weight, jnp.exp(jnp.where(is_weight, raw - most, 0.0)), 0.0)
    weight = power / jnp.sum(power, axis=1, keepdims=True)
    decay = jnp.exp(-jnp.abs(raw))
    soft = jnp.maximum(raw, 0.0) + jnp.log1p(decay)
    sigmoid = jnp.where(raw >= 0.0, 1.0, decay) / (1.0 + decay)
    curve = jnp.tanh(raw)
    softness = jnp.exp(0.25 * raw[:, BANDS + 2 : BANDS + 3])
    scale = (PATCH / 32.0) * softness
    spread = (0.5 + soft) * scale
    return is_flux, is_shift, is_weight, is_spread, weight, soft, sigmoid, curve, scale, spread


def start_copies(pairs, sems):
    copies = [pltpu.make_async_copy(src, dst, sems.at[i]) for i, (src, dst) in enumerate(pairs)]
    for copy in copies:
        copy.start()
    return copies


def build_tables(taps, conv, back):
    tap, spot = iota((TAPS, COLS), 0), iota((TAPS, COLS), 1)

    def spread_out(x, places):
        return dot(x, (places == spot).astype(bf16))

    def turned(row, rows, shift):
        wide = jnp.broadcast_to(row, (rows, COLS))
        return pltpu.roll(wide, shift, 1, stride=1, stride_axis=0)

    lane = iota((HALF_SPAN, COLS), 1)
    for side in range(2):
        high, low = halves(taps[side])
        ahead = spread_out(high, tap) + spread_out(high, tap + STEP) + spread_out(low, tap + 2 * STEP)
        behind = [spread_out(half, lax.rem(COLS - tap, COLS)) for half in (high, low)]
        for b in range(BANDS):
            conv[side, b * GROUP : (b + 1) * GROUP, :] = turned(ahead[b : b + 1], GROUP, 0).astype(bf16)
            for part in range(2):
                shift = (HALF_SPAN - BACK_START) * part
                near = turned(behind[0][b : b + 1], HALF_SPAN, shift)
                far = turned(behind[0][b : b + 1], HALF_SPAN, shift + HALF_SPAN)
                small = turned(behind[1][b : b + 1], HALF_SPAN, shift)
                both = jnp.where(lane < HALF_SPAN, near, jnp.where(lane < SPAN, far, 0.0))
                small = jnp.where(lane < HALF_SPAN, small, 0.0)
                cols = slice(b * COLS, (b + 1) * COLS)
                back[side, part, :HALF_SPAN, cols] = both.astype(bf16)
                back[side, part, HALF_SPAN:, cols] = small.astype(bf16)


def send_kernel(
    params,
    offsets,
    counts,
    psf_y,
    psf_x,
    out,
    conv,
    back,
    pulls,
    prior,
    theta,
    place,
    taps,
    mine,
    landed,
    load_sem,
    send_sem,
    recv_sem,
):
    tile, band = lax.axis_index("tile"), lax.axis_index("band")
    barrier = pltpu.get_barrier_semaphore()
    for other_tile, other_band, _, _ in owners(tile, band):
        pl.semaphore_signal(barrier, inc=1, device_id=(other_tile, other_band), device_id_type=MESH)
    loads = start_copies(
        ((params, theta), (offsets, place), (psf_y, taps.at[0]), (psf_x, taps.at[1])), load_sem
    )
    for load in loads:
        load.wait()
    is_flux, is_shift, is_weight, is_spread, weight, soft, sigmoid, curve, scale, spread = derived(
        theta[...], parameter_lanes()
    )
    slot, lane = iota((SRC, LANES), 0), iota((SRC, LANES), 1)
    live = (slot < counts[0]).astype(f32)
    row = jnp.where(is_flux, flux_scale * soft * live, 0.0)
    row = jnp.where(is_shift, (PATCH / 16.0) * curve, row)
    row = jnp.where(is_weight, weight, row)
    row = jnp.where(is_spread, spread, row)
    start = place[...].astype(f32)
    diagonal = iota((SRC, SRC), 0) == iota((SRC, SRC), 1)
    for side in range(2):
        start_side = jnp.sum(jnp.where(diagonal, start[side : side + 1, :], 0.0), axis=1, keepdims=True)
        row = jnp.where(lane == TOP + side, start_side, row)
    mine[...] = jnp.where(lane == LIVE, live, row)

    slope = jnp.where(is_flux, sigmoid / soft, 0.0)
    slope = jnp.where(is_shift, (PATCH / 16.0) * (1.0 - curve * curve), slope)
    slope = jnp.where(is_weight, 1.0, slope)
    pulls[0] = jnp.where(is_spread, scale * sigmoid, slope)
    pulls[1] = jnp.where(is_weight, weight, 0.0)
    pulls[2] = jnp.where(is_spread, spread, 0.0)
    prior[...] = prior_weight * theta[...] * live[:, :PARAMS]

    pl.semaphore_wait(barrier, PARTNERS)
    copies = []
    for i, (other_tile, other_band, block, _) in enumerate(viewers(tile, band)):
        copy = pltpu.make_async_remote_copy(
            src_ref=mine,
            dst_ref=landed.at[block],
            send_sem=send_sem.at[i],
            recv_sem=recv_sem.at[block],
            device_id=(other_tile, other_band),
            device_id_type=MESH,
        )
        copy.start()
        copies.append(copy)

    build_tables(taps, conv, back)

    for i, (other_tile, other_band, block, _) in enumerate(reversed(owners(tile, band))):
        pltpu.make_async_remote_copy(
            src_ref=mine,
            dst_ref=landed.at[block],
            send_sem=send_sem.at[i],
            recv_sem=recv_sem.at[block],
            device_id=(other_tile, other_band),
            device_id_type=MESH,
        ).wait_recv()
        out[block * SRC : (block + 1) * SRC, :] = landed[block]
    for copy in copies:
        copy.wait_send()


def quadrant_of(image, tile, band):
    half_y, half_x = band // 2, lax.rem(band, 2)
    rows = pl.ds(pl.multiple_of(half_y * QUAD, QUAD), QUAD)
    cols = pl.ds(pl.multiple_of(half_x * (COLS // 2), COLS // 2), COLS)
    return image.at[0, :, rows, cols]


def column_comps():
    column = iota((1, COLS), 1)
    place = (column * 5462) >> 16
    return place, iota((16, COLS), 0) == column - COMPONENTS * place


def one_of(values, base):
    mine = column_comps()[1]
    return jnp.sum(jnp.where(mine, values[base : base + 16], 0.0), axis=0, keepdims=True)


def geometry(values, side):
    spread = one_of(values, (SPREAD_Y, SPREAD_X)[side])
    inverse = 1.0 / jnp.where(spread > 0.0, spread, 1.0)
    shift = values[BANDS + side : BANDS + side + 1]
    start = values[TOP + side : TOP + side + 1]
    spot = iota((SPAN, COLS), 0).astype(f32) - (start + float(HALF))
    inside = (spot >= 0.0) & (spot < PATCH)
    ratio = (spot + (0.5 - PATCH / 2.0) - shift) * inverse
    spot = iota((QUAD, COLS), 0).astype(f32) - start
    window = ((spot >= 0.0) & (spot < PATCH)).astype(f32)
    return inverse, inside, ratio, window


def render(values, conv, profiles, factors, model, c):
    y_factor, x_factor = factors
    weight = one_of(values, WEIGHT)
    for side in range(2):
        _, inside, ratio, window = geometry(values, side)
        profile = jnp.where(inside, jnp.exp(-0.5 * ratio * ratio), 0.0)
        profiles[c, side] = profile
        high, low = halves(profile)
        for start in range(0, QUAD, GROUP):
            rows = slice(start, start + STEP)
            blank = jnp.zeros((COLS - 3 * STEP, COLS), bf16)
            stack = jnp.concatenate([high[rows], low[rows], high[rows], blank], axis=0)
            factor = dot(conv[side], stack)
            seen = window[start : start + GROUP]
            for b in range(BANDS):
                scale = seen * (weight * values[b : b + 1]) if side == 0 else seen
                high_low = halves(factor[b * GROUP : (b + 1) * GROUP] * scale)
                for half in range(2):
                    put = half * QUAD + start
                    factors[side][c, b, put : put + GROUP] = high_low[half]
    for b in range(BANDS):
        x = (x_factor[c, b, :QUAD], x_factor[c, b, QUAD:])
        model[b] += dot3(y_factor[c, b], x, ((1,), (1,)))


def leave(pixels, background, model, residual, half_x):
    turn = lax.rem(COLS - half_x * (QUAD - COLS // 2), COLS)
    for b in range(BANDS):
        observed = pltpu.roll(pixels[b], turn, 1)[:, :QUAD]
        left = observed / (background[0:1, b : b + 1] + model[b]) - 1.0
        left = left * (1.0 / (PATCH * PATCH))
        for way, r in enumerate((left, left.T)):
            high_low = halves(r)
            for half in range(2):
                residual[way, b, half * QUAD : (half + 1) * QUAD] = high_low[half]


def pull(values, onehot, back, profiles, factors, residual, stack, c):
    y_factor, x_factor = factors
    mine = column_comps()[1]
    weight = one_of(values, WEIGHT)
    rows = []
    inverse_y, _, ratio_y, window_y = geometry(values, 0)
    inverse_x, _, ratio_x, window_x = geometry(values, 1)
    blank = jnp.zeros((COLS - SPAN, COLS), bf16)
    for b in range(BANDS):
        y = (y_factor[c, b, :QUAD], y_factor[c, b, QUAD:])
        x = (x_factor[c, b, :QUAD], x_factor[c, b, QUAD:])
        along_y = dot3(residual[0, b], x)
        along_x = dot3(residual[1, b], y)
        factor = y[0].astype(f32) + y[1].astype(f32)
        rows.append(jnp.sum(along_y * factor, axis=0, keepdims=True))
        along_y = along_y * (window_y * (weight * values[b : b + 1]))
        along_x = along_x * window_x
        for side, along in enumerate((along_y, along_x)):
            high, low = halves(along)
            for part, start in enumerate((0, BACK_START)):
                here = slice(start, start + HALF_SPAN)
                put = b * COLS
                stack[side, part, put : put + HALF_SPAN] = high[here]
                stack[side, part, put + HALF_SPAN : put + SPAN] = low[here]
                stack[side, part, put + SPAN : put + COLS] = blank
    ds = []
    for side in range(2):
        d = []
        for part in range(2):
            both = dot(back[side, part], stack[side, part])
            d.append(both[:HALF_SPAN] + both[HALF_SPAN:])
        ds.append(jnp.concatenate(d, axis=0))
    by_comp = rows[0] + rows[1] + rows[2] + rows[3] + rows[4]
    spreads = []
    for side, (d, inverse, ratio) in enumerate(((ds[0], inverse_y, ratio_y), (ds[1], inverse_x, ratio_x))):
        first = d * profiles[c, side] * ratio
        rows.append(inverse * jnp.sum(first, axis=0, keepdims=True))
        spreads.append(inverse * jnp.sum(first * ratio, axis=0, keepdims=True))
    pieces = rows + [jnp.zeros((16 - len(rows), COLS), f32)]
    for by in (by_comp, spreads[0], spreads[1]):
        pieces.append(jnp.where(mine, by, 0.0))
    pieces.append(jnp.zeros((LANES - 64, COLS), f32))
    return dot(onehot, jnp.concatenate(pieces, axis=0), ((1,), (1,)), highest)


def find_kernel(
    slots,
    background,
    image,
    conv,
    back,
    values_out,
    onehot_out,
    rest_model,
    rest_parts,
    sky,
    pixels,
    profiles,
    y_factor,
    x_factor,
    whole,
    residual,
    stack,
    load_sem,
):
    tile, band = lax.axis_index("tile"), lax.axis_index("band")
    row, col = tile // TILE_COLS, lax.rem(tile, TILE_COLS)
    half_y, half_x = band // 2, lax.rem(band, 2)

    slot = iota((SLOTS, LANES), 0)
    lane = iota((SLOTS, LANES), 1)
    far_y, far_x = slot // (SLOTS // 2), lax.rem(slot // (SLOTS // 4), 2)

    def moved(far, half, place):
        origin = jnp.where(far == 0, 0, TILE_SIDE * (2 * half - 1)) - QUAD * half
        beyond = place + 2 * half - 1
        there = (far == 0) | ((beyond >= 0) & (beyond < TILE_COLS))
        return origin.astype(f32), there

    origin_y, there_y = moved(far_y, half_y, row)
    origin_x, there_x = moved(far_x, half_x, col)
    data = slots[...]
    data = jnp.where(lane == TOP, data + origin_y, jnp.where(lane == LEFT, data + origin_x, data))
    top, left, live = data[:, TOP : TOP + 1], data[:, LEFT : LEFT + 1], data[:, LIVE : LIVE + 1]
    reach = (live > 0.0) & (top > -PATCH) & (top < QUAD) & (left > -PATCH) & (left < QUAD)
    active = jnp.where(there_y & there_x & reach, 1.0, 0.0)
    before = jnp.where(lane < slot, 1.0, 0.0).astype(bf16)
    order = dot(before, active.astype(bf16))
    count = jnp.sum(active[:, 0:1]).astype(jnp.int32)
    order = jnp.where(active > 0.0, order, -1.0)[:, 0:1].astype(jnp.int32)
    place = column_comps()[0]

    def picked(c):
        return jnp.where((place < PER_CHUNK) & (order - c * PER_CHUNK == place), 1.0, 0.0)

    def gathered(c):
        return dot(data, picked(c), ((0,), (0,)), highest)

    onehot_out[...] = picked(0)
    values_out[...] = gathered(0)
    rest_model[...] = jnp.zeros_like(rest_model)
    rest_parts[...] = jnp.zeros_like(rest_parts)

    @pl.when(count > PER_CHUNK)
    def _():
        factors = (y_factor, x_factor)
        loads = start_copies(
            ((quadrant_of(image, tile, band), pixels), (background, sky)), load_sem
        )
        chunks = (count + PER_CHUNK - 1) // PER_CHUNK

        def add(c, carry):
            render(gathered(c), conv, profiles, factors, rest_model, c)
            return carry

        lax.fori_loop(1, chunks, add, 0)
        whole[...] = rest_model[...]
        render(gathered(0), conv, profiles, factors, whole, 0)
        for load in loads:
            load.wait()
        leave(pixels, sky, whole, residual, half_x)

        def take(c, carry):
            rest_parts[...] += pull(gathered(c), picked(c), back, profiles, factors, residual, stack, c)
            return carry

        lax.fori_loop(1, chunks, take, 0)


def return_kernel(
    values_in,
    onehot,
    rest_model,
    rest_parts,
    background,
    image,
    conv,
    back,
    pulls,
    prior,
    out,
    sky,
    pixels,
    profiles,
    y_factor,
    x_factor,
    model,
    residual,
    stack,
    parts,
    landed,
    load_sem,
    send_sem,
    recv_sem,
):
    tile, band = lax.axis_index("tile"), lax.axis_index("band")
    half_x = lax.rem(band, 2)
    barrier = pltpu.get_barrier_semaphore()
    for other_tile, other_band, _, _ in viewers(tile, band):
        pl.semaphore_signal(barrier, inc=1, device_id=(other_tile, other_band), device_id_type=MESH)
    loads = start_copies(((quadrant_of(image, tile, band), pixels), (background, sky)), load_sem)
    factors = (y_factor, x_factor)
    values = values_in[...]
    model[...] = rest_model[...]
    render(values, conv, profiles, factors, model, 0)
    for load in loads:
        load.wait()
    leave(pixels, sky, model, residual, half_x)
    parts[...] = rest_parts[...] + pull(values, onehot[...], back, profiles, factors, residual, stack, 0)

    pl.semaphore_wait(barrier, PARTNERS)
    copies = []
    for i, (other_tile, other_band, block, answer) in enumerate(owners(tile, band)):
        copy = pltpu.make_async_remote_copy(
            src_ref=parts.at[block * SRC : (block + 1) * SRC, :],
            dst_ref=landed.at[answer],
            send_sem=send_sem.at[i],
            recv_sem=recv_sem.at[answer],
            device_id=(other_tile, other_band),
            device_id_type=MESH,
        )
        copy.start()
        copies.append(copy)
    lanes = parameter_lanes().astype(bf16)
    total = jnp.zeros((SRC, LANES), f32)
    for i, (other_tile, other_band, _, answer) in enumerate(reversed(viewers(tile, band))):
        pltpu.make_async_remote_copy(
            src_ref=parts.at[0:SRC, :],
            dst_ref=landed.at[answer],
            send_sem=send_sem.at[i],
            recv_sem=recv_sem.at[answer],
            device_id=(other_tile, other_band),
            device_id_type=MESH,
        ).wait_recv()
        total = total + landed[answer]
    lane = iota((SRC, LANES), 1)
    is_weight = (lane >= WEIGHT) & (lane < WEIGHT + COMPONENTS)
    all_weights = jnp.sum(jnp.where(is_weight, total, 0.0), axis=1, keepdims=True)
    all_spreads = jnp.sum(total * pulls[2], axis=1, keepdims=True)
    pulled = total * pulls[0] - pulls[1] * all_weights
    pulled = jnp.where(lane == BANDS + 2, 0.25 * all_spreads, pulled)
    high, low = halves(pulled)
    rest = (pulled - high.astype(f32) - low.astype(f32)).astype(bf16)
    thirds = dot(jnp.concatenate([high, low, rest], axis=0), lanes, ((1,), (1,)))
    out[...] = thirds[:SRC] + (thirds[SRC : 2 * SRC] + thirds[2 * SRC :]) - prior[...]
    for copy in copies:
        copy.wait_send()


def vmem(count):
    return [pl.BlockSpec(memory_space=pltpu.VMEM)] * count


def hbm(count):
    return [pl.BlockSpec(memory_space=pltpu.HBM)] * count


def work_space(chunks):
    return [
        pltpu.VMEM((1, BANDS), f32),
        pltpu.VMEM((BANDS, QUAD, COLS), f32),
        pltpu.VMEM((chunks, 2, SPAN, COLS), f32),
        pltpu.VMEM((chunks, BANDS, 2 * QUAD, COLS), bf16),
        pltpu.VMEM((chunks, BANDS, 2 * QUAD, COLS), bf16),
        pltpu.VMEM((BANDS, QUAD, QUAD), f32),
        pltpu.VMEM((2, BANDS, 2 * QUAD, QUAD), bf16),
        pltpu.VMEM((2, 2, BANDS * COLS, COLS), bf16),
    ]


def shape(*dims, kind=f32):
    return jax.ShapeDtypeStruct(dims, kind)


def body(params, offsets, counts, image, background, psf_y, psf_x):
    smem = pl.BlockSpec(memory_space=pltpu.SMEM)
    params, offsets, image, background, psf_y, psf_x = (
        pltpu.with_memory_space_constraint(x, pltpu.HBM)
        for x in (params, offsets.T, image, background, psf_y, psf_x)
    )
    partners = [pltpu.SemaphoreType.DMA((PARTNERS,))] * 2
    slots, conv, back, pulls, prior = pl.pallas_call(
        send_kernel,
        out_shape=[shape(SLOTS, LANES)]
        + [shape(2, BANDS * GROUP, COLS, kind=bf16), shape(2, 2, SPAN, BANDS * COLS, kind=bf16)]
        + [shape(3, SRC, LANES), shape(SRC, PARAMS)],
        in_specs=hbm(2) + [smem] + hbm(2),
        out_specs=vmem(5),
        scratch_shapes=[
            pltpu.VMEM((SRC, PARAMS), f32),
            pltpu.VMEM((2, SRC), jnp.int32),
            pltpu.VMEM((2, BANDS, TAPS), f32),
            pltpu.VMEM((SRC, LANES), f32),
            pltpu.VMEM((PARTNERS, SRC, LANES), f32),
            pltpu.SemaphoreType.DMA((4,)),
        ]
        + partners,
        compiler_params=pltpu.CompilerParams(
            collective_id=0, has_side_effects=True, vmem_limit_bytes=16 * 1024 * 1024
        ),
        name="send_slots",
    )(params, offsets, counts, psf_y, psf_x)
    values, onehot, rest_model, rest_parts = pl.pallas_call(
        find_kernel,
        out_shape=[
            shape(LANES, COLS),
            shape(SLOTS, COLS),
            shape(BANDS, QUAD, QUAD),
            shape(SLOTS, LANES),
        ],
        in_specs=vmem(1) + hbm(2) + vmem(2),
        out_specs=vmem(4),
        scratch_shapes=work_space(CHUNKS) + [pltpu.SemaphoreType.DMA((2,))],
        compiler_params=pltpu.CompilerParams(vmem_limit_bytes=40 * 1024 * 1024),
        name="find_sources",
    )(slots, background, image, conv, back)
    return pl.pallas_call(
        return_kernel,
        out_shape=shape(SRC, PARAMS),
        in_specs=vmem(4) + hbm(2) + vmem(4),
        out_specs=vmem(1)[0],
        scratch_shapes=work_space(1)
        + [
            pltpu.VMEM((SLOTS, LANES), f32),
            pltpu.VMEM((PARTNERS, SRC, LANES), f32),
            pltpu.SemaphoreType.DMA((2,)),
        ]
        + partners,
        compiler_params=pltpu.CompilerParams(
            collective_id=1, has_side_effects=True, vmem_limit_bytes=24 * 1024 * 1024
        ),
        name="return_parts",
    )(
        values, onehot, rest_model, rest_parts, background, image, conv, back, pulls, prior
    )


def solution(mesh):
    placed = (
        P(("tile", "band"), None),
        P(("tile", "band"), None),
        P(("tile", "band")),
        P("tile", None, None, None),
        P("tile", None),
        P(),
        P(),
    )
    return jax.shard_map(
        body, mesh=mesh, in_specs=placed, out_specs=P(("tile", "band"), None), check_vma=False
    )
```

```python
import functools

import jax
import jax.numpy as jnp
from jax import lax
from jax.experimental import pallas as pl
from jax.experimental.pallas import tpu as pltpu
from jax.sharding import PartitionSpec as P

BANDS = 5
COMPONENTS = 12
PARAMS = 44
PATCH = 64
TAPS = 25
HALF = TAPS // 2
TILE_COLS = 8
TILE_SIDE = 384
QUAD = TILE_SIDE // 2
SRC = 8
TILES = 64
N_BAND = 4
PARTNERS = 16
SLOTS = PARTNERS * SRC
LANES = 128

TOP, LEFT, LIVE = 8, 9, 10
WEIGHT, SPREAD_Y, SPREAD_X = 16, 32, 48
HALVES = 64

PER_CHUNK = 21
COLS = 256
CHUNKS = -(-SLOTS // PER_CHUNK)
SPAN = 224
GROUP = 48
STEP = 80
HALF_SPAN = SPAN // 2
BACK_START = QUAD - HALF_SPAN

flux_scale = 2.0
prior_weight = 0.1
highest = lax.Precision.HIGHEST
f32 = jnp.float32
bf16 = jnp.bfloat16
MESH = pl.DeviceIdType.MESH


def iota(shape, axis):
    return lax.broadcasted_iota(jnp.int32, shape, axis)


def dot(a, b, dims=((1,), (0,)), precision=None):
    return lax.dot_general(a, b, (dims, ((), ())), precision=precision, preferred_element_type=f32)


def halves(x):
    high = x.astype(bf16)
    return high, (x - high.astype(f32)).astype(bf16)


def dot3(a, b, dims=((1,), (0,))):
    rows = a.shape[0] // 2
    both = dot(a, b[0], dims)
    return both[:rows] + (both[rows:] + dot(a[:rows], b[1], dims))


def wrapped_tile(row, col):
    return lax.rem(row + TILE_COLS, TILE_COLS) * TILE_COLS + lax.rem(col + TILE_COLS, TILE_COLS)


def viewers(tile, band):
    home = lax.rem(tile + TILES // 2, TILES)
    row, col = home // TILE_COLS, lax.rem(home, TILE_COLS)
    found = []
    for step_y, half_y in ((1, 0), (-1, 1), (0, 0), (0, 1)):
        for step_x, half_x in ((1, 0), (-1, 1), (0, 0), (0, 1)):
            far = 2 * abs(step_y) + abs(step_x)
            answer = (2 * abs(step_y) + half_y) * 4 + 2 * abs(step_x) + half_x
            found.append(
                (wrapped_tile(row + step_y, col + step_x), 2 * half_y + half_x, far * N_BAND + band, answer)
            )
    return found


def owners(tile, band):
    row, col = tile // TILE_COLS, lax.rem(tile, TILE_COLS)
    half_y, half_x = band // 2, lax.rem(band, 2)
    found = []
    for far_y in (1, 0):
        for far_x in (1, 0):
            home = wrapped_tile(row + far_y * (2 * half_y - 1), col + far_x * (2 * half_x - 1))
            holder = lax.rem(home + TILES // 2, TILES)
            answer = (2 * far_y + half_y) * 4 + 2 * far_x + half_x
            for other in range(N_BAND):
                found.append((holder, other, (2 * far_y + far_x) * N_BAND + other, answer))
    return found


def parameter_lanes():
    lane = iota((1, LANES), 1)
    source = jnp.where(lane < BANDS + 2, lane, -1)
    source = jnp.where(lane == BANDS + 2, PARAMS - 1, source)
    for j, base in enumerate((WEIGHT, SPREAD_Y, SPREAD_X)):
        here = (lane >= base) & (lane < base + COMPONENTS)
        source = jnp.where(here, BANDS + 2 + 3 * (lane - base) + j, source)
    return (iota((PARAMS, LANES), 0) == source).astype(bf16)


def parameter_columns():
    lane = iota((LANES, LANES), 0)
    target = jnp.where(lane < BANDS + 2, lane, -1)
    target = jnp.where(lane == BANDS + 2, PARAMS - 1, target)
    for j, base in enumerate((WEIGHT, SPREAD_Y, SPREAD_X)):
        here = (lane >= base) & (lane < base + COMPONENTS)
        target = jnp.where(here, BANDS + 2 + 3 * (lane - base) + j, target)
    return (iota((LANES, LANES), 1) == target).astype(bf16)


def thirds_of(x):
    high, low = halves(x)
    return jnp.concatenate([high, low, (x - high.astype(f32) - low.astype(f32)).astype(bf16)], axis=0)


def summed(x):
    rows = x.shape[0] // 3
    return x[:rows] + (x[rows : 2 * rows] + x[2 * rows :])


def derived(params):
    raw = summed(dot(thirds_of(params), parameter_lanes()))
    lane = iota(raw.shape, 1)
    is_flux = lane < BANDS
    is_shift = (lane >= BANDS) & (lane < BANDS + 2)
    is_weight = (lane >= WEIGHT) & (lane < WEIGHT + COMPONENTS)
    is_spread = ((lane >= SPREAD_Y) & (lane < SPREAD_Y + COMPONENTS)) | (
        (lane >= SPREAD_X) & (lane < SPREAD_X + COMPONENTS)
    )
    most = jnp.max(jnp.where(is_weight, raw, -jnp.inf), axis=1, keepdims=True)
    power = jnp.where(is_weight, jnp.exp(jnp.where(is_weight, raw - most, 0.0)), 0.0)
    weight = power / jnp.sum(power, axis=1, keepdims=True)
    decay = jnp.exp(-jnp.abs(raw))
    soft = jnp.maximum(raw, 0.0) + jnp.log1p(decay)
    sigmoid = jnp.where(raw >= 0.0, 1.0, decay) / (1.0 + decay)
    curve = jnp.tanh(raw)
    softness = jnp.exp(0.25 * raw[:, BANDS + 2 : BANDS + 3])
    scale = (PATCH / 32.0) * softness
    spread = (0.5 + soft) * scale
    return raw, is_flux, is_shift, is_weight, is_spread, weight, soft, sigmoid, curve, scale, spread


def start_copies(pairs, sems):
    copies = [pltpu.make_async_copy(src, dst, sems.at[i]) for i, (src, dst) in enumerate(pairs)]
    for copy in copies:
        copy.start()
    return copies


def build_tables(taps, conv, back):
    tap, spot = iota((TAPS, COLS), 0), iota((TAPS, COLS), 1)

    def spread_out(x, places):
        return dot(x, (places == spot).astype(bf16))

    def turned(row, rows, shift):
        wide = jnp.broadcast_to(row, (rows, COLS))
        return pltpu.roll(wide, shift, 1, stride=1, stride_axis=0)

    lane = iota((HALF_SPAN, COLS), 1)
    for side in range(2):
        high, low = halves(taps[side])
        ahead = spread_out(high, tap) + spread_out(high, tap + STEP) + spread_out(low, tap + 2 * STEP)
        behind = [spread_out(half, lax.rem(COLS - tap, COLS)) for half in (high, low)]
        for b in range(BANDS):
            conv[side, b * GROUP : (b + 1) * GROUP, :] = turned(ahead[b : b + 1], GROUP, 0).astype(bf16)
            for part in range(2):
                shift = (HALF_SPAN - BACK_START) * part
                near = turned(behind[0][b : b + 1], HALF_SPAN, shift)
                far = turned(behind[0][b : b + 1], HALF_SPAN, shift + HALF_SPAN)
                small = turned(behind[1][b : b + 1], HALF_SPAN, shift)
                both = jnp.where(lane < HALF_SPAN, near, jnp.where(lane < SPAN, far, 0.0))
                small = jnp.where(lane < HALF_SPAN, small, 0.0)
                cols = slice(b * COLS, (b + 1) * COLS)
                back[side, part, :HALF_SPAN, cols] = both.astype(bf16)
                back[side, part, HALF_SPAN:, cols] = small.astype(bf16)


def send_kernel(
    params,
    offsets,
    counts,
    psf_y,
    psf_x,
    out,
    conv,
    back,
    pulls,
    prior,
    theta,
    place,
    taps,
    mine,
    landed,
    load_sem,
    send_sem,
    recv_sem,
):
    tile, band = lax.axis_index("tile"), lax.axis_index("band")
    loads = start_copies(
        ((params, theta), (offsets, place), (psf_y, taps.at[0]), (psf_x, taps.at[1])), load_sem
    )
    barrier = pltpu.get_barrier_semaphore()
    for other_tile, other_band, _, _ in owners(tile, band):
        pl.semaphore_signal(barrier, inc=1, device_id=(other_tile, other_band), device_id_type=MESH)
    for load in loads[:2]:
        load.wait()
    raw, is_flux, is_shift, is_weight, is_spread, weight, soft, sigmoid, curve, scale, spread = derived(
        theta[...]
    )
    slot, lane = iota((SRC, LANES), 0), iota((SRC, LANES), 1)
    live = (slot < counts[0]).astype(f32)
    row = jnp.where(is_flux, flux_scale * soft * live, 0.0)
    row = jnp.where(is_shift, (PATCH / 16.0) * curve, row)
    row = jnp.where(is_weight, weight, row)
    row = jnp.where(is_spread, spread, row)
    start = place[...].astype(f32)
    diagonal = iota((SRC, SRC), 0) == iota((SRC, SRC), 1)
    for side in range(2):
        start_side = jnp.sum(jnp.where(diagonal, start[side : side + 1, :], 0.0), axis=1, keepdims=True)
        row = jnp.where(lane == TOP + side, start_side, row)
    mine[...] = jnp.where(lane == LIVE, live, row)

    pl.semaphore_wait(barrier, PARTNERS)
    copies = []
    for i, (other_tile, other_band, block, _) in enumerate(viewers(tile, band)):
        copy = pltpu.make_async_remote_copy(
            src_ref=mine,
            dst_ref=landed.at[block],
            send_sem=send_sem.at[i],
            recv_sem=recv_sem.at[block],
            device_id=(other_tile, other_band),
            device_id_type=MESH,
        )
        copy.start()
        copies.append(copy)

    for load in loads[2:]:
        load.wait()
    build_tables(taps, conv, back)

    slope = jnp.where(is_flux, sigmoid / soft, 0.0)
    slope = jnp.where(is_shift, (PATCH / 16.0) * (1.0 - curve * curve), slope)
    slope = jnp.where(is_weight, 1.0, slope)
    pulls[0] = jnp.where(is_spread, scale * sigmoid, slope)
    pulls[1] = jnp.where(is_weight, 1.0, 0.0)
    pulls[2] = jnp.where(is_spread, spread, 0.0)
    columns = parameter_columns()
    prior[0] = prior_weight * summed(dot(thirds_of(raw), columns)) * live
    prior[1] = summed(dot(thirds_of(jnp.where(is_weight, weight, 0.0)), columns))

    for i, (other_tile, other_band, block, _) in enumerate(reversed(owners(tile, band))):
        pltpu.make_async_remote_copy(
            src_ref=mine,
            dst_ref=landed.at[block],
            send_sem=send_sem.at[i],
            recv_sem=recv_sem.at[block],
            device_id=(other_tile, other_band),
            device_id_type=MESH,
        ).wait_recv()
        out[block * SRC : (block + 1) * SRC, :] = landed[block]
    for copy in copies:
        copy.wait_send()


def quadrant_of(image, tile, band):
    half_y, half_x = band // 2, lax.rem(band, 2)
    rows = pl.ds(pl.multiple_of(half_y * QUAD, QUAD), QUAD)
    cols = pl.ds(pl.multiple_of(half_x * (COLS // 2), COLS // 2), COLS)
    return image.at[0, :, rows, cols]


def column_comps():
    column = iota((1, COLS), 1)
    place = (column * 5462) >> 16
    return place, iota((16, COLS), 0) == column - COMPONENTS * place


def one_of(values, base):
    mine = column_comps()[1]
    return jnp.sum(jnp.where(mine, values[base : base + 16], 0.0), axis=0, keepdims=True)


def geometry(values, side):
    spread = one_of(values, (SPREAD_Y, SPREAD_X)[side])
    inverse = 1.0 / jnp.where(spread > 0.0, spread, 1.0)
    shift = values[BANDS + side : BANDS + side + 1]
    start = values[TOP + side : TOP + side + 1]
    spot = iota((SPAN, COLS), 0).astype(f32) - (start + float(HALF))
    inside = (spot >= 0.0) & (spot < PATCH)
    ratio = (spot + (0.5 - PATCH / 2.0) - shift) * inverse
    spot = iota((QUAD, COLS), 0).astype(f32) - start
    window = ((spot >= 0.0) & (spot < PATCH)).astype(f32)
    return inverse, inside, ratio, window


def render(values, conv, profiles, factors, c):
    weight = one_of(values, WEIGHT)
    for side in range(2):
        _, inside, ratio, window = geometry(values, side)
        profile = jnp.where(inside, jnp.exp(-0.5 * ratio * ratio), 0.0)
        profiles[c, side] = profile
        high, low = halves(profile)
        for start in range(0, QUAD, GROUP):
            rows = slice(start, start + STEP)
            blank = jnp.zeros((COLS - 3 * STEP, COLS), bf16)
            stack = jnp.concatenate([high[rows], low[rows], high[rows], blank], axis=0)
            factor = dot(conv[side], stack)
            seen = window[start : start + GROUP]
            for b in range(BANDS):
                scale = seen * (weight * values[b : b + 1]) if side == 0 else seen
                high_low = halves(factor[b * GROUP : (b + 1) * GROUP] * scale)
                for half in range(2):
                    put = half * QUAD + start
                    factors[side][c, b, put : put + GROUP] = high_low[half]


def model_of(factors, c, b):
    y_factor, x_factor = factors
    x = (x_factor[c, b, :QUAD], x_factor[c, b, QUAD:])
    return dot3(y_factor[c, b], x, ((1,), (1,)))


def leave(pixels, background, model, residual, half_x, b):
    turn = lax.rem(COLS - half_x * (QUAD - COLS // 2), COLS)
    observed = pltpu.roll(pixels[b], turn, 1)[:, :QUAD]
    left = observed / (background[0:1, b : b + 1] + model) - 1.0
    left = left * (1.0 / (PATCH * PATCH))
    for way, r in enumerate((left, left.T)):
        high_low = halves(r)
        for half in range(2):
            residual[way, b, half * QUAD : (half + 1) * QUAD] = high_low[half]


def pull(values, onehot, back, profiles, factors, residual, stack, c):
    y_factor, x_factor = factors
    mine = column_comps()[1]
    weight = one_of(values, WEIGHT)
    rows = []
    inverse_y, _, ratio_y, window_y = geometry(values, 0)
    inverse_x, _, ratio_x, window_x = geometry(values, 1)
    blank = jnp.zeros((COLS - SPAN, COLS), bf16)
    for b in range(BANDS):
        y = (y_factor[c, b, :QUAD], y_factor[c, b, QUAD:])
        x = (x_factor[c, b, :QUAD], x_factor[c, b, QUAD:])
        along_y = dot3(residual[0, b], x)
        along_x = dot3(residual[1, b], y)
        factor = y[0].astype(f32) + y[1].astype(f32)
        rows.append(jnp.sum(along_y * factor, axis=0, keepdims=True))
        along_y = along_y * (window_y * (weight * values[b : b + 1]))
        along_x = along_x * window_x
        for side, along in enumerate((along_y, along_x)):
            high, low = halves(along)
            for part, start in enumerate((0, BACK_START)):
                here = slice(start, start + HALF_SPAN)
                put = b * COLS
                stack[side, part, put : put + HALF_SPAN] = high[here]
                stack[side, part, put + HALF_SPAN : put + SPAN] = low[here]
                stack[side, part, put + SPAN : put + COLS] = blank
    ds = []
    for side in range(2):
        d = []
        for part in range(2):
            both = dot(back[side, part], stack[side, part])
            d.append(both[:HALF_SPAN] + both[HALF_SPAN:])
        ds.append(jnp.concatenate(d, axis=0))
    by_comp = rows[0] + rows[1] + rows[2] + rows[3] + rows[4]
    spreads = []
    for side, (d, inverse, ratio) in enumerate(((ds[0], inverse_y, ratio_y), (ds[1], inverse_x, ratio_x))):
        first = d * profiles[c, side] * ratio
        rows.append(inverse * jnp.sum(first, axis=0, keepdims=True))
        spreads.append(inverse * jnp.sum(first * ratio, axis=0, keepdims=True))
    pieces = rows + [jnp.zeros((16 - len(rows), COLS), f32)]
    for by in (by_comp, spreads[0], spreads[1]):
        pieces.append(jnp.where(mine, by, 0.0))
    high_low = jnp.concatenate(halves(jnp.concatenate(pieces, axis=0)), axis=0)
    return dot(onehot, high_low, ((1,), (1,)))


def find(data, tile, band):
    row, col = tile // TILE_COLS, lax.rem(tile, TILE_COLS)
    half_y, half_x = band // 2, lax.rem(band, 2)
    slot = iota((SLOTS, LANES), 0)
    lane = iota((SLOTS, LANES), 1)
    far_y, far_x = slot // (SLOTS // 2), lax.rem(slot // (SLOTS // 4), 2)

    def moved(far, half, place):
        origin = jnp.where(far == 0, 0, TILE_SIDE * (2 * half - 1)) - QUAD * half
        beyond = place + 2 * half - 1
        there = (far == 0) | ((beyond >= 0) & (beyond < TILE_COLS))
        return origin.astype(f32), there

    origin_y, there_y = moved(far_y, half_y, row)
    origin_x, there_x = moved(far_x, half_x, col)
    data = data + jnp.where(lane == TOP, origin_y, jnp.where(lane == LEFT, origin_x, 0.0))
    is_place = (lane == TOP) | (lane == LEFT)
    reach = is_place & (data > -PATCH) & (data < QUAD) | (lane == LIVE) & (data > 0.0)
    met = jnp.where(reach & there_y & there_x, 1.0, 0.0).astype(bf16)
    active = jnp.where(dot(met, jnp.ones((LANES, LANES), bf16)) > 2.5, 1.0, 0.0)
    count = jnp.sum(active, axis=0, keepdims=True)

    def chunk_makers():
        before = jnp.where(lane < slot, 1.0, 0.0).astype(bf16)
        order = dot(before, active.astype(bf16))
        order = jnp.where(active > 0.0, order, -1.0)[:, 0:1].astype(jnp.int32)
        place = column_comps()[0]

        def picked(c):
            here = (place < PER_CHUNK) & (order - c * PER_CHUNK == place)
            return jnp.where(here, 1.0, 0.0).astype(bf16)

        thirds = thirds_of(data.T[:HALVES])

        def gathered(c):
            return summed(dot(thirds, picked(c)))

        return picked, gathered

    return count, chunk_makers


def more_kernel(
    slots,
    background,
    image,
    conv,
    back,
    rest_model,
    rest_parts,
    sky,
    pixels,
    profiles,
    y_factor,
    x_factor,
    residual,
    stack,
    load_sem,
):
    tile, band = lax.axis_index("tile"), lax.axis_index("band")
    counts, chunk_makers = find(slots[...], tile, band)
    count = counts[0, 0].astype(jnp.int32)

    @pl.when(count > PER_CHUNK)
    def _():
        picked, gathered = chunk_makers()
        factors = (y_factor, x_factor)
        loads = start_copies(
            ((quadrant_of(image, tile, band), pixels), (background, sky)), load_sem
        )
        chunks = (count + PER_CHUNK - 1) // PER_CHUNK
        rest_model[...] = jnp.zeros_like(rest_model)
        rest_parts[...] = jnp.zeros_like(rest_parts)

        def add(c, carry):
            render(gathered(c), conv, profiles, factors, c)
            for b in range(BANDS):
                rest_model[b] += model_of(factors, c, b)
            return carry

        lax.fori_loop(1, chunks, add, 0)
        render(gathered(0), conv, profiles, factors, 0)
        for load in loads:
            load.wait()
        for b in range(BANDS):
            model = rest_model[b] + model_of(factors, 0, b)
            leave(pixels, sky, model, residual, lax.rem(band, 2), b)

        def take(c, carry):
            rest_parts[...] += pull(gathered(c), picked(c), back, profiles, factors, residual, stack, c)
            return carry

        lax.fori_loop(1, chunks, take, 0)


def return_kernel(
    slots,
    rest_model,
    rest_parts,
    background,
    image,
    conv,
    back,
    pulls,
    prior,
    out,
    sky,
    pixels,
    profiles,
    y_factor,
    x_factor,
    residual,
    stack,
    parts,
    landed,
    load_sem,
    send_sem,
    recv_sem,
):
    tile, band = lax.axis_index("tile"), lax.axis_index("band")
    half_x = lax.rem(band, 2)
    barrier = pltpu.get_barrier_semaphore()
    for other_tile, other_band, _, _ in viewers(tile, band):
        pl.semaphore_signal(barrier, inc=1, device_id=(other_tile, other_band), device_id_type=MESH)
    loads = start_copies(((quadrant_of(image, tile, band), pixels), (background, sky)), load_sem)
    factors = (y_factor, x_factor)
    count, chunk_makers = find(slots[...], tile, band)
    picked, gathered = chunk_makers()
    onehot, values = picked(0), gathered(0)
    more = count[:, 0:1] > PER_CHUNK
    render(values, conv, profiles, factors, 0)
    for load in loads:
        load.wait()
    for b in range(BANDS):
        model = model_of(factors, 0, b) + jnp.where(more, rest_model[b], 0.0)
        leave(pixels, sky, model, residual, half_x, b)
    pulled = pull(values, onehot, back, profiles, factors, residual, stack, 0)
    parts[...] = pulled + jnp.where(more, rest_parts[...], 0.0)

    pl.semaphore_wait(barrier, PARTNERS)
    copies = []
    for i, (other_tile, other_band, block, answer) in enumerate(owners(tile, band)):
        copy = pltpu.make_async_remote_copy(
            src_ref=parts.at[block * SRC : (block + 1) * SRC, :],
            dst_ref=landed.at[answer],
            send_sem=send_sem.at[i],
            recv_sem=recv_sem.at[answer],
            device_id=(other_tile, other_band),
            device_id_type=MESH,
        )
        copy.start()
        copies.append(copy)
    lanes = jnp.concatenate([parameter_columns(), jnp.ones((LANES, LANES), bf16)], axis=1)
    prior_rows, weights, slopes = prior[0], prior[1], pulls[0]
    softness = iota((SRC, LANES), 1) == PARAMS - 1
    total = jnp.zeros((SRC, LANES), f32)
    for i, (other_tile, other_band, _, answer) in enumerate(reversed(viewers(tile, band))):
        pltpu.make_async_remote_copy(
            src_ref=parts.at[0:SRC, :],
            dst_ref=landed.at[answer],
            send_sem=send_sem.at[i],
            recv_sem=recv_sem.at[answer],
            device_id=(other_tile, other_band),
            device_id_type=MESH,
        ).wait_recv()
        total = total + landed[answer]
    total = total + pltpu.roll(total, HALVES, 1)
    three = jnp.concatenate([total * slopes, total * pulls[1], total * pulls[2]], axis=0)
    sums = summed(dot(thirds_of(three), lanes))
    alone = sums[:SRC, :LANES]
    all_weights, all_spreads = sums[SRC : 2 * SRC, LANES:], sums[2 * SRC :, LANES:]
    grad = alone - weights * all_weights + jnp.where(softness, 0.25 * all_spreads, 0.0) - prior_rows
    out[...] = grad[:, :PARAMS]
    for copy in copies:
        copy.wait_send()


def vmem(count):
    return [pl.BlockSpec(memory_space=pltpu.VMEM)] * count


def hbm(count):
    return [pl.BlockSpec(memory_space=pltpu.HBM)] * count


def work_space(chunks):
    return [
        pltpu.VMEM((1, BANDS), f32),
        pltpu.VMEM((BANDS, QUAD, COLS), f32),
        pltpu.VMEM((chunks, 2, SPAN, COLS), f32),
        pltpu.VMEM((chunks, BANDS, 2 * QUAD, COLS), bf16),
        pltpu.VMEM((chunks, BANDS, 2 * QUAD, COLS), bf16),
        pltpu.VMEM((2, BANDS, 2 * QUAD, QUAD), bf16),
        pltpu.VMEM((2, 2, BANDS * COLS, COLS), bf16),
    ]


def shape(*dims, kind=f32):
    return jax.ShapeDtypeStruct(dims, kind)


def body(params, offsets, counts, image, background, psf_y, psf_x):
    smem = pl.BlockSpec(memory_space=pltpu.SMEM)
    params, offsets, image, background, psf_y, psf_x = (
        pltpu.with_memory_space_constraint(x, pltpu.HBM)
        for x in (params, offsets.T, image, background, psf_y, psf_x)
    )
    partners = [pltpu.SemaphoreType.DMA((PARTNERS,))] * 2
    slots, conv, back, pulls, prior = pl.pallas_call(
        send_kernel,
        out_shape=[shape(SLOTS, LANES)]
        + [shape(2, BANDS * GROUP, COLS, kind=bf16), shape(2, 2, SPAN, BANDS * COLS, kind=bf16)]
        + [shape(3, SRC, LANES), shape(2, SRC, LANES)],
        in_specs=hbm(2) + [smem] + hbm(2),
        out_specs=vmem(5),
        scratch_shapes=[
            pltpu.VMEM((SRC, PARAMS), f32),
            pltpu.VMEM((2, SRC), jnp.int32),
            pltpu.VMEM((2, BANDS, TAPS), f32),
            pltpu.VMEM((SRC, LANES), f32),
            pltpu.VMEM((PARTNERS, SRC, LANES), f32),
            pltpu.SemaphoreType.DMA((4,)),
        ]
        + partners,
        compiler_params=pltpu.CompilerParams(
            collective_id=0, has_side_effects=True, vmem_limit_bytes=16 * 1024 * 1024
        ),
        name="send_slots",
    )(params, offsets, counts, psf_y, psf_x)
    rest_model, rest_parts = pl.pallas_call(
        more_kernel,
        out_shape=[shape(BANDS, QUAD, QUAD), shape(SLOTS, LANES)],
        in_specs=vmem(1) + hbm(2) + vmem(2),
        out_specs=vmem(2),
        scratch_shapes=work_space(CHUNKS) + [pltpu.SemaphoreType.DMA((2,))],
        compiler_params=pltpu.CompilerParams(vmem_limit_bytes=40 * 1024 * 1024),
        name="more_sources",
    )(slots, background, image, conv, back)
    return pl.pallas_call(
        return_kernel,
        out_shape=shape(SRC, PARAMS),
        in_specs=vmem(3) + hbm(2) + vmem(4),
        out_specs=vmem(1)[0],
        scratch_shapes=work_space(1)
        + [
            pltpu.VMEM((SLOTS, LANES), f32),
            pltpu.VMEM((PARTNERS, SRC, LANES), f32),
            pltpu.SemaphoreType.DMA((2,)),
        ]
        + partners,
        compiler_params=pltpu.CompilerParams(
            collective_id=1, has_side_effects=True, vmem_limit_bytes=24 * 1024 * 1024
        ),
        name="return_parts",
    )(
        slots, rest_model, rest_parts, background, image, conv, back, pulls, prior
    )


def solution(mesh):
    placed = (
        P(("tile", "band"), None),
        P(("tile", "band"), None),
        P(("tile", "band")),
        P("tile", None, None, None),
        P("tile", None),
        P(),
        P(),
    )
    return jax.shard_map(
        body, mesh=mesh, in_specs=placed, out_specs=P(("tile", "band"), None), check_vma=False
    )
```

```python
import functools

import jax
import jax.numpy as jnp
from jax import lax
from jax.experimental import pallas as pl
from jax.experimental.pallas import tpu as pltpu
from jax.sharding import PartitionSpec as P

BANDS = 5
COMPONENTS = 12
PARAMS = 44
PATCH = 64
TAPS = 25
HALF = TAPS // 2
TILE_COLS = 8
TILE_SIDE = 384
QUAD = TILE_SIDE // 2
SRC = 8
TILES = 64
N_BAND = 4
PARTNERS = 16
SLOTS = PARTNERS * SRC
LANES = 128

TOP, LEFT, LIVE = 8, 9, 10
WEIGHT, SPREAD_Y, SPREAD_X = 16, 32, 48
HALVES = 64

PER_CHUNK = 21
COLS = 256
CHUNKS = -(-SLOTS // PER_CHUNK)
SPAN = 224
GROUP = 48
STEP = 80
HALF_SPAN = SPAN // 2
BACK_START = QUAD - HALF_SPAN

flux_scale = 2.0
prior_weight = 0.1
highest = lax.Precision.HIGHEST
f32 = jnp.float32
bf16 = jnp.bfloat16
MESH = pl.DeviceIdType.MESH


def iota(shape, axis):
    return lax.broadcasted_iota(jnp.int32, shape, axis)


def dot(a, b, dims=((1,), (0,)), precision=None):
    return lax.dot_general(a, b, (dims, ((), ())), precision=precision, preferred_element_type=f32)


def halves(x):
    high = x.astype(bf16)
    return high, (x - high.astype(f32)).astype(bf16)


def dot3(a, b, dims=((1,), (0,))):
    rows = a.shape[0] // 2
    both = dot(a, b[0], dims)
    return both[:rows] + (both[rows:] + dot(a[:rows], b[1], dims))


def wrapped_tile(row, col):
    return lax.rem(row + TILE_COLS, TILE_COLS) * TILE_COLS + lax.rem(col + TILE_COLS, TILE_COLS)


def inside(row, col):
    return (row >= 0) & (row < TILE_COLS) & (col >= 0) & (col < TILE_COLS)


def viewers(tile, band):
    home = lax.rem(tile + TILES // 2, TILES)
    row, col = home // TILE_COLS, lax.rem(home, TILE_COLS)
    found = []
    for step_y, half_y in ((1, 0), (-1, 1), (0, 0), (0, 1)):
        for step_x, half_x in ((1, 0), (-1, 1), (0, 0), (0, 1)):
            far = 2 * abs(step_y) + abs(step_x)
            answer = (2 * abs(step_y) + half_y) * 4 + 2 * abs(step_x) + half_x
            to_row, to_col = row + step_y, col + step_x
            found.append(
                (
                    wrapped_tile(to_row, to_col),
                    2 * half_y + half_x,
                    far * N_BAND + band,
                    answer,
                    inside(to_row, to_col),
                )
            )
    return found


def owners(tile, band):
    row, col = tile // TILE_COLS, lax.rem(tile, TILE_COLS)
    half_y, half_x = band // 2, lax.rem(band, 2)
    found = []
    for far_y in (1, 0):
        for far_x in (1, 0):
            from_row, from_col = row + far_y * (2 * half_y - 1), col + far_x * (2 * half_x - 1)
            holder = lax.rem(wrapped_tile(from_row, from_col) + TILES // 2, TILES)
            answer = (2 * far_y + half_y) * 4 + 2 * far_x + half_x
            for other in range(N_BAND):
                block = (2 * far_y + far_x) * N_BAND + other
                found.append((holder, other, block, answer, inside(from_row, from_col)))
    return found


def greet(barrier, callers):
    for other_tile, other_band, _, _, there in callers:

        @pl.when(there)
        def _():
            pl.semaphore_signal(
                barrier, inc=1, device_id=(other_tile, other_band), device_id_type=MESH
            )


def how_many(partners):
    return sum(there.astype(jnp.int32) for _, _, _, _, there in partners)


def parameter_lanes():
    lane = iota((1, LANES), 1)
    source = jnp.where(lane < BANDS + 2, lane, -1)
    source = jnp.where(lane == BANDS + 2, PARAMS - 1, source)
    for j, base in enumerate((WEIGHT, SPREAD_Y, SPREAD_X)):
        here = (lane >= base) & (lane < base + COMPONENTS)
        source = jnp.where(here, BANDS + 2 + 3 * (lane - base) + j, source)
    return (iota((PARAMS, LANES), 0) == source).astype(bf16)


def parameter_columns():
    lane = iota((LANES, LANES), 0)
    target = jnp.where(lane < BANDS + 2, lane, -1)
    target = jnp.where(lane == BANDS + 2, PARAMS - 1, target)
    for j, base in enumerate((WEIGHT, SPREAD_Y, SPREAD_X)):
        here = (lane >= base) & (lane < base + COMPONENTS)
        target = jnp.where(here, BANDS + 2 + 3 * (lane - base) + j, target)
    return (iota((LANES, LANES), 1) == target).astype(bf16)


def thirds_of(x):
    high, low = halves(x)
    return jnp.concatenate([high, low, (x - high.astype(f32) - low.astype(f32)).astype(bf16)], axis=0)


def summed(x):
    rows = x.shape[0] // 3
    return x[:rows] + (x[rows : 2 * rows] + x[2 * rows :])


def derived(params):
    raw = summed(dot(thirds_of(params), parameter_lanes()))
    lane = iota(raw.shape, 1)
    is_flux = lane < BANDS
    is_shift = (lane >= BANDS) & (lane < BANDS + 2)
    is_weight = (lane >= WEIGHT) & (lane < WEIGHT + COMPONENTS)
    is_spread = ((lane >= SPREAD_Y) & (lane < SPREAD_Y + COMPONENTS)) | (
        (lane >= SPREAD_X) & (lane < SPREAD_X + COMPONENTS)
    )
    most = jnp.max(jnp.where(is_weight, raw, -jnp.inf), axis=1, keepdims=True)
    power = jnp.where(is_weight, jnp.exp(jnp.where(is_weight, raw - most, 0.0)), 0.0)
    weight = power / jnp.sum(power, axis=1, keepdims=True)
    decay = jnp.exp(-jnp.abs(raw))
    soft = jnp.maximum(raw, 0.0) + jnp.log1p(decay)
    sigmoid = jnp.where(raw >= 0.0, 1.0, decay) / (1.0 + decay)
    curve = jnp.tanh(raw)
    softness = jnp.exp(0.25 * raw[:, BANDS + 2 : BANDS + 3])
    scale = (PATCH / 32.0) * softness
    spread = (0.5 + soft) * scale
    return raw, is_flux, is_shift, is_weight, is_spread, weight, soft, sigmoid, curve, scale, spread


def start_copies(pairs, sems):
    copies = [pltpu.make_async_copy(src, dst, sems.at[i]) for i, (src, dst) in enumerate(pairs)]
    for copy in copies:
        copy.start()
    return copies


def build_tables(taps, conv, back):
    tap, spot = iota((TAPS, COLS), 0), iota((TAPS, COLS), 1)

    def spread_out(x, places):
        return dot(x, (places == spot).astype(bf16))

    def turned(row, rows, shift):
        wide = jnp.broadcast_to(row, (rows, COLS))
        return pltpu.roll(wide, shift, 1, stride=1, stride_axis=0)

    lane = iota((HALF_SPAN, COLS), 1)
    for side in range(2):
        high, low = halves(taps[side])
        ahead = spread_out(high, tap) + spread_out(high, tap + STEP) + spread_out(low, tap + 2 * STEP)
        behind = [spread_out(half, lax.rem(COLS - tap, COLS)) for half in (high, low)]
        for b in range(BANDS):
            conv[side, b * GROUP : (b + 1) * GROUP, :] = turned(ahead[b : b + 1], GROUP, 0).astype(bf16)
            for part in range(2):
                shift = (HALF_SPAN - BACK_START) * part
                near = turned(behind[0][b : b + 1], HALF_SPAN, shift)
                far = turned(behind[0][b : b + 1], HALF_SPAN, shift + HALF_SPAN)
                small = turned(behind[1][b : b + 1], HALF_SPAN, shift)
                both = jnp.where(lane < HALF_SPAN, near, jnp.where(lane < SPAN, far, 0.0))
                small = jnp.where(lane < HALF_SPAN, small, 0.0)
                cols = slice(b * COLS, (b + 1) * COLS)
                back[side, part, :HALF_SPAN, cols] = both.astype(bf16)
                back[side, part, HALF_SPAN:, cols] = small.astype(bf16)


def send_kernel(
    params,
    offsets,
    counts,
    psf_y,
    psf_x,
    background,
    image,
    out,
    conv,
    back,
    prior,
    sky,
    observed,
    theta,
    place,
    taps,
    pixels,
    mine,
    landed,
    load_sem,
    send_sem,
    recv_sem,
):
    tile, band = lax.axis_index("tile"), lax.axis_index("band")
    loads = start_copies(
        (
            (params, theta),
            (offsets, place),
            (psf_y, taps.at[0]),
            (psf_x, taps.at[1]),
            (background, sky),
            (quadrant_of(image, tile, band), pixels),
        ),
        load_sem,
    )
    barrier = pltpu.get_barrier_semaphore()
    greet(barrier, owners(tile, band))
    for load in loads[:2]:
        load.wait()
    raw, is_flux, is_shift, is_weight, is_spread, weight, soft, sigmoid, curve, scale, spread = derived(
        theta[...]
    )
    slot, lane = iota((SRC, LANES), 0), iota((SRC, LANES), 1)
    live = (slot < counts[0]).astype(f32)
    row = jnp.where(is_flux, flux_scale * soft * live, 0.0)
    row = jnp.where(is_shift, (PATCH / 16.0) * curve, row)
    row = jnp.where(is_weight, weight, row)
    row = jnp.where(is_spread, spread, row)
    start = place[...].astype(f32)
    diagonal = iota((SRC, SRC), 0) == iota((SRC, SRC), 1)
    for side in range(2):
        start_side = jnp.sum(jnp.where(diagonal, start[side : side + 1, :], 0.0), axis=1, keepdims=True)
        row = jnp.where(lane == TOP + side, start_side, row)
    row = jnp.where(lane == LIVE, live, row)
    slope = jnp.where(is_flux, sigmoid / soft, 0.0)
    slope = jnp.where(is_shift, (PATCH / 16.0) * (1.0 - curve * curve), slope)
    slope = jnp.where(is_weight, 1.0, slope)
    slope = jnp.where(is_spread, scale * sigmoid, slope)
    mine[...] = row + pltpu.roll(slope, HALVES, 1)

    pl.semaphore_wait(barrier, how_many(viewers(tile, band)))
    copies = []
    for i, (other_tile, other_band, block, _, there) in enumerate(viewers(tile, band)):
        copy = pltpu.make_async_remote_copy(
            src_ref=mine,
            dst_ref=landed.at[block],
            send_sem=send_sem.at[i],
            recv_sem=recv_sem.at[block],
            device_id=(other_tile, other_band),
            device_id_type=MESH,
        )
        copies.append((copy, there))
        pl.when(there)(copy.start)
    for _, _, block, _, there in owners(tile, band):

        @pl.when(jnp.logical_not(there))
        def _():
            landed[block] = jnp.zeros((SRC, LANES), f32)

    for load in loads[2:]:
        load.wait()
    build_tables(taps, conv, back)

    prior[...] = prior_weight * theta[...] * live[:, :PARAMS]
    turn = lax.rem(COLS - lax.rem(band, 2) * (QUAD - COLS // 2), COLS)
    for b in range(BANDS):
        observed[b] = pltpu.roll(pixels[b], turn, 1)[:, :QUAD]

    for i, (other_tile, other_band, block, _, there) in enumerate(reversed(owners(tile, band))):
        copy = pltpu.make_async_remote_copy(
            src_ref=mine,
            dst_ref=landed.at[block],
            send_sem=send_sem.at[i],
            recv_sem=recv_sem.at[block],
            device_id=(other_tile, other_band),
            device_id_type=MESH,
        )
        pl.when(there)(copy.wait_recv)
        out[block * SRC : (block + 1) * SRC, :] = landed[block]
    for copy, there in copies:
        pl.when(there)(copy.wait_send)


def quadrant_of(image, tile, band):
    half_y, half_x = band // 2, lax.rem(band, 2)
    rows = pl.ds(pl.multiple_of(half_y * QUAD, QUAD), QUAD)
    cols = pl.ds(pl.multiple_of(half_x * (COLS // 2), COLS // 2), COLS)
    return image.at[0, :, rows, cols]


def column_comps():
    column = iota((1, COLS), 1)
    place = (column * 5462) >> 16
    return place, iota((16, COLS), 0) == column - COMPONENTS * place


def one_of(values, base):
    mine = column_comps()[1]
    return jnp.sum(jnp.where(mine, values[base : base + 16], 0.0), axis=0, keepdims=True)


def geometry(values, side):
    spread = one_of(values, (SPREAD_Y, SPREAD_X)[side])
    inverse = 1.0 / jnp.where(spread > 0.0, spread, 1.0)
    shift = values[BANDS + side : BANDS + side + 1]
    start = values[TOP + side : TOP + side + 1]
    spot = iota((SPAN, COLS), 0).astype(f32) - (start + float(HALF))
    inside = (spot >= 0.0) & (spot < PATCH)
    ratio = (spot + (0.5 - PATCH / 2.0) - shift) * inverse
    spot = iota((QUAD, COLS), 0).astype(f32) - start
    window = ((spot >= 0.0) & (spot < PATCH)).astype(f32)
    return inverse, inside, ratio, window


def render(values, conv, profiles, factors, c):
    weight = one_of(values, WEIGHT)
    for side in range(2):
        _, inside, ratio, window = geometry(values, side)
        profile = jnp.where(inside, jnp.exp(-0.5 * ratio * ratio), 0.0)
        profiles[c, side] = profile
        high, low = halves(profile)
        for start in range(0, QUAD, GROUP):
            rows = slice(start, start + STEP)
            blank = jnp.zeros((COLS - 3 * STEP, COLS), bf16)
            stack = jnp.concatenate([high[rows], low[rows], high[rows], blank], axis=0)
            factor = dot(conv[side], stack)
            seen = window[start : start + GROUP]
            for b in range(BANDS):
                scale = seen * (weight * values[b : b + 1]) if side == 0 else seen
                high_low = halves(factor[b * GROUP : (b + 1) * GROUP] * scale)
                for half in range(2):
                    put = half * QUAD + start
                    factors[side][c, b, put : put + GROUP] = high_low[half]


def model_of(factors, c, b):
    y_factor, x_factor = factors
    x = (x_factor[c, b, :QUAD], x_factor[c, b, QUAD:])
    return dot3(y_factor[c, b], x, ((1,), (1,)))


def leave(observed, background, model, residual, b):
    left = observed[b] / (background[0:1, b : b + 1] + model) - 1.0
    left = left * (1.0 / (PATCH * PATCH))
    for way, r in enumerate((left, left.T)):
        high_low = halves(r)
        for half in range(2):
            residual[way, b, half * QUAD : (half + 1) * QUAD] = high_low[half]


def pull(values, onehot, back, profiles, factors, residual, stack, c):
    y_factor, x_factor = factors
    mine = column_comps()[1]
    weight = one_of(values, WEIGHT)
    rows = []
    inverse_y, _, ratio_y, window_y = geometry(values, 0)
    inverse_x, _, ratio_x, window_x = geometry(values, 1)
    blank = jnp.zeros((COLS - SPAN, COLS), bf16)
    for b in range(BANDS):
        y = (y_factor[c, b, :QUAD], y_factor[c, b, QUAD:])
        x = (x_factor[c, b, :QUAD], x_factor[c, b, QUAD:])
        along_y = dot3(residual[0, b], x)
        along_x = dot3(residual[1, b], y)
        factor = y[0].astype(f32) + y[1].astype(f32)
        rows.append(jnp.sum(along_y * factor, axis=0, keepdims=True))
        along_y = along_y * (window_y * (weight * values[b : b + 1]))
        along_x = along_x * window_x
        for side, along in enumerate((along_y, along_x)):
            high, low = halves(along)
            for part, start in enumerate((0, BACK_START)):
                here = slice(start, start + HALF_SPAN)
                put = b * COLS
                stack[side, part, put : put + HALF_SPAN] = high[here]
                stack[side, part, put + HALF_SPAN : put + SPAN] = low[here]
                stack[side, part, put + SPAN : put + COLS] = blank
    ds = []
    for side in range(2):
        d = []
        for part in range(2):
            both = dot(back[side, part], stack[side, part])
            d.append(both[:HALF_SPAN] + both[HALF_SPAN:])
        ds.append(jnp.concatenate(d, axis=0))
    by_comp = rows[0] + rows[1] + rows[2] + rows[3] + rows[4]
    spreads = []
    for side, (d, inverse, ratio) in enumerate(((ds[0], inverse_y, ratio_y), (ds[1], inverse_x, ratio_x))):
        first = d * profiles[c, side] * ratio
        rows.append(inverse * jnp.sum(first, axis=0, keepdims=True))
        spreads.append(inverse * jnp.sum(first * ratio, axis=0, keepdims=True))
    pieces = rows + [jnp.zeros((16 - len(rows), COLS), f32)]
    for by in (by_comp, spreads[0], spreads[1]):
        pieces.append(jnp.where(mine, by, 0.0))
    high_low = jnp.concatenate(halves(jnp.concatenate(pieces, axis=0)), axis=0)
    return dot(onehot, high_low, ((1,), (1,)))


def find(data, tile, band):
    row, col = tile // TILE_COLS, lax.rem(tile, TILE_COLS)
    half_y, half_x = band // 2, lax.rem(band, 2)
    slot = iota((SLOTS, LANES), 0)
    lane = iota((SLOTS, LANES), 1)
    far_y, far_x = slot // (SLOTS // 2), lax.rem(slot // (SLOTS // 4), 2)

    def moved(far, half, place):
        origin = jnp.where(far == 0, 0, TILE_SIDE * (2 * half - 1)) - QUAD * half
        beyond = place + 2 * half - 1
        there = (far == 0) | ((beyond >= 0) & (beyond < TILE_COLS))
        return origin.astype(f32), there

    origin_y, there_y = moved(far_y, half_y, row)
    origin_x, there_x = moved(far_x, half_x, col)
    data = data + jnp.where(lane == TOP, origin_y, jnp.where(lane == LEFT, origin_x, 0.0))
    is_place = (lane == TOP) | (lane == LEFT)
    reach = is_place & (data > -PATCH) & (data < QUAD) | (lane == LIVE) & (data > 0.0)
    met = jnp.where(reach & there_y & there_x, 1.0, 0.0).astype(bf16)
    active = jnp.where(dot(met, jnp.ones((LANES, LANES), bf16)) > 2.5, 1.0, 0.0)
    count = jnp.sum(active, axis=0, keepdims=True)

    def chunk_makers():
        before = jnp.where(lane < slot, 1.0, 0.0).astype(bf16)
        order = dot(before, active.astype(bf16))
        order = jnp.where(active > 0.0, order, -1.0)[:, 0:1].astype(jnp.int32)
        place = column_comps()[0]

        def picked(c):
            here = (place < PER_CHUNK) & (order - c * PER_CHUNK == place)
            return jnp.where(here, 1.0, 0.0).astype(bf16)

        thirds = thirds_of(data.T[:HALVES])

        def gathered(c):
            return summed(dot(thirds, picked(c)))

        return picked, gathered

    return count, chunk_makers


def more_kernel(
    slots,
    sky,
    observed,
    conv,
    back,
    rest_model,
    rest_parts,
    profiles,
    y_factor,
    x_factor,
    residual,
    stack,
):
    tile, band = lax.axis_index("tile"), lax.axis_index("band")
    counts, chunk_makers = find(slots[...], tile, band)
    count = counts[0, 0].astype(jnp.int32)

    @pl.when(count > PER_CHUNK)
    def _():
        picked, gathered = chunk_makers()
        factors = (y_factor, x_factor)
        chunks = (count + PER_CHUNK - 1) // PER_CHUNK
        rest_model[...] = jnp.zeros_like(rest_model)
        rest_parts[...] = jnp.zeros_like(rest_parts)

        def add(c, carry):
            render(gathered(c), conv, profiles, factors, c)
            for b in range(BANDS):
                rest_model[b] += model_of(factors, c, b)
            return carry

        lax.fori_loop(1, chunks, add, 0)
        render(gathered(0), conv, profiles, factors, 0)
        for b in range(BANDS):
            model = rest_model[b] + model_of(factors, 0, b)
            leave(observed, sky, model, residual, b)

        def take(c, carry):
            rest_parts[...] += pull(gathered(c), picked(c), back, profiles, factors, residual, stack, c)
            return carry

        lax.fori_loop(1, chunks, take, 0)


def to_parameters(pulled, data):
    lane = iota((SLOTS, LANES), 1)
    is_weight = (lane >= WEIGHT) & (lane < WEIGHT + COMPONENTS)
    is_spread = ((lane >= SPREAD_Y) & (lane < SPREAD_Y + COMPONENTS)) | (
        (lane >= SPREAD_X) & (lane < SPREAD_X + COMPONENTS)
    )
    weight = jnp.where(is_weight, data, 0.0)
    groups = jnp.concatenate(
        [jnp.where(is_weight, pulled, 0.0), jnp.where(is_spread, pulled * data, 0.0)], axis=0
    )
    sums = summed(dot(thirds_of(groups), jnp.ones((LANES, LANES), bf16)))
    slope = jnp.where(lane < HALVES, pltpu.roll(data, HALVES, 1), 0.0)
    by_lane = pulled * slope - weight * sums[:SLOTS]
    by_lane = jnp.where(lane == BANDS + 2, 0.25 * sums[SLOTS:], by_lane)
    return summed(dot(thirds_of(by_lane), parameter_columns()))


def return_kernel(
    slots,
    rest_model,
    rest_parts,
    sky,
    observed,
    conv,
    back,
    prior,
    out,
    profiles,
    y_factor,
    x_factor,
    residual,
    stack,
    parts,
    landed,
    send_sem,
    recv_sem,
):
    tile, band = lax.axis_index("tile"), lax.axis_index("band")
    barrier = pltpu.get_barrier_semaphore()
    greet(barrier, viewers(tile, band))
    factors = (y_factor, x_factor)
    count, chunk_makers = find(slots[...], tile, band)
    picked, gathered = chunk_makers()
    onehot, values = picked(0), gathered(0)
    more = count[:, 0:1] > PER_CHUNK
    render(values, conv, profiles, factors, 0)
    for b in range(BANDS):
        model = model_of(factors, 0, b) + jnp.where(more, rest_model[b], 0.0)
        leave(observed, sky, model, residual, b)
    pulled = pull(values, onehot, back, profiles, factors, residual, stack, 0)
    pulled = pulled + jnp.where(more, rest_parts[...], 0.0)
    parts[...] = to_parameters(pulled + pltpu.roll(pulled, HALVES, 1), slots[...])

    pl.semaphore_wait(barrier, how_many(owners(tile, band)))
    copies = []
    for i, (other_tile, other_band, block, answer, there) in enumerate(owners(tile, band)):
        copy = pltpu.make_async_remote_copy(
            src_ref=parts.at[block * SRC : (block + 1) * SRC, :],
            dst_ref=landed.at[answer],
            send_sem=send_sem.at[i],
            recv_sem=recv_sem.at[answer],
            device_id=(other_tile, other_band),
            device_id_type=MESH,
        )
        copies.append((copy, there))
        pl.when(there)(copy.start)
    for _, _, _, answer, there in viewers(tile, band):

        @pl.when(jnp.logical_not(there))
        def _():
            landed[answer] = jnp.zeros((SRC, LANES), f32)

    total = jnp.zeros((SRC, LANES), f32)
    for i, (other_tile, other_band, _, answer, there) in enumerate(reversed(viewers(tile, band))):
        copy = pltpu.make_async_remote_copy(
            src_ref=parts.at[0:SRC, :],
            dst_ref=landed.at[answer],
            send_sem=send_sem.at[i],
            recv_sem=recv_sem.at[answer],
            device_id=(other_tile, other_band),
            device_id_type=MESH,
        )
        pl.when(there)(copy.wait_recv)
        total = total + landed[answer]
    out[...] = total[:, :PARAMS] - prior[...]
    for copy, there in copies:
        pl.when(there)(copy.wait_send)


def vmem(count):
    return [pl.BlockSpec(memory_space=pltpu.VMEM)] * count


def hbm(count):
    return [pl.BlockSpec(memory_space=pltpu.HBM)] * count


def work_space(chunks):
    return [
        pltpu.VMEM((chunks, 2, SPAN, COLS), f32),
        pltpu.VMEM((chunks, BANDS, 2 * QUAD, COLS), bf16),
        pltpu.VMEM((chunks, BANDS, 2 * QUAD, COLS), bf16),
        pltpu.VMEM((2, BANDS, 2 * QUAD, QUAD), bf16),
        pltpu.VMEM((2, 2, BANDS * COLS, COLS), bf16),
    ]


def shape(*dims, kind=f32):
    return jax.ShapeDtypeStruct(dims, kind)


def body(params, offsets, counts, image, background, psf_y, psf_x):
    smem = pl.BlockSpec(memory_space=pltpu.SMEM)
    params, offsets, image, background, psf_y, psf_x = (
        pltpu.with_memory_space_constraint(x, pltpu.HBM)
        for x in (params, offsets.T, image, background, psf_y, psf_x)
    )
    partners = [pltpu.SemaphoreType.DMA((PARTNERS,))] * 2
    slots, conv, back, prior, sky, observed = pl.pallas_call(
        send_kernel,
        out_shape=[shape(SLOTS, LANES)]
        + [shape(2, BANDS * GROUP, COLS, kind=bf16), shape(2, 2, SPAN, BANDS * COLS, kind=bf16)]
        + [shape(SRC, PARAMS), shape(1, BANDS), shape(BANDS, QUAD, QUAD)],
        in_specs=hbm(2) + [smem] + hbm(4),
        out_specs=vmem(6),
        scratch_shapes=[
            pltpu.VMEM((SRC, PARAMS), f32),
            pltpu.VMEM((2, SRC), jnp.int32),
            pltpu.VMEM((2, BANDS, TAPS), f32),
            pltpu.VMEM((BANDS, QUAD, COLS), f32),
            pltpu.VMEM((SRC, LANES), f32),
            pltpu.VMEM((PARTNERS, SRC, LANES), f32),
            pltpu.SemaphoreType.DMA((6,)),
        ]
        + partners,
        compiler_params=pltpu.CompilerParams(
            collective_id=0, has_side_effects=True, vmem_limit_bytes=16 * 1024 * 1024
        ),
        name="send_slots",
    )(params, offsets, counts, psf_y, psf_x, background, image)
    rest_model, rest_parts = pl.pallas_call(
        more_kernel,
        out_shape=[shape(BANDS, QUAD, QUAD), shape(SLOTS, LANES)],
        in_specs=vmem(5),
        out_specs=vmem(2),
        scratch_shapes=work_space(CHUNKS),
        compiler_params=pltpu.CompilerParams(vmem_limit_bytes=40 * 1024 * 1024),
        name="more_sources",
    )(slots, sky, observed, conv, back)
    return pl.pallas_call(
        return_kernel,
        out_shape=shape(SRC, PARAMS),
        in_specs=vmem(8),
        out_specs=vmem(1)[0],
        scratch_shapes=work_space(1)
        + [
            pltpu.VMEM((SLOTS, LANES), f32),
            pltpu.VMEM((PARTNERS, SRC, LANES), f32),
        ]
        + partners,
        compiler_params=pltpu.CompilerParams(
            collective_id=1, has_side_effects=True, vmem_limit_bytes=24 * 1024 * 1024
        ),
        name="return_parts",
    )(
        slots, rest_model, rest_parts, sky, observed, conv, back, prior
    )


def solution(mesh):
    placed = (
        P(("tile", "band"), None),
        P(("tile", "band"), None),
        P(("tile", "band")),
        P("tile", None, None, None),
        P("tile", None),
        P(),
        P(),
    )
    return jax.shard_map(
        body, mesh=mesh, in_specs=placed, out_specs=P(("tile", "band"), None), check_vma=False
    )
```

```python
import functools

import jax
import jax.numpy as jnp
from jax import lax
from jax.experimental import pallas as pl
from jax.experimental.pallas import tpu as pltpu
from jax.sharding import PartitionSpec as P

BANDS = 5
COMPONENTS = 12
PARAMS = 44
PATCH = 64
TAPS = 25
HALF = TAPS // 2
TILE_COLS = 8
TILE_SIDE = 384
QUAD = TILE_SIDE // 2
SRC = 8
TILES = 64
N_BAND = 4
PARTNERS = 16
SLOTS = PARTNERS * SRC
LANES = 128

TOP, LEFT, LIVE = 8, 9, 10
WEIGHT, SPREAD_Y, SPREAD_X = 16, 32, 48
HALVES = 64

PER_CHUNK = 21
COLS = 256
CHUNKS = -(-SLOTS // PER_CHUNK)
SPAN = 224
GROUP = 48
STEP = 80
HALF_SPAN = SPAN // 2
BACK_START = QUAD - HALF_SPAN

flux_scale = 2.0
prior_weight = 0.1
highest = lax.Precision.HIGHEST
f32 = jnp.float32
bf16 = jnp.bfloat16
MESH = pl.DeviceIdType.MESH


def iota(shape, axis):
    return lax.broadcasted_iota(jnp.int32, shape, axis)


def dot(a, b, dims=((1,), (0,)), precision=None):
    return lax.dot_general(a, b, (dims, ((), ())), precision=precision, preferred_element_type=f32)


def halves(x):
    high = x.astype(bf16)
    return high, (x - high.astype(f32)).astype(bf16)


def dot3(a, b, dims=((1,), (0,))):
    rows = a.shape[0] // 2
    both = dot(a, b[0], dims)
    return both[:rows] + (both[rows:] + dot(a[:rows], b[1], dims))


def wrapped_tile(row, col):
    return lax.rem(row + TILE_COLS, TILE_COLS) * TILE_COLS + lax.rem(col + TILE_COLS, TILE_COLS)


def inside(row, col):
    return (row >= 0) & (row < TILE_COLS) & (col >= 0) & (col < TILE_COLS)


def viewers(tile, band):
    home = lax.rem(tile + TILES // 2, TILES)
    row, col = home // TILE_COLS, lax.rem(home, TILE_COLS)
    found = []
    for step_y, half_y in ((1, 0), (-1, 1), (0, 0), (0, 1)):
        for step_x, half_x in ((1, 0), (-1, 1), (0, 0), (0, 1)):
            far = 2 * abs(step_y) + abs(step_x)
            answer = (2 * abs(step_y) + half_y) * 4 + 2 * abs(step_x) + half_x
            to_row, to_col = row + step_y, col + step_x
            found.append(
                (
                    wrapped_tile(to_row, to_col),
                    2 * half_y + half_x,
                    far * N_BAND + band,
                    answer,
                    inside(to_row, to_col),
                )
            )
    return found


def owners(tile, band):
    row, col = tile // TILE_COLS, lax.rem(tile, TILE_COLS)
    half_y, half_x = band // 2, lax.rem(band, 2)
    found = []
    for far_y in (1, 0):
        for far_x in (1, 0):
            from_row, from_col = row + far_y * (2 * half_y - 1), col + far_x * (2 * half_x - 1)
            holder = lax.rem(wrapped_tile(from_row, from_col) + TILES // 2, TILES)
            answer = (2 * far_y + half_y) * 4 + 2 * far_x + half_x
            for other in range(N_BAND):
                block = (2 * far_y + far_x) * N_BAND + other
                found.append((holder, other, block, answer, inside(from_row, from_col)))
    return found


def greet(barrier, callers):
    for other_tile, other_band, _, _, there in callers:

        @pl.when(there)
        def _():
            pl.semaphore_signal(
                barrier, inc=1, device_id=(other_tile, other_band), device_id_type=MESH
            )


def how_many(partners):
    return sum(there.astype(jnp.int32) for _, _, _, _, there in partners)


def parameter_lanes():
    lane = iota((1, LANES), 1)
    source = jnp.where(lane < BANDS + 2, lane, -1)
    source = jnp.where(lane == BANDS + 2, PARAMS - 1, source)
    for j, base in enumerate((WEIGHT, SPREAD_Y, SPREAD_X)):
        here = (lane >= base) & (lane < base + COMPONENTS)
        source = jnp.where(here, BANDS + 2 + 3 * (lane - base) + j, source)
    return (iota((PARAMS, LANES), 0) == source).astype(bf16)


def parameter_columns():
    lane = iota((LANES, LANES), 0)
    target = jnp.where(lane < BANDS + 2, lane, -1)
    target = jnp.where(lane == BANDS + 2, PARAMS - 1, target)
    for j, base in enumerate((WEIGHT, SPREAD_Y, SPREAD_X)):
        here = (lane >= base) & (lane < base + COMPONENTS)
        target = jnp.where(here, BANDS + 2 + 3 * (lane - base) + j, target)
    return (iota((LANES, LANES), 1) == target).astype(bf16)


def thirds_of(x):
    high = x.astype(bf16).astype(f32)
    low = (x - high).astype(bf16).astype(f32)
    return jnp.concatenate([high, low, x - high - low], axis=0).astype(bf16)


def summed(x):
    rows = x.shape[0] // 3
    return x[:rows] + (x[rows : 2 * rows] + x[2 * rows :])


def derived(params):
    raw = summed(dot(thirds_of(params), parameter_lanes()))
    lane = iota(raw.shape, 1)
    is_flux = lane < BANDS
    is_shift = (lane >= BANDS) & (lane < BANDS + 2)
    is_weight = (lane >= WEIGHT) & (lane < WEIGHT + COMPONENTS)
    is_spread = ((lane >= SPREAD_Y) & (lane < SPREAD_Y + COMPONENTS)) | (
        (lane >= SPREAD_X) & (lane < SPREAD_X + COMPONENTS)
    )
    most = jnp.max(jnp.where(is_weight, raw, -jnp.inf), axis=1, keepdims=True)
    power = jnp.where(is_weight, jnp.exp(jnp.where(is_weight, raw - most, 0.0)), 0.0)
    weight = power / jnp.sum(power, axis=1, keepdims=True)
    decay = jnp.exp(-jnp.abs(raw))
    soft = jnp.maximum(raw, 0.0) + jnp.log1p(decay)
    sigmoid = jnp.where(raw >= 0.0, 1.0, decay) / (1.0 + decay)
    curve = jnp.tanh(raw)
    softness = jnp.exp(0.25 * raw[:, BANDS + 2 : BANDS + 3])
    scale = (PATCH / 32.0) * softness
    spread = (0.5 + soft) * scale
    return raw, is_flux, is_shift, is_weight, is_spread, weight, soft, sigmoid, curve, scale, spread


def start_copies(pairs, sems):
    copies = [pltpu.make_async_copy(src, dst, sems.at[i]) for i, (src, dst) in enumerate(pairs)]
    for copy in copies:
        copy.start()
    return copies


def build_tables(taps, conv, back):
    tap, spot = iota((TAPS, COLS), 0), iota((TAPS, COLS), 1)

    def spread_out(x, places):
        return dot(x, (places == spot).astype(bf16))

    def turned(row, rows, shift):
        wide = jnp.broadcast_to(row, (rows, COLS))
        return pltpu.roll(wide, shift, 1, stride=1, stride_axis=0)

    lane = iota((HALF_SPAN, COLS), 1)
    for side in range(2):
        high, low = halves(taps[side])
        ahead = spread_out(high, tap) + spread_out(high, tap + STEP) + spread_out(low, tap + 2 * STEP)
        behind = [spread_out(half, lax.rem(COLS - tap, COLS)) for half in (high, low)]
        for b in range(BANDS):
            conv[side, b * GROUP : (b + 1) * GROUP, :] = turned(ahead[b : b + 1], GROUP, 0).astype(bf16)
            for part in range(2):
                shift = (HALF_SPAN - BACK_START) * part
                near = turned(behind[0][b : b + 1], HALF_SPAN, shift)
                far = turned(behind[0][b : b + 1], HALF_SPAN, shift + HALF_SPAN)
                small = turned(behind[1][b : b + 1], HALF_SPAN, shift)
                both = jnp.where(lane < HALF_SPAN, near, jnp.where(lane < SPAN, far, 0.0))
                small = jnp.where(lane < HALF_SPAN, small, 0.0)
                cols = slice(b * COLS, (b + 1) * COLS)
                back[side, part, :HALF_SPAN, cols] = both.astype(bf16)
                back[side, part, HALF_SPAN:, cols] = small.astype(bf16)


def send_kernel(
    params,
    offsets,
    counts,
    psf_y,
    psf_x,
    background,
    image,
    out,
    conv,
    back,
    prior,
    sky,
    observed,
    theta,
    place,
    taps,
    pixels,
    mine,
    landed,
    load_sem,
    send_sem,
    recv_sem,
):
    tile, band = lax.axis_index("tile"), lax.axis_index("band")
    barrier = pltpu.get_barrier_semaphore()
    greet(barrier, owners(tile, band))
    loads = start_copies(
        (
            (params, theta),
            (offsets, place),
            (psf_y, taps.at[0]),
            (psf_x, taps.at[1]),
            (background, sky),
            (quadrant_of(image, tile, band), pixels),
        ),
        load_sem,
    )
    for load in loads[:2]:
        load.wait()
    raw, is_flux, is_shift, is_weight, is_spread, weight, soft, sigmoid, curve, scale, spread = derived(
        theta[...]
    )
    slot, lane = iota((SRC, LANES), 0), iota((SRC, LANES), 1)
    live = (slot < counts[0]).astype(f32)
    row = jnp.where(is_flux, flux_scale * soft * live, 0.0)
    row = jnp.where(is_shift, (PATCH / 16.0) * curve, row)
    row = jnp.where(is_weight, weight, row)
    row = jnp.where(is_spread, spread, row)
    start = place[...].astype(f32)
    diagonal = iota((SRC, SRC), 0) == iota((SRC, SRC), 1)
    for side in range(2):
        start_side = jnp.sum(jnp.where(diagonal, start[side : side + 1, :], 0.0), axis=1, keepdims=True)
        row = jnp.where(lane == TOP + side, start_side, row)
    row = jnp.where(lane == LIVE, live, row)
    slope = jnp.where(is_flux, sigmoid / soft, 0.0)
    slope = jnp.where(is_shift, (PATCH / 16.0) * (1.0 - curve * curve), slope)
    slope = jnp.where(is_weight, 1.0, slope)
    slope = jnp.where(is_spread, scale * sigmoid, slope)
    mine[...] = row + pltpu.roll(slope, HALVES, 1)

    pl.semaphore_wait(barrier, how_many(viewers(tile, band)))
    copies = []
    for i, (other_tile, other_band, block, _, there) in enumerate(viewers(tile, band)):
        copy = pltpu.make_async_remote_copy(
            src_ref=mine,
            dst_ref=landed.at[block],
            send_sem=send_sem.at[i],
            recv_sem=recv_sem.at[block],
            device_id=(other_tile, other_band),
            device_id_type=MESH,
        )
        copies.append((copy, there))
        pl.when(there)(copy.start)
    for _, _, block, _, there in owners(tile, band):

        @pl.when(jnp.logical_not(there))
        def _():
            landed[block] = jnp.zeros((SRC, LANES), f32)

    for load in loads[2:]:
        load.wait()
    build_tables(taps, conv, back)

    prior[...] = prior_weight * theta[...] * live[:, :PARAMS]
    turn = lax.rem(COLS - lax.rem(band, 2) * (QUAD - COLS // 2), COLS)
    for b in range(BANDS):
        observed[b] = pltpu.roll(pixels[b], turn, 1)[:, :QUAD]

    for i, (other_tile, other_band, block, _, there) in enumerate(reversed(owners(tile, band))):
        copy = pltpu.make_async_remote_copy(
            src_ref=mine,
            dst_ref=landed.at[block],
            send_sem=send_sem.at[i],
            recv_sem=recv_sem.at[block],
            device_id=(other_tile, other_band),
            device_id_type=MESH,
        )
        pl.when(there)(copy.wait_recv)
        out[block * SRC : (block + 1) * SRC, :] = landed[block]
    for copy, there in copies:
        pl.when(there)(copy.wait_send)


def quadrant_of(image, tile, band):
    half_y, half_x = band // 2, lax.rem(band, 2)
    rows = pl.ds(pl.multiple_of(half_y * QUAD, QUAD), QUAD)
    cols = pl.ds(pl.multiple_of(half_x * (COLS // 2), COLS // 2), COLS)
    return image.at[0, :, rows, cols]


def column_comps():
    column = iota((1, COLS), 1)
    place = (column * 5462) >> 16
    return place, iota((16, COLS), 0) == column - COMPONENTS * place


def one_of(values, base):
    mine = column_comps()[1]
    return jnp.sum(jnp.where(mine, values[base : base + 16], 0.0), axis=0, keepdims=True)


def geometry(values, side):
    spread = one_of(values, (SPREAD_Y, SPREAD_X)[side])
    inverse = 1.0 / jnp.where(spread > 0.0, spread, 1.0)
    shift = values[BANDS + side : BANDS + side + 1]
    start = values[TOP + side : TOP + side + 1]
    spot = iota((SPAN, COLS), 0).astype(f32) - (start + float(HALF))
    inside = (spot >= 0.0) & (spot < PATCH)
    ratio = (spot + (0.5 - PATCH / 2.0) - shift) * inverse
    spot = iota((QUAD, COLS), 0).astype(f32) - start
    window = ((spot >= 0.0) & (spot < PATCH)).astype(f32)
    return inverse, inside, ratio, window


def render(values, conv, profiles, factors, c):
    weight = one_of(values, WEIGHT)
    for side in range(2):
        _, inside, ratio, window = geometry(values, side)
        profile = jnp.where(inside, jnp.exp(-0.5 * ratio * ratio), 0.0)
        profiles[c, side] = profile
        high, low = halves(profile)
        for start in range(0, QUAD, GROUP):
            rows = slice(start, start + STEP)
            blank = jnp.zeros((COLS - 3 * STEP, COLS), bf16)
            stack = jnp.concatenate([high[rows], low[rows], high[rows], blank], axis=0)
            factor = dot(conv[side], stack)
            seen = window[start : start + GROUP]
            for b in range(BANDS):
                scale = seen * (weight * values[b : b + 1]) if side == 0 else seen
                high_low = halves(factor[b * GROUP : (b + 1) * GROUP] * scale)
                for half in range(2):
                    put = half * QUAD + start
                    factors[side][c, b, put : put + GROUP] = high_low[half]


def model_of(factors, c, b):
    y_factor, x_factor = factors
    x = (x_factor[c, b, :QUAD], x_factor[c, b, QUAD:])
    return dot3(y_factor[c, b], x, ((1,), (1,)))


def leave(observed, background, model, residual, b):
    left = observed[b] / (background[0:1, b : b + 1] + model) - 1.0
    left = left * (1.0 / (PATCH * PATCH))
    for way, r in enumerate((left, left.T)):
        high_low = halves(r)
        for half in range(2):
            residual[way, b, half * QUAD : (half + 1) * QUAD] = high_low[half]


def pull(values, onehot, back, profiles, factors, residual, stack, c):
    y_factor, x_factor = factors
    mine = column_comps()[1]
    weight = one_of(values, WEIGHT)
    rows = []
    inverse_y, _, ratio_y, window_y = geometry(values, 0)
    inverse_x, _, ratio_x, window_x = geometry(values, 1)
    blank = jnp.zeros((COLS - SPAN, COLS), bf16)
    for b in range(BANDS):
        y = (y_factor[c, b, :QUAD], y_factor[c, b, QUAD:])
        x = (x_factor[c, b, :QUAD], x_factor[c, b, QUAD:])
        along_y = dot3(residual[0, b], x)
        along_x = dot3(residual[1, b], y)
        factor = y[0].astype(f32) + y[1].astype(f32)
        rows.append(jnp.sum(along_y * factor, axis=0, keepdims=True))
        along_y = along_y * (window_y * (weight * values[b : b + 1]))
        along_x = along_x * window_x
        for side, along in enumerate((along_y, along_x)):
            high, low = halves(along)
            for part, start in enumerate((0, BACK_START)):
                here = slice(start, start + HALF_SPAN)
                put = b * COLS
                stack[side, part, put : put + HALF_SPAN] = high[here]
                stack[side, part, put + HALF_SPAN : put + SPAN] = low[here]
                stack[side, part, put + SPAN : put + COLS] = blank
    ds = []
    for side in range(2):
        d = []
        for part in range(2):
            both = dot(back[side, part], stack[side, part])
            d.append(both[:HALF_SPAN] + both[HALF_SPAN:])
        ds.append(jnp.concatenate(d, axis=0))
    by_comp = rows[0] + rows[1] + rows[2] + rows[3] + rows[4]
    spreads = []
    for side, (d, inverse, ratio) in enumerate(((ds[0], inverse_y, ratio_y), (ds[1], inverse_x, ratio_x))):
        first = d * profiles[c, side] * ratio
        rows.append(inverse * jnp.sum(first, axis=0, keepdims=True))
        spreads.append(inverse * jnp.sum(first * ratio, axis=0, keepdims=True))
    pieces = rows + [jnp.zeros((16 - len(rows), COLS), f32)]
    for by in (by_comp, spreads[0], spreads[1]):
        pieces.append(jnp.where(mine, by, 0.0))
    high_low = jnp.concatenate(halves(jnp.concatenate(pieces, axis=0)), axis=0)
    return dot(onehot, high_low, ((1,), (1,)))


def find(data, tile, band):
    row, col = tile // TILE_COLS, lax.rem(tile, TILE_COLS)
    half_y, half_x = band // 2, lax.rem(band, 2)
    slot = iota((SLOTS, LANES), 0)
    lane = iota((SLOTS, LANES), 1)
    far_y, far_x = slot // (SLOTS // 2), lax.rem(slot // (SLOTS // 4), 2)

    def moved(far, half, place):
        origin = jnp.where(far == 0, 0, TILE_SIDE * (2 * half - 1)) - QUAD * half
        beyond = place + 2 * half - 1
        there = (far == 0) | ((beyond >= 0) & (beyond < TILE_COLS))
        return origin.astype(f32), there

    origin_y, there_y = moved(far_y, half_y, row)
    origin_x, there_x = moved(far_x, half_x, col)
    data = data + jnp.where(lane == TOP, origin_y, jnp.where(lane == LEFT, origin_x, 0.0))
    is_place = (lane == TOP) | (lane == LEFT)
    reach = is_place & (data > -PATCH) & (data < QUAD) | (lane == LIVE) & (data > 0.0)
    met = jnp.where(reach & there_y & there_x, 1.0, 0.0).astype(bf16)
    active = jnp.where(dot(met, jnp.ones((LANES, LANES), bf16)) > 2.5, 1.0, 0.0)
    count = jnp.sum(active, axis=0, keepdims=True)

    def chunk_makers():
        before = jnp.where(lane < slot, 1.0, 0.0).astype(bf16)
        order = dot(before, active.astype(bf16))
        order = jnp.where(active > 0.0, order, -1.0)[:, 0:1].astype(jnp.int32)
        place = column_comps()[0]

        def picked(c):
            here = (place < PER_CHUNK) & (order - c * PER_CHUNK == place)
            return jnp.where(here, 1.0, 0.0).astype(bf16)

        thirds = thirds_of(data.T[:HALVES])

        def gathered(c):
            return summed(dot(thirds, picked(c)))

        return picked, gathered

    return count, chunk_makers


def more_kernel(
    slots,
    sky,
    observed,
    conv,
    back,
    rest_model,
    rest_parts,
    profiles,
    y_factor,
    x_factor,
    residual,
    stack,
):
    tile, band = lax.axis_index("tile"), lax.axis_index("band")
    counts, chunk_makers = find(slots[...], tile, band)
    count = counts[0, 0].astype(jnp.int32)

    @pl.when(count > PER_CHUNK)
    def _():
        picked, gathered = chunk_makers()
        factors = (y_factor, x_factor)
        chunks = (count + PER_CHUNK - 1) // PER_CHUNK
        rest_model[...] = jnp.zeros_like(rest_model)
        rest_parts[...] = jnp.zeros_like(rest_parts)

        def add(c, carry):
            render(gathered(c), conv, profiles, factors, c)
            for b in range(BANDS):
                rest_model[b] += model_of(factors, c, b)
            return carry

        lax.fori_loop(1, chunks, add, 0)
        render(gathered(0), conv, profiles, factors, 0)
        for b in range(BANDS):
            model = rest_model[b] + model_of(factors, 0, b)
            leave(observed, sky, model, residual, b)

        def take(c, carry):
            rest_parts[...] += pull(gathered(c), picked(c), back, profiles, factors, residual, stack, c)
            return carry

        lax.fori_loop(1, chunks, take, 0)


def to_parameters(pulled, data):
    lane = iota((SLOTS, LANES), 1)
    is_weight = (lane >= WEIGHT) & (lane < WEIGHT + COMPONENTS)
    is_spread = ((lane >= SPREAD_Y) & (lane < SPREAD_Y + COMPONENTS)) | (
        (lane >= SPREAD_X) & (lane < SPREAD_X + COMPONENTS)
    )
    weight = jnp.where(is_weight, data, 0.0)
    groups = jnp.concatenate(
        [jnp.where(is_weight, pulled, 0.0), jnp.where(is_spread, pulled * data, 0.0)], axis=0
    )
    sums = summed(dot(thirds_of(groups), jnp.ones((LANES, LANES), bf16)))
    slope = jnp.where(lane < HALVES, pltpu.roll(data, HALVES, 1), 0.0)
    by_lane = pulled * slope - weight * sums[:SLOTS]
    by_lane = jnp.where(lane == BANDS + 2, 0.25 * sums[SLOTS:], by_lane)
    return summed(dot(thirds_of(by_lane), parameter_columns()))


def return_kernel(
    slots,
    rest_model,
    rest_parts,
    sky,
    observed,
    conv,
    back,
    prior,
    out,
    profiles,
    y_factor,
    x_factor,
    residual,
    stack,
    parts,
    landed,
    send_sem,
    recv_sem,
):
    tile, band = lax.axis_index("tile"), lax.axis_index("band")
    barrier = pltpu.get_barrier_semaphore()
    greet(barrier, viewers(tile, band))
    factors = (y_factor, x_factor)
    count, chunk_makers = find(slots[...], tile, band)
    picked, gathered = chunk_makers()
    onehot, values = picked(0), gathered(0)
    more = count[:, 0:1] > PER_CHUNK
    render(values, conv, profiles, factors, 0)
    for b in range(BANDS):
        model = model_of(factors, 0, b) + jnp.where(more, rest_model[b], 0.0)
        leave(observed, sky, model, residual, b)
    pulled = pull(values, onehot, back, profiles, factors, residual, stack, 0)
    pulled = pulled + jnp.where(more, rest_parts[...], 0.0)
    parts[...] = to_parameters(pulled + pltpu.roll(pulled, HALVES, 1), slots[...])

    pl.semaphore_wait(barrier, how_many(owners(tile, band)))
    copies = []
    for i, (other_tile, other_band, block, answer, there) in enumerate(owners(tile, band)):
        copy = pltpu.make_async_remote_copy(
            src_ref=parts.at[block * SRC : (block + 1) * SRC, :],
            dst_ref=landed.at[answer],
            send_sem=send_sem.at[i],
            recv_sem=recv_sem.at[answer],
            device_id=(other_tile, other_band),
            device_id_type=MESH,
        )
        copies.append((copy, there))
        pl.when(there)(copy.start)
    for _, _, _, answer, there in viewers(tile, band):

        @pl.when(jnp.logical_not(there))
        def _():
            landed[answer] = jnp.zeros((SRC, LANES), f32)

    total = jnp.zeros((SRC, LANES), f32)
    for i, (other_tile, other_band, _, answer, there) in enumerate(reversed(viewers(tile, band))):
        copy = pltpu.make_async_remote_copy(
            src_ref=parts.at[0:SRC, :],
            dst_ref=landed.at[answer],
            send_sem=send_sem.at[i],
            recv_sem=recv_sem.at[answer],
            device_id=(other_tile, other_band),
            device_id_type=MESH,
        )
        pl.when(there)(copy.wait_recv)
        total = total + landed[answer]
    out[...] = total[:, :PARAMS] - prior[...]
    for copy, there in copies:
        pl.when(there)(copy.wait_send)


def vmem(count):
    return [pl.BlockSpec(memory_space=pltpu.VMEM)] * count


def hbm(count):
    return [pl.BlockSpec(memory_space=pltpu.HBM)] * count


def work_space(chunks):
    return [
        pltpu.VMEM((chunks, 2, SPAN, COLS), f32),
        pltpu.VMEM((chunks, BANDS, 2 * QUAD, COLS), bf16),
        pltpu.VMEM((chunks, BANDS, 2 * QUAD, COLS), bf16),
        pltpu.VMEM((2, BANDS, 2 * QUAD, QUAD), bf16),
        pltpu.VMEM((2, 2, BANDS * COLS, COLS), bf16),
    ]


def shape(*dims, kind=f32):
    return jax.ShapeDtypeStruct(dims, kind)


def body(params, offsets, counts, image, background, psf_y, psf_x):
    smem = pl.BlockSpec(memory_space=pltpu.SMEM)
    params, offsets, image, background, psf_y, psf_x = (
        pltpu.with_memory_space_constraint(x, pltpu.HBM)
        for x in (params, offsets.T, image, background, psf_y, psf_x)
    )
    partners = [pltpu.SemaphoreType.DMA((PARTNERS,))] * 2
    slots, conv, back, prior, sky, observed = pl.pallas_call(
        send_kernel,
        out_shape=[shape(SLOTS, LANES)]
        + [shape(2, BANDS * GROUP, COLS, kind=bf16), shape(2, 2, SPAN, BANDS * COLS, kind=bf16)]
        + [shape(SRC, PARAMS), shape(1, BANDS), shape(BANDS, QUAD, QUAD)],
        in_specs=hbm(2) + [smem] + hbm(4),
        out_specs=vmem(6),
        scratch_shapes=[
            pltpu.VMEM((SRC, PARAMS), f32),
            pltpu.VMEM((2, SRC), jnp.int32),
            pltpu.VMEM((2, BANDS, TAPS), f32),
            pltpu.VMEM((BANDS, QUAD, COLS), f32),
            pltpu.VMEM((SRC, LANES), f32),
            pltpu.VMEM((PARTNERS, SRC, LANES), f32),
            pltpu.SemaphoreType.DMA((6,)),
        ]
        + partners,
        compiler_params=pltpu.CompilerParams(
            collective_id=0, has_side_effects=True, vmem_limit_bytes=16 * 1024 * 1024
        ),
        name="send_slots",
    )(params, offsets, counts, psf_y, psf_x, background, image)
    rest_model, rest_parts = pl.pallas_call(
        more_kernel,
        out_shape=[shape(BANDS, QUAD, QUAD), shape(SLOTS, LANES)],
        in_specs=vmem(5),
        out_specs=vmem(2),
        scratch_shapes=work_space(CHUNKS),
        compiler_params=pltpu.CompilerParams(vmem_limit_bytes=40 * 1024 * 1024),
        name="more_sources",
    )(slots, sky, observed, conv, back)
    return pl.pallas_call(
        return_kernel,
        out_shape=shape(SRC, PARAMS),
        in_specs=vmem(8),
        out_specs=vmem(1)[0],
        scratch_shapes=work_space(1)
        + [
            pltpu.VMEM((SLOTS, LANES), f32),
            pltpu.VMEM((PARTNERS, SRC, LANES), f32),
        ]
        + partners,
        compiler_params=pltpu.CompilerParams(
            collective_id=1, has_side_effects=True, vmem_limit_bytes=24 * 1024 * 1024
        ),
        name="return_parts",
    )(
        slots, rest_model, rest_parts, sky, observed, conv, back, prior
    )


def solution(mesh):
    placed = (
        P(("tile", "band"), None),
        P(("tile", "band"), None),
        P(("tile", "band")),
        P("tile", None, None, None),
        P("tile", None),
        P(),
        P(),
    )
    return jax.shard_map(
        body, mesh=mesh, in_specs=placed, out_specs=P(("tile", "band"), None), check_vma=False
    )
```

```python
import functools

import jax
import jax.numpy as jnp
from jax import lax
from jax.experimental import pallas as pl
from jax.experimental.pallas import tpu as pltpu
from jax.sharding import PartitionSpec as P

BANDS = 5
COMPONENTS = 12
PARAMS = 44
PATCH = 64
TAPS = 25
HALF = TAPS // 2
TILE_COLS = 8
TILE_SIDE = 384
QUAD = TILE_SIDE // 2
SRC = 8
TILES = 64
N_BAND = 4
PARTNERS = 16
SLOTS = PARTNERS * SRC
LANES = 128

TOP, LEFT, LIVE = 8, 9, 10
WEIGHT, SPREAD_Y, SPREAD_X = 16, 32, 48
HALVES = 64

PER_CHUNK = 21
COLS = 256
CHUNKS = -(-SLOTS // PER_CHUNK)
SPAN = 224
GROUP = 48
STEP = 80
HALF_SPAN = SPAN // 2
BACK_START = QUAD - HALF_SPAN

flux_scale = 2.0
prior_weight = 0.1
highest = lax.Precision.HIGHEST
f32 = jnp.float32
bf16 = jnp.bfloat16
MESH = pl.DeviceIdType.MESH


def iota(shape, axis):
    return lax.broadcasted_iota(jnp.int32, shape, axis)


def dot(a, b, dims=((1,), (0,)), precision=None):
    return lax.dot_general(a, b, (dims, ((), ())), precision=precision, preferred_element_type=f32)


def halves(x):
    high = x.astype(bf16)
    return high, (x - high.astype(f32)).astype(bf16)


def dot3(a, b, dims=((1,), (0,))):
    rows = a.shape[0] // 2
    both = dot(a, b[0], dims)
    return both[:rows] + (both[rows:] + dot(a[:rows], b[1], dims))


def wrapped_tile(row, col):
    return lax.rem(row + TILE_COLS, TILE_COLS) * TILE_COLS + lax.rem(col + TILE_COLS, TILE_COLS)


def inside(row, col):
    return (row >= 0) & (row < TILE_COLS) & (col >= 0) & (col < TILE_COLS)


def viewers(tile, band):
    home = lax.rem(tile + TILES // 2, TILES)
    row, col = home // TILE_COLS, lax.rem(home, TILE_COLS)
    found = []
    for step_y, half_y in ((1, 0), (-1, 1), (0, 0), (0, 1)):
        for step_x, half_x in ((1, 0), (-1, 1), (0, 0), (0, 1)):
            far = 2 * abs(step_y) + abs(step_x)
            answer = (2 * abs(step_y) + half_y) * 4 + 2 * abs(step_x) + half_x
            to_row, to_col = row + step_y, col + step_x
            found.append(
                (
                    wrapped_tile(to_row, to_col),
                    2 * half_y + half_x,
                    far * N_BAND + band,
                    answer,
                    inside(to_row, to_col),
                )
            )
    return found


def owners(tile, band):
    row, col = tile // TILE_COLS, lax.rem(tile, TILE_COLS)
    half_y, half_x = band // 2, lax.rem(band, 2)
    found = []
    for far_y in (1, 0):
        for far_x in (1, 0):
            from_row, from_col = row + far_y * (2 * half_y - 1), col + far_x * (2 * half_x - 1)
            holder = lax.rem(wrapped_tile(from_row, from_col) + TILES // 2, TILES)
            answer = (2 * far_y + half_y) * 4 + 2 * far_x + half_x
            for other in range(N_BAND):
                block = (2 * far_y + far_x) * N_BAND + other
                found.append((holder, other, block, answer, inside(from_row, from_col)))
    return found


def greet(barrier, callers):
    for other_tile, other_band, _, _, there in callers:

        @pl.when(there)
        def _():
            pl.semaphore_signal(
                barrier, inc=1, device_id=(other_tile, other_band), device_id_type=MESH
            )


def how_many(partners):
    return sum(there.astype(jnp.int32) for _, _, _, _, there in partners)


def parameter_lanes():
    lane = iota((1, LANES), 1)
    source = jnp.where(lane < BANDS + 2, lane, -1)
    source = jnp.where(lane == BANDS + 2, PARAMS - 1, source)
    for j, base in enumerate((WEIGHT, SPREAD_Y, SPREAD_X)):
        here = (lane >= base) & (lane < base + COMPONENTS)
        source = jnp.where(here, BANDS + 2 + 3 * (lane - base) + j, source)
    return (iota((PARAMS, LANES), 0) == source).astype(bf16)


def parameter_columns():
    lane = iota((LANES, LANES), 0)
    target = jnp.where(lane < BANDS + 2, lane, -1)
    target = jnp.where(lane == BANDS + 2, PARAMS - 1, target)
    for j, base in enumerate((WEIGHT, SPREAD_Y, SPREAD_X)):
        here = (lane >= base) & (lane < base + COMPONENTS)
        target = jnp.where(here, BANDS + 2 + 3 * (lane - base) + j, target)
    return (iota((LANES, LANES), 1) == target).astype(bf16)


def thirds_of(x):
    high = x.astype(bf16).astype(f32)
    low = (x - high).astype(bf16).astype(f32)
    return jnp.concatenate([high, low, x - high - low], axis=0).astype(bf16)


def summed(x):
    rows = x.shape[0] // 3
    return x[:rows] + (x[rows : 2 * rows] + x[2 * rows :])


def derived(params):
    raw = summed(dot(thirds_of(params), parameter_lanes()))
    lane = iota(raw.shape, 1)
    is_flux = lane < BANDS
    is_shift = (lane >= BANDS) & (lane < BANDS + 2)
    is_weight = (lane >= WEIGHT) & (lane < WEIGHT + COMPONENTS)
    is_spread = ((lane >= SPREAD_Y) & (lane < SPREAD_Y + COMPONENTS)) | (
        (lane >= SPREAD_X) & (lane < SPREAD_X + COMPONENTS)
    )
    most = jnp.max(jnp.where(is_weight, raw, -jnp.inf), axis=1, keepdims=True)
    power = jnp.where(is_weight, jnp.exp(jnp.where(is_weight, raw - most, 0.0)), 0.0)
    weight = power / jnp.sum(power, axis=1, keepdims=True)
    decay = jnp.exp(-jnp.abs(raw))
    soft = jnp.maximum(raw, 0.0) + jnp.log1p(decay)
    sigmoid = jnp.where(raw >= 0.0, 1.0, decay) / (1.0 + decay)
    curve = jnp.tanh(raw)
    softness = jnp.exp(0.25 * raw[:, BANDS + 2 : BANDS + 3])
    scale = (PATCH / 32.0) * softness
    spread = (0.5 + soft) * scale
    return raw, is_flux, is_shift, is_weight, is_spread, weight, soft, sigmoid, curve, scale, spread


def start_copies(pairs, sems):
    copies = [pltpu.make_async_copy(src, dst, sems.at[i]) for i, (src, dst) in enumerate(pairs)]
    for copy in copies:
        copy.start()
    return copies


def build_tables(taps, conv, back):
    tap, spot = iota((TAPS, COLS), 0), iota((TAPS, COLS), 1)

    def spread_out(x, places):
        return dot(x, (places == spot).astype(bf16))

    def turned(row, rows, shift):
        wide = jnp.broadcast_to(row, (rows, COLS))
        return pltpu.roll(wide, shift, 1, stride=1, stride_axis=0)

    lane = iota((HALF_SPAN, COLS), 1)
    for side in range(2):
        high, low = halves(taps[side])
        ahead = spread_out(high, tap) + spread_out(high, tap + STEP) + spread_out(low, tap + 2 * STEP)
        behind = [spread_out(half, lax.rem(COLS - tap, COLS)) for half in (high, low)]
        for b in range(BANDS):
            conv[side, b * GROUP : (b + 1) * GROUP, :] = turned(ahead[b : b + 1], GROUP, 0).astype(bf16)
            for part in range(2):
                shift = (HALF_SPAN - BACK_START) * part
                near = turned(behind[0][b : b + 1], HALF_SPAN, shift)
                far = turned(behind[0][b : b + 1], HALF_SPAN, shift + HALF_SPAN)
                small = turned(behind[1][b : b + 1], HALF_SPAN, shift)
                both = jnp.where(lane < HALF_SPAN, near, jnp.where(lane < SPAN, far, 0.0))
                small = jnp.where(lane < HALF_SPAN, small, 0.0)
                cols = slice(b * COLS, (b + 1) * COLS)
                back[side, part, :HALF_SPAN, cols] = both.astype(bf16)
                back[side, part, HALF_SPAN:, cols] = small.astype(bf16)


def send_kernel(
    params,
    offsets,
    counts,
    psf_y,
    psf_x,
    background,
    image,
    out,
    conv,
    back,
    prior,
    sky,
    observed,
    theta,
    place,
    taps,
    pixels,
    mine,
    landed,
    load_sem,
    send_sem,
    recv_sem,
):
    tile, band = lax.axis_index("tile"), lax.axis_index("band")
    loads = start_copies(
        (
            (params, theta),
            (offsets, place),
            (psf_y, taps.at[0]),
            (psf_x, taps.at[1]),
            (background, sky),
            (quadrant_of(image, tile, band), pixels),
        ),
        load_sem,
    )
    barrier = pltpu.get_barrier_semaphore()
    greet(barrier, owners(tile, band))
    for load in loads[:2]:
        load.wait()
    raw, is_flux, is_shift, is_weight, is_spread, weight, soft, sigmoid, curve, scale, spread = derived(
        theta[...]
    )
    slot, lane = iota((SRC, LANES), 0), iota((SRC, LANES), 1)
    live = (slot < counts[0]).astype(f32)
    row = jnp.where(is_flux, flux_scale * soft * live, 0.0)
    row = jnp.where(is_shift, (PATCH / 16.0) * curve, row)
    row = jnp.where(is_weight, weight, row)
    row = jnp.where(is_spread, spread, row)
    start = place[...].astype(f32)
    diagonal = iota((SRC, SRC), 0) == iota((SRC, SRC), 1)
    for side in range(2):
        start_side = jnp.sum(jnp.where(diagonal, start[side : side + 1, :], 0.0), axis=1, keepdims=True)
        row = jnp.where(lane == TOP + side, start_side, row)
    row = jnp.where(lane == LIVE, live, row)
    slope = jnp.where(is_flux, sigmoid / soft, 0.0)
    slope = jnp.where(is_shift, (PATCH / 16.0) * (1.0 - curve * curve), slope)
    slope = jnp.where(is_weight, 1.0, slope)
    slope = jnp.where(is_spread, scale * sigmoid, slope)
    mine[...] = row + pltpu.roll(slope, HALVES, 1)

    pl.semaphore_wait(barrier, how_many(viewers(tile, band)))
    copies = []
    for i, (other_tile, other_band, block, _, there) in enumerate(viewers(tile, band)):
        copy = pltpu.make_async_remote_copy(
            src_ref=mine,
            dst_ref=landed.at[block],
            send_sem=send_sem.at[i],
            recv_sem=recv_sem.at[block],
            device_id=(other_tile, other_band),
            device_id_type=MESH,
        )
        copies.append((copy, there))
        pl.when(there)(copy.start)
    for _, _, block, _, there in owners(tile, band):

        @pl.when(jnp.logical_not(there))
        def _():
            landed[block] = jnp.zeros((SRC, LANES), f32)

    for load in loads[2:]:
        load.wait()
    build_tables(taps, conv, back)

    prior[...] = prior_weight * theta[...] * live[:, :PARAMS]
    turn = lax.rem(COLS - lax.rem(band, 2) * (QUAD - COLS // 2), COLS)
    for b in range(BANDS):
        observed[b] = pltpu.roll(pixels[b], turn, 1)[:, :QUAD]

    for i, (other_tile, other_band, block, _, there) in enumerate(reversed(owners(tile, band))):
        copy = pltpu.make_async_remote_copy(
            src_ref=mine,
            dst_ref=landed.at[block],
            send_sem=send_sem.at[i],
            recv_sem=recv_sem.at[block],
            device_id=(other_tile, other_band),
            device_id_type=MESH,
        )
        pl.when(there)(copy.wait_recv)
        out[block * SRC : (block + 1) * SRC, :] = landed[block]
    for copy, there in copies:
        pl.when(there)(copy.wait_send)


def quadrant_of(image, tile, band):
    half_y, half_x = band // 2, lax.rem(band, 2)
    rows = pl.ds(pl.multiple_of(half_y * QUAD, QUAD), QUAD)
    cols = pl.ds(pl.multiple_of(half_x * (COLS // 2), COLS // 2), COLS)
    return image.at[0, :, rows, cols]


def column_comps():
    column = iota((1, COLS), 1)
    place = (column * 5462) >> 16
    return place, iota((16, COLS), 0) == column - COMPONENTS * place


def one_of(values, base):
    mine = column_comps()[1]
    return jnp.sum(jnp.where(mine, values[base : base + 16], 0.0), axis=0, keepdims=True)


def geometry(values, side):
    spread = one_of(values, (SPREAD_Y, SPREAD_X)[side])
    inverse = 1.0 / jnp.where(spread > 0.0, spread, 1.0)
    shift = values[BANDS + side : BANDS + side + 1]
    start = values[TOP + side : TOP + side + 1]
    spot = iota((SPAN, COLS), 0).astype(f32) - (start + float(HALF))
    inside = (spot >= 0.0) & (spot < PATCH)
    ratio = (spot + (0.5 - PATCH / 2.0) - shift) * inverse
    spot = iota((QUAD, COLS), 0).astype(f32) - start
    window = ((spot >= 0.0) & (spot < PATCH)).astype(f32)
    return inverse, inside, ratio, window


def render(values, conv, profiles, factors, c):
    weight = one_of(values, WEIGHT)
    for side in range(2):
        _, inside, ratio, window = geometry(values, side)
        profile = jnp.where(inside, jnp.exp(-0.5 * ratio * ratio), 0.0)
        profiles[c, side] = profile
        high, low = halves(profile)
        for start in range(0, QUAD, GROUP):
            rows = slice(start, start + STEP)
            blank = jnp.zeros((COLS - 3 * STEP, COLS), bf16)
            stack = jnp.concatenate([high[rows], low[rows], high[rows], blank], axis=0)
            factor = dot(conv[side], stack)
            seen = window[start : start + GROUP]
            for b in range(BANDS):
                scale = seen * (weight * values[b : b + 1]) if side == 0 else seen
                high_low = halves(factor[b * GROUP : (b + 1) * GROUP] * scale)
                for half in range(2):
                    put = half * QUAD + start
                    factors[side][c, b, put : put + GROUP] = high_low[half]


def model_of(factors, c, b):
    y_factor, x_factor = factors
    x = (x_factor[c, b, :QUAD], x_factor[c, b, QUAD:])
    return dot3(y_factor[c, b], x, ((1,), (1,)))


def leave(observed, background, model, residual, b):
    left = observed[b] / (background[0:1, b : b + 1] + model) - 1.0
    left = left * (1.0 / (PATCH * PATCH))
    for way, r in enumerate((left, left.T)):
        high_low = halves(r)
        for half in range(2):
            residual[way, b, half * QUAD : (half + 1) * QUAD] = high_low[half]


def pull(values, onehot, back, profiles, factors, residual, stack, c):
    y_factor, x_factor = factors
    mine = column_comps()[1]
    weight = one_of(values, WEIGHT)
    rows = []
    inverse_y, _, ratio_y, window_y = geometry(values, 0)
    inverse_x, _, ratio_x, window_x = geometry(values, 1)
    blank = jnp.zeros((COLS - SPAN, COLS), bf16)
    for b in range(BANDS):
        y = (y_factor[c, b, :QUAD], y_factor[c, b, QUAD:])
        x = (x_factor[c, b, :QUAD], x_factor[c, b, QUAD:])
        along_y = dot3(residual[0, b], x)
        along_x = dot3(residual[1, b], y)
        factor = y[0].astype(f32) + y[1].astype(f32)
        rows.append(jnp.sum(along_y * factor, axis=0, keepdims=True))
        along_y = along_y * (window_y * (weight * values[b : b + 1]))
        along_x = along_x * window_x
        for side, along in enumerate((along_y, along_x)):
            high, low = halves(along)
            for part, start in enumerate((0, BACK_START)):
                here = slice(start, start + HALF_SPAN)
                put = b * COLS
                stack[side, part, put : put + HALF_SPAN] = high[here]
                stack[side, part, put + HALF_SPAN : put + SPAN] = low[here]
                stack[side, part, put + SPAN : put + COLS] = blank
    ds = []
    for side in range(2):
        d = []
        for part in range(2):
            both = dot(back[side, part], stack[side, part])
            d.append(both[:HALF_SPAN] + both[HALF_SPAN:])
        ds.append(jnp.concatenate(d, axis=0))
    by_comp = rows[0] + rows[1] + rows[2] + rows[3] + rows[4]
    spreads = []
    for side, (d, inverse, ratio) in enumerate(((ds[0], inverse_y, ratio_y), (ds[1], inverse_x, ratio_x))):
        first = d * profiles[c, side] * ratio
        rows.append(inverse * jnp.sum(first, axis=0, keepdims=True))
        spreads.append(inverse * jnp.sum(first * ratio, axis=0, keepdims=True))
    pieces = rows + [jnp.zeros((16 - len(rows), COLS), f32)]
    for by in (by_comp, spreads[0], spreads[1]):
        pieces.append(jnp.where(mine, by, 0.0))
    high_low = jnp.concatenate(halves(jnp.concatenate(pieces, axis=0)), axis=0)
    return dot(onehot, high_low, ((1,), (1,)))


def find(data, tile, band):
    row, col = tile // TILE_COLS, lax.rem(tile, TILE_COLS)
    half_y, half_x = band // 2, lax.rem(band, 2)
    slot = iota((SLOTS, LANES), 0)
    lane = iota((SLOTS, LANES), 1)
    far_y, far_x = slot // (SLOTS // 2), lax.rem(slot // (SLOTS // 4), 2)

    def moved(far, half, place):
        origin = jnp.where(far == 0, 0, TILE_SIDE * (2 * half - 1)) - QUAD * half
        beyond = place + 2 * half - 1
        there = (far == 0) | ((beyond >= 0) & (beyond < TILE_COLS))
        return origin.astype(f32), there

    origin_y, there_y = moved(far_y, half_y, row)
    origin_x, there_x = moved(far_x, half_x, col)
    data = data + jnp.where(lane == TOP, origin_y, jnp.where(lane == LEFT, origin_x, 0.0))
    is_place = (lane == TOP) | (lane == LEFT)
    reach = is_place & (data > -PATCH) & (data < QUAD) | (lane == LIVE) & (data > 0.0)
    met = jnp.where(reach & there_y & there_x, 1.0, 0.0).astype(bf16)
    active = jnp.where(dot(met, jnp.ones((LANES, LANES), bf16)) > 2.5, 1.0, 0.0)
    count = jnp.sum(active, axis=0, keepdims=True)

    def chunk_makers():
        before = jnp.where(lane < slot, 1.0, 0.0).astype(bf16)
        order = dot(before, active.astype(bf16))
        order = jnp.where(active > 0.0, order, -1.0)[:, 0:1].astype(jnp.int32)
        place = column_comps()[0]

        def picked(c):
            here = (place < PER_CHUNK) & (order - c * PER_CHUNK == place)
            return jnp.where(here, 1.0, 0.0).astype(bf16)

        thirds = thirds_of(data.T[:HALVES])

        def gathered(c):
            return summed(dot(thirds, picked(c)))

        return picked, gathered

    return count, chunk_makers


def more_kernel(
    slots,
    sky,
    observed,
    conv,
    back,
    rest_model,
    rest_parts,
    profiles,
    y_factor,
    x_factor,
    residual,
    stack,
):
    tile, band = lax.axis_index("tile"), lax.axis_index("band")
    counts, chunk_makers = find(slots[...], tile, band)
    count = counts[0, 0].astype(jnp.int32)

    @pl.when(count > PER_CHUNK)
    def _():
        picked, gathered = chunk_makers()
        factors = (y_factor, x_factor)
        chunks = (count + PER_CHUNK - 1) // PER_CHUNK
        rest_model[...] = jnp.zeros_like(rest_model)
        rest_parts[...] = jnp.zeros_like(rest_parts)

        def add(c, carry):
            render(gathered(c), conv, profiles, factors, c)
            for b in range(BANDS):
                rest_model[b] += model_of(factors, c, b)
            return carry

        lax.fori_loop(1, chunks, add, 0)
        render(gathered(0), conv, profiles, factors, 0)
        for b in range(BANDS):
            model = rest_model[b] + model_of(factors, 0, b)
            leave(observed, sky, model, residual, b)

        def take(c, carry):
            rest_parts[...] += pull(gathered(c), picked(c), back, profiles, factors, residual, stack, c)
            return carry

        lax.fori_loop(1, chunks, take, 0)


def to_parameters(pulled, data):
    lane = iota((SLOTS, LANES), 1)
    is_weight = (lane >= WEIGHT) & (lane < WEIGHT + COMPONENTS)
    is_spread = ((lane >= SPREAD_Y) & (lane < SPREAD_Y + COMPONENTS)) | (
        (lane >= SPREAD_X) & (lane < SPREAD_X + COMPONENTS)
    )
    weight = jnp.where(is_weight, data, 0.0)
    groups = jnp.concatenate(
        [jnp.where(is_weight, pulled, 0.0), jnp.where(is_spread, pulled * data, 0.0)], axis=0
    )
    sums = summed(dot(thirds_of(groups), jnp.ones((LANES, LANES), bf16)))
    slope = jnp.where(lane < HALVES, pltpu.roll(data, HALVES, 1), 0.0)
    by_lane = pulled * slope - weight * sums[:SLOTS]
    by_lane = jnp.where(lane == BANDS + 2, 0.25 * sums[SLOTS:], by_lane)
    return summed(dot(thirds_of(by_lane), parameter_columns()))


def return_kernel(
    slots,
    rest_model,
    rest_parts,
    sky,
    observed,
    conv,
    back,
    prior,
    out,
    profiles,
    y_factor,
    x_factor,
    residual,
    stack,
    parts,
    landed,
    send_sem,
    recv_sem,
):
    tile, band = lax.axis_index("tile"), lax.axis_index("band")
    barrier = pltpu.get_barrier_semaphore()
    greet(barrier, viewers(tile, band))
    factors = (y_factor, x_factor)
    count, chunk_makers = find(slots[...], tile, band)
    picked, gathered = chunk_makers()
    onehot, values = picked(0), gathered(0)
    more = count[:, 0:1] > PER_CHUNK
    render(values, conv, profiles, factors, 0)
    for b in range(BANDS):
        model = model_of(factors, 0, b) + jnp.where(more, rest_model[b], 0.0)
        leave(observed, sky, model, residual, b)
    pulled = pull(values, onehot, back, profiles, factors, residual, stack, 0)
    pulled = pulled + jnp.where(more, rest_parts[...], 0.0)
    parts[...] = to_parameters(pulled + pltpu.roll(pulled, HALVES, 1), slots[...])

    pl.semaphore_wait(barrier, how_many(owners(tile, band)))
    copies = []
    for i, (other_tile, other_band, block, answer, there) in enumerate(owners(tile, band)):
        copy = pltpu.make_async_remote_copy(
            src_ref=parts.at[block * SRC : (block + 1) * SRC, :],
            dst_ref=landed.at[answer],
            send_sem=send_sem.at[i],
            recv_sem=recv_sem.at[answer],
            device_id=(other_tile, other_band),
            device_id_type=MESH,
        )
        copies.append((copy, there))
        pl.when(there)(copy.start)
    for _, _, _, answer, there in viewers(tile, band):

        @pl.when(jnp.logical_not(there))
        def _():
            landed[answer] = jnp.zeros((SRC, LANES), f32)

    total = jnp.zeros((SRC, LANES), f32)
    for i, (other_tile, other_band, _, answer, there) in enumerate(reversed(viewers(tile, band))):
        copy = pltpu.make_async_remote_copy(
            src_ref=parts.at[0:SRC, :],
            dst_ref=landed.at[answer],
            send_sem=send_sem.at[i],
            recv_sem=recv_sem.at[answer],
            device_id=(other_tile, other_band),
            device_id_type=MESH,
        )
        pl.when(there)(copy.wait_recv)
        total = total + landed[answer]
    out[...] = total[:, :PARAMS] - prior[...]
    for copy, there in copies:
        pl.when(there)(copy.wait_send)


def vmem(count):
    return [pl.BlockSpec(memory_space=pltpu.VMEM)] * count


def hbm(count):
    return [pl.BlockSpec(memory_space=pltpu.HBM)] * count


def work_space(chunks):
    return [
        pltpu.VMEM((chunks, 2, SPAN, COLS), f32),
        pltpu.VMEM((chunks, BANDS, 2 * QUAD, COLS), bf16),
        pltpu.VMEM((chunks, BANDS, 2 * QUAD, COLS), bf16),
        pltpu.VMEM((2, BANDS, 2 * QUAD, QUAD), bf16),
        pltpu.VMEM((2, 2, BANDS * COLS, COLS), bf16),
    ]


def shape(*dims, kind=f32):
    return jax.ShapeDtypeStruct(dims, kind)


def body(params, offsets, counts, image, background, psf_y, psf_x):
    smem = pl.BlockSpec(memory_space=pltpu.SMEM)
    params, offsets, image, background, psf_y, psf_x = (
        pltpu.with_memory_space_constraint(x, pltpu.HBM)
        for x in (params, offsets.T, image, background, psf_y, psf_x)
    )
    partners = [pltpu.SemaphoreType.DMA((PARTNERS,))] * 2
    slots, conv, back, prior, sky, observed = pl.pallas_call(
        send_kernel,
        out_shape=[shape(SLOTS, LANES)]
        + [shape(2, BANDS * GROUP, COLS, kind=bf16), shape(2, 2, SPAN, BANDS * COLS, kind=bf16)]
        + [shape(SRC, PARAMS), shape(1, BANDS), shape(BANDS, QUAD, QUAD)],
        in_specs=hbm(2) + [smem] + hbm(4),
        out_specs=vmem(6),
        scratch_shapes=[
            pltpu.VMEM((SRC, PARAMS), f32),
            pltpu.VMEM((2, SRC), jnp.int32),
            pltpu.VMEM((2, BANDS, TAPS), f32),
            pltpu.VMEM((BANDS, QUAD, COLS), f32),
            pltpu.VMEM((SRC, LANES), f32),
            pltpu.VMEM((PARTNERS, SRC, LANES), f32),
            pltpu.SemaphoreType.DMA((6,)),
        ]
        + partners,
        compiler_params=pltpu.CompilerParams(
            collective_id=0, has_side_effects=True, vmem_limit_bytes=16 * 1024 * 1024
        ),
        name="send_slots",
    )(params, offsets, counts, psf_y, psf_x, background, image)
    rest_model, rest_parts = pl.pallas_call(
        more_kernel,
        out_shape=[shape(BANDS, QUAD, QUAD), shape(SLOTS, LANES)],
        in_specs=vmem(5),
        out_specs=vmem(2),
        scratch_shapes=work_space(CHUNKS),
        compiler_params=pltpu.CompilerParams(vmem_limit_bytes=40 * 1024 * 1024),
        name="more_sources",
    )(slots, sky, observed, conv, back)
    return pl.pallas_call(
        return_kernel,
        out_shape=shape(SRC, PARAMS),
        in_specs=vmem(8),
        out_specs=vmem(1)[0],
        scratch_shapes=work_space(1)
        + [
            pltpu.VMEM((SLOTS, LANES), f32),
            pltpu.VMEM((PARTNERS, SRC, LANES), f32),
        ]
        + partners,
        compiler_params=pltpu.CompilerParams(
            collective_id=1, has_side_effects=True, vmem_limit_bytes=24 * 1024 * 1024
        ),
        name="return_parts",
    )(
        slots, rest_model, rest_parts, sky, observed, conv, back, prior
    )


def solution(mesh):
    placed = (
        P(("tile", "band"), None),
        P(("tile", "band"), None),
        P(("tile", "band")),
        P("tile", None, None, None),
        P("tile", None),
        P(),
        P(),
    )
    return jax.shard_map(
        body, mesh=mesh, in_specs=placed, out_specs=P(("tile", "band"), None), check_vma=False
    )
```

```python
import functools

import jax
import jax.numpy as jnp
from jax import lax
from jax.experimental import pallas as pl
from jax.experimental.pallas import tpu as pltpu
from jax.sharding import PartitionSpec as P

BANDS = 5
COMPONENTS = 12
PARAMS = 44
PATCH = 64
TAPS = 25
HALF = TAPS // 2
TILE_COLS = 8
TILE_SIDE = 384
QUAD = TILE_SIDE // 2
SRC = 8
TILES = 64
N_BAND = 4
PARTNERS = 16
SLOTS = PARTNERS * SRC
LANES = 128

TOP, LEFT, LIVE = 8, 9, 10
WEIGHT, SPREAD_Y, SPREAD_X = 16, 32, 48
HALVES = 64

PER_CHUNK = 21
COLS = 256
CHUNKS = -(-SLOTS // PER_CHUNK)
SPAN = 224
GROUP = 48
STEP = 80
HALF_SPAN = SPAN // 2
BACK_START = QUAD - HALF_SPAN

flux_scale = 2.0
prior_weight = 0.1
highest = lax.Precision.HIGHEST
f32 = jnp.float32
bf16 = jnp.bfloat16
MESH = pl.DeviceIdType.MESH


def iota(shape, axis):
    return lax.broadcasted_iota(jnp.int32, shape, axis)


def dot(a, b, dims=((1,), (0,)), precision=None):
    return lax.dot_general(a, b, (dims, ((), ())), precision=precision, preferred_element_type=f32)


def halves(x):
    high = x.astype(bf16)
    return high, (x - high.astype(f32)).astype(bf16)


def dot3(a, b, dims=((1,), (0,))):
    rows = a.shape[0] // 2
    both = dot(a, b[0], dims)
    return both[:rows] + (both[rows:] + dot(a[:rows], b[1], dims))


def wrapped_tile(row, col):
    return lax.rem(row + TILE_COLS, TILE_COLS) * TILE_COLS + lax.rem(col + TILE_COLS, TILE_COLS)


def inside(row, col):
    return (row >= 0) & (row < TILE_COLS) & (col >= 0) & (col < TILE_COLS)


def viewers(tile, band):
    home = lax.rem(tile + TILES // 2, TILES)
    row, col = home // TILE_COLS, lax.rem(home, TILE_COLS)
    found = []
    for step_y, half_y in ((1, 0), (-1, 1), (0, 0), (0, 1)):
        for step_x, half_x in ((1, 0), (-1, 1), (0, 0), (0, 1)):
            far = 2 * abs(step_y) + abs(step_x)
            answer = (2 * abs(step_y) + half_y) * 4 + 2 * abs(step_x) + half_x
            to_row, to_col = row + step_y, col + step_x
            found.append(
                (
                    wrapped_tile(to_row, to_col),
                    2 * half_y + half_x,
                    far * N_BAND + band,
                    answer,
                    inside(to_row, to_col),
                )
            )
    return found


def owners(tile, band):
    row, col = tile // TILE_COLS, lax.rem(tile, TILE_COLS)
    half_y, half_x = band // 2, lax.rem(band, 2)
    found = []
    for far_y in (1, 0):
        for far_x in (1, 0):
            from_row, from_col = row + far_y * (2 * half_y - 1), col + far_x * (2 * half_x - 1)
            holder = lax.rem(wrapped_tile(from_row, from_col) + TILES // 2, TILES)
            answer = (2 * far_y + half_y) * 4 + 2 * far_x + half_x
            for other in range(N_BAND):
                block = (2 * far_y + far_x) * N_BAND + other
                found.append((holder, other, block, answer, inside(from_row, from_col)))
    return found


def greet(barrier, callers):
    for other_tile, other_band, _, _, there in callers:

        @pl.when(there)
        def _():
            pl.semaphore_signal(
                barrier, inc=1, device_id=(other_tile, other_band), device_id_type=MESH
            )


def how_many(partners):
    return sum(there.astype(jnp.int32) for _, _, _, _, there in partners)


def parameter_lanes():
    lane = iota((1, LANES), 1)
    source = jnp.where(lane < BANDS + 2, lane, -1)
    source = jnp.where(lane == BANDS + 2, PARAMS - 1, source)
    for j, base in enumerate((WEIGHT, SPREAD_Y, SPREAD_X)):
        here = (lane >= base) & (lane < base + COMPONENTS)
        source = jnp.where(here, BANDS + 2 + 3 * (lane - base) + j, source)
    return (iota((PARAMS, LANES), 0) == source).astype(bf16)


def parameter_columns():
    lane = iota((LANES, LANES), 0)
    target = jnp.where(lane < BANDS + 2, lane, -1)
    target = jnp.where(lane == BANDS + 2, PARAMS - 1, target)
    for j, base in enumerate((WEIGHT, SPREAD_Y, SPREAD_X)):
        here = (lane >= base) & (lane < base + COMPONENTS)
        target = jnp.where(here, BANDS + 2 + 3 * (lane - base) + j, target)
    return (iota((LANES, LANES), 1) == target).astype(bf16)


def thirds_of(x):
    high = x.astype(bf16).astype(f32)
    low = (x - high).astype(bf16).astype(f32)
    return jnp.concatenate([high, low, x - high - low], axis=0).astype(bf16)


def summed(x):
    rows = x.shape[0] // 3
    return x[:rows] + (x[rows : 2 * rows] + x[2 * rows :])


def twice(x, table):
    rows = x.shape[0]
    both = dot(jnp.concatenate(halves(x), axis=0), table)
    return both[:rows] + both[rows:]


def derived(params):
    raw = summed(dot(thirds_of(params), parameter_lanes()))
    lane = iota(raw.shape, 1)
    is_flux = lane < BANDS
    is_shift = (lane >= BANDS) & (lane < BANDS + 2)
    is_weight = (lane >= WEIGHT) & (lane < WEIGHT + COMPONENTS)
    is_spread = ((lane >= SPREAD_Y) & (lane < SPREAD_Y + COMPONENTS)) | (
        (lane >= SPREAD_X) & (lane < SPREAD_X + COMPONENTS)
    )
    most = jnp.max(jnp.where(is_weight, raw, -jnp.inf), axis=1, keepdims=True)
    power = jnp.where(is_weight, jnp.exp(jnp.where(is_weight, raw - most, 0.0)), 0.0)
    weight = power / jnp.sum(power, axis=1, keepdims=True)
    decay = jnp.exp(-jnp.abs(raw))
    soft = jnp.maximum(raw, 0.0) + jnp.log1p(decay)
    sigmoid = jnp.where(raw >= 0.0, 1.0, decay) / (1.0 + decay)
    curve = jnp.tanh(raw)
    softness = jnp.exp(0.25 * raw[:, BANDS + 2 : BANDS + 3])
    scale = (PATCH / 32.0) * softness
    spread = (0.5 + soft) * scale
    return raw, is_flux, is_shift, is_weight, is_spread, weight, soft, sigmoid, curve, scale, spread


def start_copies(pairs, sems):
    copies = [pltpu.make_async_copy(src, dst, sems.at[i]) for i, (src, dst) in enumerate(pairs)]
    for copy in copies:
        copy.start()
    return copies


def build_tables(taps, conv, back):
    tap, spot = iota((TAPS, COLS), 0), iota((TAPS, COLS), 1)

    def spread_out(x, places):
        return dot(x, (places == spot).astype(bf16))

    def turned(row, rows, shift):
        wide = jnp.broadcast_to(row, (rows, COLS))
        return pltpu.roll(wide, shift, 1, stride=1, stride_axis=0)

    lane = iota((HALF_SPAN, COLS), 1)
    for side in range(2):
        high, low = halves(taps[side])
        ahead = spread_out(high, tap) + spread_out(high, tap + STEP) + spread_out(low, tap + 2 * STEP)
        behind = [spread_out(half, lax.rem(COLS - tap, COLS)) for half in (high, low)]
        for b in range(BANDS):
            conv[side, b * GROUP : (b + 1) * GROUP, :] = turned(ahead[b : b + 1], GROUP, 0).astype(bf16)
            for part in range(2):
                shift = (HALF_SPAN - BACK_START) * part
                near = turned(behind[0][b : b + 1], HALF_SPAN, shift)
                far = turned(behind[0][b : b + 1], HALF_SPAN, shift + HALF_SPAN)
                small = turned(behind[1][b : b + 1], HALF_SPAN, shift)
                both = jnp.where(lane < HALF_SPAN, near, jnp.where(lane < SPAN, far, 0.0))
                small = jnp.where(lane < HALF_SPAN, small, 0.0)
                cols = slice(b * COLS, (b + 1) * COLS)
                back[side, part, :HALF_SPAN, cols] = both.astype(bf16)
                back[side, part, HALF_SPAN:, cols] = small.astype(bf16)


def send_kernel(
    params,
    offsets,
    counts,
    psf_y,
    psf_x,
    background,
    image,
    out,
    conv,
    back,
    prior,
    sky,
    observed,
    theta,
    place,
    taps,
    pixels,
    mine,
    landed,
    load_sem,
    send_sem,
    recv_sem,
):
    tile, band = lax.axis_index("tile"), lax.axis_index("band")
    loads = start_copies(
        (
            (params, theta),
            (offsets, place),
            (psf_y, taps.at[0]),
            (psf_x, taps.at[1]),
            (background, sky),
            (quadrant_of(image, tile, band), pixels),
        ),
        load_sem,
    )
    barrier = pltpu.get_barrier_semaphore()
    greet(barrier, owners(tile, band))
    for load in loads[:2]:
        load.wait()
    raw, is_flux, is_shift, is_weight, is_spread, weight, soft, sigmoid, curve, scale, spread = derived(
        theta[...]
    )
    slot, lane = iota((SRC, LANES), 0), iota((SRC, LANES), 1)
    live = (slot < counts[0]).astype(f32)
    row = jnp.where(is_flux, flux_scale * soft * live, 0.0)
    row = jnp.where(is_shift, (PATCH / 16.0) * curve, row)
    row = jnp.where(is_weight, weight, row)
    row = jnp.where(is_spread, spread, row)
    start = place[...].astype(f32)
    diagonal = iota((SRC, SRC), 0) == iota((SRC, SRC), 1)
    for side in range(2):
        start_side = jnp.sum(jnp.where(diagonal, start[side : side + 1, :], 0.0), axis=1, keepdims=True)
        row = jnp.where(lane == TOP + side, start_side, row)
    row = jnp.where(lane == LIVE, live, row)
    slope = jnp.where(is_flux, sigmoid / soft, 0.0)
    slope = jnp.where(is_shift, (PATCH / 16.0) * (1.0 - curve * curve), slope)
    slope = jnp.where(is_weight, 1.0, slope)
    slope = jnp.where(is_spread, scale * sigmoid, slope)
    mine[...] = row + pltpu.roll(slope, HALVES, 1)

    pl.semaphore_wait(barrier, how_many(viewers(tile, band)))
    copies = []
    for i, (other_tile, other_band, block, _, there) in enumerate(viewers(tile, band)):
        copy = pltpu.make_async_remote_copy(
            src_ref=mine,
            dst_ref=landed.at[block],
            send_sem=send_sem.at[i],
            recv_sem=recv_sem.at[block],
            device_id=(other_tile, other_band),
            device_id_type=MESH,
        )
        copies.append((copy, there))
        pl.when(there)(copy.start)
    for _, _, block, _, there in owners(tile, band):

        @pl.when(jnp.logical_not(there))
        def _():
            landed[block] = jnp.zeros((SRC, LANES), f32)

    for load in loads[2:]:
        load.wait()
    build_tables(taps, conv, back)

    prior[...] = prior_weight * theta[...] * live[:, :PARAMS]
    turn = lax.rem(COLS - lax.rem(band, 2) * (QUAD - COLS // 2), COLS)
    for b in range(BANDS):
        observed[b] = pltpu.roll(pixels[b], turn, 1)[:, :QUAD]

    for i, (other_tile, other_band, block, _, there) in enumerate(reversed(owners(tile, band))):
        copy = pltpu.make_async_remote_copy(
            src_ref=mine,
            dst_ref=landed.at[block],
            send_sem=send_sem.at[i],
            recv_sem=recv_sem.at[block],
            device_id=(other_tile, other_band),
            device_id_type=MESH,
        )
        pl.when(there)(copy.wait_recv)
        out[block * SRC : (block + 1) * SRC, :] = landed[block]
    for copy, there in copies:
        pl.when(there)(copy.wait_send)


def quadrant_of(image, tile, band):
    half_y, half_x = band // 2, lax.rem(band, 2)
    rows = pl.ds(pl.multiple_of(half_y * QUAD, QUAD), QUAD)
    cols = pl.ds(pl.multiple_of(half_x * (COLS // 2), COLS // 2), COLS)
    return image.at[0, :, rows, cols]


def column_comps():
    column = iota((1, COLS), 1)
    place = (column * 5462) >> 16
    return place, iota((16, COLS), 0) == column - COMPONENTS * place


def one_of(values, base):
    mine = column_comps()[1]
    return jnp.sum(jnp.where(mine, values[base : base + 16], 0.0), axis=0, keepdims=True)


def geometry(values, side):
    spread = one_of(values, (SPREAD_Y, SPREAD_X)[side])
    inverse = 1.0 / jnp.where(spread > 0.0, spread, 1.0)
    shift = values[BANDS + side : BANDS + side + 1]
    start = values[TOP + side : TOP + side + 1]
    spot = iota((SPAN, COLS), 0).astype(f32) - (start + float(HALF))
    inside = (spot >= 0.0) & (spot < PATCH)
    ratio = (spot + (0.5 - PATCH / 2.0) - shift) * inverse
    spot = iota((QUAD, COLS), 0).astype(f32) - start
    window = ((spot >= 0.0) & (spot < PATCH)).astype(f32)
    return inverse, inside, ratio, window


def render(values, conv, profiles, factors, c):
    weight = one_of(values, WEIGHT)
    for side in range(2):
        _, inside, ratio, window = geometry(values, side)
        profile = jnp.where(inside, jnp.exp(-0.5 * ratio * ratio), 0.0)
        profiles[c, side] = profile
        high, low = halves(profile)
        for start in range(0, QUAD, GROUP):
            rows = slice(start, start + STEP)
            blank = jnp.zeros((COLS - 3 * STEP, COLS), bf16)
            stack = jnp.concatenate([high[rows], low[rows], high[rows], blank], axis=0)
            factor = dot(conv[side], stack)
            seen = window[start : start + GROUP]
            for b in range(BANDS):
                scale = seen * (weight * values[b : b + 1]) if side == 0 else seen
                high_low = halves(factor[b * GROUP : (b + 1) * GROUP] * scale)
                for half in range(2):
                    put = half * QUAD + start
                    factors[side][c, b, put : put + GROUP] = high_low[half]


def model_of(factors, c, b):
    y_factor, x_factor = factors
    x = (x_factor[c, b, :QUAD], x_factor[c, b, QUAD:])
    return dot3(y_factor[c, b], x, ((1,), (1,)))


def leave(observed, background, model, residual, b):
    left = observed[b] / (background[0:1, b : b + 1] + model) - 1.0
    left = left * (1.0 / (PATCH * PATCH))
    for way, r in enumerate((left, left.T)):
        high_low = halves(r)
        for half in range(2):
            residual[way, b, half * QUAD : (half + 1) * QUAD] = high_low[half]


def pull(values, onehot, back, profiles, factors, residual, stack, c):
    y_factor, x_factor = factors
    mine = column_comps()[1]
    weight = one_of(values, WEIGHT)
    rows = []
    inverse_y, _, ratio_y, window_y = geometry(values, 0)
    inverse_x, _, ratio_x, window_x = geometry(values, 1)
    blank = jnp.zeros((COLS - SPAN, COLS), bf16)
    for b in range(BANDS):
        y = (y_factor[c, b, :QUAD], y_factor[c, b, QUAD:])
        x = (x_factor[c, b, :QUAD], x_factor[c, b, QUAD:])
        along_y = dot3(residual[0, b], x)
        along_x = dot3(residual[1, b], y)
        factor = y[0].astype(f32) + y[1].astype(f32)
        rows.append(jnp.sum(along_y * factor, axis=0, keepdims=True))
        along_y = along_y * (window_y * (weight * values[b : b + 1]))
        along_x = along_x * window_x
        for side, along in enumerate((along_y, along_x)):
            high, low = halves(along)
            for part, start in enumerate((0, BACK_START)):
                here = slice(start, start + HALF_SPAN)
                put = b * COLS
                stack[side, part, put : put + HALF_SPAN] = high[here]
                stack[side, part, put + HALF_SPAN : put + SPAN] = low[here]
                stack[side, part, put + SPAN : put + COLS] = blank
    ds = []
    for side in range(2):
        d = []
        for part in range(2):
            both = dot(back[side, part], stack[side, part])
            d.append(both[:HALF_SPAN] + both[HALF_SPAN:])
        ds.append(jnp.concatenate(d, axis=0))
    by_comp = rows[0] + rows[1] + rows[2] + rows[3] + rows[4]
    spreads = []
    for side, (d, inverse, ratio) in enumerate(((ds[0], inverse_y, ratio_y), (ds[1], inverse_x, ratio_x))):
        first = d * profiles[c, side] * ratio
        rows.append(inverse * jnp.sum(first, axis=0, keepdims=True))
        spreads.append(inverse * jnp.sum(first * ratio, axis=0, keepdims=True))
    pieces = rows + [jnp.zeros((16 - len(rows), COLS), f32)]
    for by in (by_comp, spreads[0], spreads[1]):
        pieces.append(jnp.where(mine, by, 0.0))
    high_low = jnp.concatenate(halves(jnp.concatenate(pieces, axis=0)), axis=0)
    return dot(onehot, high_low, ((1,), (1,)))


def find(data, tile, band):
    row, col = tile // TILE_COLS, lax.rem(tile, TILE_COLS)
    half_y, half_x = band // 2, lax.rem(band, 2)
    slot = iota((SLOTS, LANES), 0)
    lane = iota((SLOTS, LANES), 1)
    far_y, far_x = slot // (SLOTS // 2), lax.rem(slot // (SLOTS // 4), 2)

    def moved(far, half, place):
        origin = jnp.where(far == 0, 0, TILE_SIDE * (2 * half - 1)) - QUAD * half
        beyond = place + 2 * half - 1
        there = (far == 0) | ((beyond >= 0) & (beyond < TILE_COLS))
        return origin.astype(f32), there

    origin_y, there_y = moved(far_y, half_y, row)
    origin_x, there_x = moved(far_x, half_x, col)
    data = data + jnp.where(lane == TOP, origin_y, jnp.where(lane == LEFT, origin_x, 0.0))
    is_place = (lane == TOP) | (lane == LEFT)
    reach = is_place & (data > -PATCH) & (data < QUAD) | (lane == LIVE) & (data > 0.0)
    met = jnp.where(reach & there_y & there_x, 1.0, 0.0).astype(bf16)
    active = jnp.where(dot(met, jnp.ones((LANES, LANES), bf16)) > 2.5, 1.0, 0.0)
    count = jnp.sum(active, axis=0, keepdims=True)

    def chunk_makers():
        before = jnp.where(lane < slot, 1.0, 0.0).astype(bf16)
        order = dot(before, active.astype(bf16))
        order = jnp.where(active > 0.0, order, -1.0)[:, 0:1].astype(jnp.int32)
        place = column_comps()[0]

        def picked(c):
            here = (place < PER_CHUNK) & (order - c * PER_CHUNK == place)
            return jnp.where(here, 1.0, 0.0).astype(bf16)

        thirds = thirds_of(data.T[:HALVES])

        def gathered(c):
            return summed(dot(thirds, picked(c)))

        return picked, gathered

    return count, chunk_makers


def more_kernel(
    slots,
    sky,
    observed,
    conv,
    back,
    rest_model,
    rest_parts,
    profiles,
    y_factor,
    x_factor,
    residual,
    stack,
):
    tile, band = lax.axis_index("tile"), lax.axis_index("band")
    counts, chunk_makers = find(slots[...], tile, band)
    count = counts[0, 0].astype(jnp.int32)

    @pl.when(count > PER_CHUNK)
    def _():
        picked, gathered = chunk_makers()
        factors = (y_factor, x_factor)
        chunks = (count + PER_CHUNK - 1) // PER_CHUNK
        rest_model[...] = jnp.zeros_like(rest_model)
        rest_parts[...] = jnp.zeros_like(rest_parts)

        def add(c, carry):
            render(gathered(c), conv, profiles, factors, c)
            for b in range(BANDS):
                rest_model[b] += model_of(factors, c, b)
            return carry

        lax.fori_loop(1, chunks, add, 0)
        render(gathered(0), conv, profiles, factors, 0)
        for b in range(BANDS):
            model = rest_model[b] + model_of(factors, 0, b)
            leave(observed, sky, model, residual, b)

        def take(c, carry):
            rest_parts[...] += pull(gathered(c), picked(c), back, profiles, factors, residual, stack, c)
            return carry

        lax.fori_loop(1, chunks, take, 0)


def to_parameters(pulled, data):
    lane = iota((SLOTS, LANES), 1)
    is_weight = (lane >= WEIGHT) & (lane < WEIGHT + COMPONENTS)
    is_spread = ((lane >= SPREAD_Y) & (lane < SPREAD_Y + COMPONENTS)) | (
        (lane >= SPREAD_X) & (lane < SPREAD_X + COMPONENTS)
    )
    weight = jnp.where(is_weight, data, 0.0)
    groups = jnp.concatenate(
        [jnp.where(is_weight, pulled, 0.0), jnp.where(is_spread, pulled * data, 0.0)], axis=0
    )
    sums = twice(groups, jnp.ones((LANES, LANES), bf16))
    slope = jnp.where(lane < HALVES, pltpu.roll(data, HALVES, 1), 0.0)
    by_lane = pulled * slope - weight * sums[:SLOTS]
    by_lane = jnp.where(lane == BANDS + 2, 0.25 * sums[SLOTS:], by_lane)
    return twice(by_lane, parameter_columns())


def return_kernel(
    slots,
    rest_model,
    rest_parts,
    sky,
    observed,
    conv,
    back,
    prior,
    out,
    profiles,
    y_factor,
    x_factor,
    residual,
    stack,
    parts,
    landed,
    send_sem,
    recv_sem,
):
    tile, band = lax.axis_index("tile"), lax.axis_index("band")
    barrier = pltpu.get_barrier_semaphore()
    greet(barrier, viewers(tile, band))
    factors = (y_factor, x_factor)
    count, chunk_makers = find(slots[...], tile, band)
    picked, gathered = chunk_makers()
    onehot, values = picked(0), gathered(0)
    more = count[:, 0:1] > PER_CHUNK
    render(values, conv, profiles, factors, 0)
    for b in range(BANDS):
        model = model_of(factors, 0, b) + jnp.where(more, rest_model[b], 0.0)
        leave(observed, sky, model, residual, b)
    pulled = pull(values, onehot, back, profiles, factors, residual, stack, 0)
    pulled = pulled + jnp.where(more, rest_parts[...], 0.0)
    parts[...] = to_parameters(pulled + pltpu.roll(pulled, HALVES, 1), slots[...])

    pl.semaphore_wait(barrier, how_many(owners(tile, band)))
    copies = []
    for i, (other_tile, other_band, block, answer, there) in enumerate(owners(tile, band)):
        copy = pltpu.make_async_remote_copy(
            src_ref=parts.at[block * SRC : (block + 1) * SRC, :],
            dst_ref=landed.at[answer],
            send_sem=send_sem.at[i],
            recv_sem=recv_sem.at[answer],
            device_id=(other_tile, other_band),
            device_id_type=MESH,
        )
        copies.append((copy, there))
        pl.when(there)(copy.start)
    for _, _, _, answer, there in viewers(tile, band):

        @pl.when(jnp.logical_not(there))
        def _():
            landed[answer] = jnp.zeros((SRC, LANES), f32)

    total = jnp.zeros((SRC, LANES), f32)
    for i, (other_tile, other_band, _, answer, there) in enumerate(reversed(viewers(tile, band))):
        copy = pltpu.make_async_remote_copy(
            src_ref=parts.at[0:SRC, :],
            dst_ref=landed.at[answer],
            send_sem=send_sem.at[i],
            recv_sem=recv_sem.at[answer],
            device_id=(other_tile, other_band),
            device_id_type=MESH,
        )
        pl.when(there)(copy.wait_recv)
        total = total + landed[answer]
    out[...] = total[:, :PARAMS] - prior[...]
    for copy, there in copies:
        pl.when(there)(copy.wait_send)


def vmem(count):
    return [pl.BlockSpec(memory_space=pltpu.VMEM)] * count


def hbm(count):
    return [pl.BlockSpec(memory_space=pltpu.HBM)] * count


def work_space(chunks):
    return [
        pltpu.VMEM((chunks, 2, SPAN, COLS), f32),
        pltpu.VMEM((chunks, BANDS, 2 * QUAD, COLS), bf16),
        pltpu.VMEM((chunks, BANDS, 2 * QUAD, COLS), bf16),
        pltpu.VMEM((2, BANDS, 2 * QUAD, QUAD), bf16),
        pltpu.VMEM((2, 2, BANDS * COLS, COLS), bf16),
    ]


def shape(*dims, kind=f32):
    return jax.ShapeDtypeStruct(dims, kind)


def body(params, offsets, counts, image, background, psf_y, psf_x):
    smem = pl.BlockSpec(memory_space=pltpu.SMEM)
    params, offsets, image, background, psf_y, psf_x = (
        pltpu.with_memory_space_constraint(x, pltpu.HBM)
        for x in (params, offsets.T, image, background, psf_y, psf_x)
    )
    partners = [pltpu.SemaphoreType.DMA((PARTNERS,))] * 2
    slots, conv, back, prior, sky, observed = pl.pallas_call(
        send_kernel,
        out_shape=[shape(SLOTS, LANES)]
        + [shape(2, BANDS * GROUP, COLS, kind=bf16), shape(2, 2, SPAN, BANDS * COLS, kind=bf16)]
        + [shape(SRC, PARAMS), shape(1, BANDS), shape(BANDS, QUAD, QUAD)],
        in_specs=hbm(2) + [smem] + hbm(4),
        out_specs=vmem(6),
        scratch_shapes=[
            pltpu.VMEM((SRC, PARAMS), f32),
            pltpu.VMEM((2, SRC), jnp.int32),
            pltpu.VMEM((2, BANDS, TAPS), f32),
            pltpu.VMEM((BANDS, QUAD, COLS), f32),
            pltpu.VMEM((SRC, LANES), f32),
            pltpu.VMEM((PARTNERS, SRC, LANES), f32),
            pltpu.SemaphoreType.DMA((6,)),
        ]
        + partners,
        compiler_params=pltpu.CompilerParams(
            collective_id=0, has_side_effects=True, vmem_limit_bytes=16 * 1024 * 1024
        ),
        name="send_slots",
    )(params, offsets, counts, psf_y, psf_x, background, image)
    rest_model, rest_parts = pl.pallas_call(
        more_kernel,
        out_shape=[shape(BANDS, QUAD, QUAD), shape(SLOTS, LANES)],
        in_specs=vmem(5),
        out_specs=vmem(2),
        scratch_shapes=work_space(CHUNKS),
        compiler_params=pltpu.CompilerParams(vmem_limit_bytes=40 * 1024 * 1024),
        name="more_sources",
    )(slots, sky, observed, conv, back)
    return pl.pallas_call(
        return_kernel,
        out_shape=shape(SRC, PARAMS),
        in_specs=vmem(8),
        out_specs=vmem(1)[0],
        scratch_shapes=work_space(1)
        + [
            pltpu.VMEM((SLOTS, LANES), f32),
            pltpu.VMEM((PARTNERS, SRC, LANES), f32),
        ]
        + partners,
        compiler_params=pltpu.CompilerParams(
            collective_id=1, has_side_effects=True, vmem_limit_bytes=24 * 1024 * 1024
        ),
        name="return_parts",
    )(
        slots, rest_model, rest_parts, sky, observed, conv, back, prior
    )


def solution(mesh):
    placed = (
        P(("tile", "band"), None),
        P(("tile", "band"), None),
        P(("tile", "band")),
        P("tile", None, None, None),
        P("tile", None),
        P(),
        P(),
    )
    return jax.shard_map(
        body, mesh=mesh, in_specs=placed, out_specs=P(("tile", "band"), None), check_vma=False
    )
```

```python
import functools

import jax
import jax.numpy as jnp
from jax import lax
from jax.experimental import pallas as pl
from jax.experimental.pallas import tpu as pltpu
from jax.sharding import PartitionSpec as P

BANDS = 5
COMPONENTS = 12
PARAMS = 44
PATCH = 64
TAPS = 25
HALF = TAPS // 2
TILE_COLS = 8
TILE_SIDE = 384
QUAD = TILE_SIDE // 2
SRC = 8
TILES = 64
N_BAND = 4
PARTNERS = 16
FARTHEST_FIRST = (2, 1, 3, 0)
SLOTS = PARTNERS * SRC
LANES = 128

TOP, LEFT, LIVE = 8, 9, 10
WEIGHT, SPREAD_Y, SPREAD_X = 16, 32, 48
HALVES = 64

PER_CHUNK = 21
COLS = 256
CHUNKS = -(-SLOTS // PER_CHUNK)
SPAN = 224
GROUP = 48
STEP = 80
HALF_SPAN = SPAN // 2
BACK_START = QUAD - HALF_SPAN

flux_scale = 2.0
prior_weight = 0.1
highest = lax.Precision.HIGHEST
f32 = jnp.float32
bf16 = jnp.bfloat16
MESH = pl.DeviceIdType.MESH


def iota(shape, axis):
    return lax.broadcasted_iota(jnp.int32, shape, axis)


def dot(a, b, dims=((1,), (0,)), precision=None):
    return lax.dot_general(a, b, (dims, ((), ())), precision=precision, preferred_element_type=f32)


def halves(x):
    high = x.astype(bf16)
    return high, (x - high.astype(f32)).astype(bf16)


def dot3(a, b, dims=((1,), (0,))):
    rows = a.shape[0] // 2
    both = dot(a, b[0], dims)
    return both[:rows] + (both[rows:] + dot(a[:rows], b[1], dims))


def wrapped_tile(row, col):
    return lax.rem(row + TILE_COLS, TILE_COLS) * TILE_COLS + lax.rem(col + TILE_COLS, TILE_COLS)


def inside(row, col):
    return (row >= 0) & (row < TILE_COLS) & (col >= 0) & (col < TILE_COLS)


def viewers(tile, band):
    home = lax.rem(tile + TILES // 2, TILES)
    row, col = home // TILE_COLS, lax.rem(home, TILE_COLS)
    found = []
    for far_y in (1, 0):
        for away in FARTHEST_FIRST:
            other = lax.rem(band + away, N_BAND)
            half_y, half_x = other // 2, lax.rem(other, 2)
            for far_x in (1, 0):
                to_row, to_col = row + far_y * (1 - 2 * half_y), col + far_x * (1 - 2 * half_x)
                found.append(
                    (
                        wrapped_tile(to_row, to_col),
                        other,
                        (2 * far_y + far_x) * N_BAND + band,
                        (2 * far_y + far_x) * N_BAND + other,
                        inside(to_row, to_col),
                    )
                )
    return found


def owners(tile, band):
    row, col = tile // TILE_COLS, lax.rem(tile, TILE_COLS)
    half_y, half_x = band // 2, lax.rem(band, 2)
    found = []
    for far_y in (1, 0):
        for away in FARTHEST_FIRST:
            other = lax.rem(band + away, N_BAND)
            for far_x in (1, 0):
                from_row, from_col = row + far_y * (2 * half_y - 1), col + far_x * (2 * half_x - 1)
                holder = lax.rem(wrapped_tile(from_row, from_col) + TILES // 2, TILES)
                far = 2 * far_y + far_x
                found.append(
                    (holder, other, far * N_BAND + other, far * N_BAND + band, inside(from_row, from_col))
                )
    return found


def greet(barrier, callers):
    for other_tile, other_band, _, _, there in callers:

        @pl.when(there)
        def _():
            pl.semaphore_signal(
                barrier, inc=1, device_id=(other_tile, other_band), device_id_type=MESH
            )


def how_many(partners):
    return sum(there.astype(jnp.int32) for _, _, _, _, there in partners)


def parameter_lanes():
    lane = iota((1, LANES), 1)
    source = jnp.where(lane < BANDS + 2, lane, -1)
    source = jnp.where(lane == BANDS + 2, PARAMS - 1, source)
    for j, base in enumerate((WEIGHT, SPREAD_Y, SPREAD_X)):
        here = (lane >= base) & (lane < base + COMPONENTS)
        source = jnp.where(here, BANDS + 2 + 3 * (lane - base) + j, source)
    return (iota((PARAMS, LANES), 0) == source).astype(bf16)


def parameter_columns():
    lane = iota((LANES, LANES), 0)
    target = jnp.where(lane < BANDS + 2, lane, -1)
    target = jnp.where(lane == BANDS + 2, PARAMS - 1, target)
    for j, base in enumerate((WEIGHT, SPREAD_Y, SPREAD_X)):
        here = (lane >= base) & (lane < base + COMPONENTS)
        target = jnp.where(here, BANDS + 2 + 3 * (lane - base) + j, target)
    return (iota((LANES, LANES), 1) == target).astype(bf16)


def thirds_of(x):
    high = x.astype(bf16).astype(f32)
    low = (x - high).astype(bf16).astype(f32)
    return jnp.concatenate([high, low, x - high - low], axis=0).astype(bf16)


def summed(x):
    rows = x.shape[0] // 3
    return x[:rows] + (x[rows : 2 * rows] + x[2 * rows :])


def derived(params):
    raw = summed(dot(thirds_of(params), parameter_lanes()))
    lane = iota(raw.shape, 1)
    is_flux = lane < BANDS
    is_shift = (lane >= BANDS) & (lane < BANDS + 2)
    is_weight = (lane >= WEIGHT) & (lane < WEIGHT + COMPONENTS)
    is_spread = ((lane >= SPREAD_Y) & (lane < SPREAD_Y + COMPONENTS)) | (
        (lane >= SPREAD_X) & (lane < SPREAD_X + COMPONENTS)
    )
    most = jnp.max(jnp.where(is_weight, raw, -jnp.inf), axis=1, keepdims=True)
    power = jnp.where(is_weight, jnp.exp(jnp.where(is_weight, raw - most, 0.0)), 0.0)
    weight = power / jnp.sum(power, axis=1, keepdims=True)
    decay = jnp.exp(-jnp.abs(raw))
    soft = jnp.maximum(raw, 0.0) + jnp.log1p(decay)
    sigmoid = jnp.where(raw >= 0.0, 1.0, decay) / (1.0 + decay)
    curve = jnp.tanh(raw)
    softness = jnp.exp(0.25 * raw[:, BANDS + 2 : BANDS + 3])
    scale = (PATCH / 32.0) * softness
    spread = (0.5 + soft) * scale
    return raw, is_flux, is_shift, is_weight, is_spread, weight, soft, sigmoid, curve, scale, spread


def start_copies(pairs, sems):
    copies = [pltpu.make_async_copy(src, dst, sems.at[i]) for i, (src, dst) in enumerate(pairs)]
    for copy in copies:
        copy.start()
    return copies


def build_tables(taps, conv, back):
    tap, spot = iota((TAPS, COLS), 0), iota((TAPS, COLS), 1)

    def spread_out(x, places):
        return dot(x, (places == spot).astype(bf16))

    def turned(row, rows, shift):
        wide = jnp.broadcast_to(row, (rows, COLS))
        return pltpu.roll(wide, shift, 1, stride=1, stride_axis=0)

    lane = iota((HALF_SPAN, COLS), 1)
    for side in range(2):
        high, low = halves(taps[side])
        ahead = spread_out(high, tap) + spread_out(high, tap + STEP) + spread_out(low, tap + 2 * STEP)
        behind = [spread_out(half, lax.rem(COLS - tap, COLS)) for half in (high, low)]
        for b in range(BANDS):
            conv[side, b * GROUP : (b + 1) * GROUP, :] = turned(ahead[b : b + 1], GROUP, 0).astype(bf16)
            for part in range(2):
                shift = (HALF_SPAN - BACK_START) * part
                near = turned(behind[0][b : b + 1], HALF_SPAN, shift)
                far = turned(behind[0][b : b + 1], HALF_SPAN, shift + HALF_SPAN)
                small = turned(behind[1][b : b + 1], HALF_SPAN, shift)
                both = jnp.where(lane < HALF_SPAN, near, jnp.where(lane < SPAN, far, 0.0))
                small = jnp.where(lane < HALF_SPAN, small, 0.0)
                cols = slice(b * COLS, (b + 1) * COLS)
                back[side, part, :HALF_SPAN, cols] = both.astype(bf16)
                back[side, part, HALF_SPAN:, cols] = small.astype(bf16)


def send_kernel(
    params,
    offsets,
    counts,
    psf_y,
    psf_x,
    background,
    image,
    out,
    conv,
    back,
    prior,
    sky,
    observed,
    theta,
    place,
    taps,
    pixels,
    mine,
    landed,
    load_sem,
    send_sem,
    recv_sem,
):
    tile, band = lax.axis_index("tile"), lax.axis_index("band")
    loads = start_copies(
        (
            (params, theta),
            (offsets, place),
            (psf_y, taps.at[0]),
            (psf_x, taps.at[1]),
            (background, sky),
            (quadrant_of(image, tile, band), pixels),
        ),
        load_sem,
    )
    barrier = pltpu.get_barrier_semaphore()
    greet(barrier, owners(tile, band))
    for load in loads[:2]:
        load.wait()
    raw, is_flux, is_shift, is_weight, is_spread, weight, soft, sigmoid, curve, scale, spread = derived(
        theta[...]
    )
    slot, lane = iota((SRC, LANES), 0), iota((SRC, LANES), 1)
    live = (slot < counts[0]).astype(f32)
    row = jnp.where(is_flux, flux_scale * soft * live, 0.0)
    row = jnp.where(is_shift, (PATCH / 16.0) * curve, row)
    row = jnp.where(is_weight, weight, row)
    row = jnp.where(is_spread, spread, row)
    start = place[...].astype(f32)
    diagonal = iota((SRC, SRC), 0) == iota((SRC, SRC), 1)
    for side in range(2):
        start_side = jnp.sum(jnp.where(diagonal, start[side : side + 1, :], 0.0), axis=1, keepdims=True)
        row = jnp.where(lane == TOP + side, start_side, row)
    row = jnp.where(lane == LIVE, live, row)
    slope = jnp.where(is_flux, sigmoid / soft, 0.0)
    slope = jnp.where(is_shift, (PATCH / 16.0) * (1.0 - curve * curve), slope)
    slope = jnp.where(is_weight, 1.0, slope)
    slope = jnp.where(is_spread, scale * sigmoid, slope)
    mine[...] = row + pltpu.roll(slope, HALVES, 1)

    pl.semaphore_wait(barrier, how_many(viewers(tile, band)))
    copies = []
    for i, (other_tile, other_band, block, _, there) in enumerate(viewers(tile, band)):
        copy = pltpu.make_async_remote_copy(
            src_ref=mine,
            dst_ref=landed.at[block],
            send_sem=send_sem.at[i],
            recv_sem=recv_sem.at[block],
            device_id=(other_tile, other_band),
            device_id_type=MESH,
        )
        copies.append((copy, there))
        pl.when(there)(copy.start)
    for _, _, block, _, there in owners(tile, band):

        @pl.when(jnp.logical_not(there))
        def _():
            landed[block] = jnp.zeros((SRC, LANES), f32)

    for load in loads[2:]:
        load.wait()
    build_tables(taps, conv, back)

    prior[...] = prior_weight * theta[...] * live[:, :PARAMS]
    turn = lax.rem(COLS - lax.rem(band, 2) * (QUAD - COLS // 2), COLS)
    for b in range(BANDS):
        observed[b] = pltpu.roll(pixels[b], turn, 1)[:, :QUAD]

    for i, (other_tile, other_band, block, _, there) in enumerate(reversed(owners(tile, band))):
        copy = pltpu.make_async_remote_copy(
            src_ref=mine,
            dst_ref=landed.at[block],
            send_sem=send_sem.at[i],
            recv_sem=recv_sem.at[block],
            device_id=(other_tile, other_band),
            device_id_type=MESH,
        )
        pl.when(there)(copy.wait_recv)
        out[pl.ds(pl.multiple_of(block * SRC, SRC), SRC), :] = landed[block]
    for copy, there in copies:
        pl.when(there)(copy.wait_send)


def quadrant_of(image, tile, band):
    half_y, half_x = band // 2, lax.rem(band, 2)
    rows = pl.ds(pl.multiple_of(half_y * QUAD, QUAD), QUAD)
    cols = pl.ds(pl.multiple_of(half_x * (COLS // 2), COLS // 2), COLS)
    return image.at[0, :, rows, cols]


def column_comps():
    column = iota((1, COLS), 1)
    place = (column * 5462) >> 16
    return place, iota((16, COLS), 0) == column - COMPONENTS * place


def one_of(values, base):
    mine = column_comps()[1]
    return jnp.sum(jnp.where(mine, values[base : base + 16], 0.0), axis=0, keepdims=True)


def geometry(values, side):
    spread = one_of(values, (SPREAD_Y, SPREAD_X)[side])
    inverse = 1.0 / jnp.where(spread > 0.0, spread, 1.0)
    shift = values[BANDS + side : BANDS + side + 1]
    start = values[TOP + side : TOP + side + 1]
    spot = iota((SPAN, COLS), 0).astype(f32) - (start + float(HALF))
    inside = (spot >= 0.0) & (spot < PATCH)
    ratio = (spot + (0.5 - PATCH / 2.0) - shift) * inverse
    spot = iota((QUAD, COLS), 0).astype(f32) - start
    window = ((spot >= 0.0) & (spot < PATCH)).astype(f32)
    return inverse, inside, ratio, window


def render(values, conv, profiles, factors, c):
    weight = one_of(values, WEIGHT)
    for side in range(2):
        _, inside, ratio, window = geometry(values, side)
        profile = jnp.where(inside, jnp.exp(-0.5 * ratio * ratio), 0.0)
        profiles[c, side] = profile
        high, low = halves(profile)
        for start in range(0, QUAD, GROUP):
            rows = slice(start, start + STEP)
            blank = jnp.zeros((COLS - 3 * STEP, COLS), bf16)
            stack = jnp.concatenate([high[rows], low[rows], high[rows], blank], axis=0)
            factor = dot(conv[side], stack)
            seen = window[start : start + GROUP]
            for b in range(BANDS):
                scale = seen * (weight * values[b : b + 1]) if side == 0 else seen
                high_low = halves(factor[b * GROUP : (b + 1) * GROUP] * scale)
                for half in range(2):
                    put = half * QUAD + start
                    factors[side][c, b, put : put + GROUP] = high_low[half]


def model_of(factors, c, b):
    y_factor, x_factor = factors
    x = (x_factor[c, b, :QUAD], x_factor[c, b, QUAD:])
    return dot3(y_factor[c, b], x, ((1,), (1,)))


def leave(observed, background, model, residual, b):
    left = observed[b] / (background[0:1, b : b + 1] + model) - 1.0
    left = left * (1.0 / (PATCH * PATCH))
    for way, r in enumerate((left, left.T)):
        high_low = halves(r)
        for half in range(2):
            residual[way, b, half * QUAD : (half + 1) * QUAD] = high_low[half]


def pull(values, onehot, back, profiles, factors, residual, stack, c):
    y_factor, x_factor = factors
    mine = column_comps()[1]
    weight = one_of(values, WEIGHT)
    rows = []
    inverse_y, _, ratio_y, window_y = geometry(values, 0)
    inverse_x, _, ratio_x, window_x = geometry(values, 1)
    blank = jnp.zeros((COLS - SPAN, COLS), bf16)
    for b in range(BANDS):
        y = (y_factor[c, b, :QUAD], y_factor[c, b, QUAD:])
        x = (x_factor[c, b, :QUAD], x_factor[c, b, QUAD:])
        along_y = dot3(residual[0, b], x)
        along_x = dot3(residual[1, b], y)
        factor = y[0].astype(f32) + y[1].astype(f32)
        rows.append(jnp.sum(along_y * factor, axis=0, keepdims=True))
        along_y = along_y * (window_y * (weight * values[b : b + 1]))
        along_x = along_x * window_x
        for side, along in enumerate((along_y, along_x)):
            high, low = halves(along)
            for part, start in enumerate((0, BACK_START)):
                here = slice(start, start + HALF_SPAN)
                put = b * COLS
                stack[side, part, put : put + HALF_SPAN] = high[here]
                stack[side, part, put + HALF_SPAN : put + SPAN] = low[here]
                stack[side, part, put + SPAN : put + COLS] = blank
    ds = []
    for side in range(2):
        d = []
        for part in range(2):
            both = dot(back[side, part], stack[side, part])
            d.append(both[:HALF_SPAN] + both[HALF_SPAN:])
        ds.append(jnp.concatenate(d, axis=0))
    by_comp = rows[0] + rows[1] + rows[2] + rows[3] + rows[4]
    spreads = []
    for side, (d, inverse, ratio) in enumerate(((ds[0], inverse_y, ratio_y), (ds[1], inverse_x, ratio_x))):
        first = d * profiles[c, side] * ratio
        rows.append(inverse * jnp.sum(first, axis=0, keepdims=True))
        spreads.append(inverse * jnp.sum(first * ratio, axis=0, keepdims=True))
    pieces = rows + [jnp.zeros((16 - len(rows), COLS), f32)]
    for by in (by_comp, spreads[0], spreads[1]):
        pieces.append(jnp.where(mine, by, 0.0))
    high_low = jnp.concatenate(halves(jnp.concatenate(pieces, axis=0)), axis=0)
    return dot(onehot, high_low, ((1,), (1,)))


def find(data, tile, band):
    row, col = tile // TILE_COLS, lax.rem(tile, TILE_COLS)
    half_y, half_x = band // 2, lax.rem(band, 2)
    slot = iota((SLOTS, LANES), 0)
    lane = iota((SLOTS, LANES), 1)
    far_y, far_x = slot // (SLOTS // 2), lax.rem(slot // (SLOTS // 4), 2)

    def moved(far, half, place):
        origin = jnp.where(far == 0, 0, TILE_SIDE * (2 * half - 1)) - QUAD * half
        beyond = place + 2 * half - 1
        there = (far == 0) | ((beyond >= 0) & (beyond < TILE_COLS))
        return origin.astype(f32), there

    origin_y, there_y = moved(far_y, half_y, row)
    origin_x, there_x = moved(far_x, half_x, col)
    data = data + jnp.where(lane == TOP, origin_y, jnp.where(lane == LEFT, origin_x, 0.0))
    is_place = (lane == TOP) | (lane == LEFT)
    reach = is_place & (data > -PATCH) & (data < QUAD) | (lane == LIVE) & (data > 0.0)
    met = jnp.where(reach & there_y & there_x, 1.0, 0.0).astype(bf16)
    active = jnp.where(dot(met, jnp.ones((LANES, LANES), bf16)) > 2.5, 1.0, 0.0)
    count = jnp.sum(active, axis=0, keepdims=True)

    def chunk_makers():
        before = jnp.where(lane < slot, 1.0, 0.0).astype(bf16)
        order = dot(before, active.astype(bf16))
        order = jnp.where(active > 0.0, order, -1.0)[:, 0:1].astype(jnp.int32)
        place = column_comps()[0]

        def picked(c):
            here = (place < PER_CHUNK) & (order - c * PER_CHUNK == place)
            return jnp.where(here, 1.0, 0.0).astype(bf16)

        thirds = thirds_of(data.T[:HALVES])

        def gathered(c):
            return summed(dot(thirds, picked(c)))

        return picked, gathered

    return count, chunk_makers


def more_kernel(
    slots,
    sky,
    observed,
    conv,
    back,
    rest_model,
    rest_parts,
    profiles,
    y_factor,
    x_factor,
    residual,
    stack,
):
    tile, band = lax.axis_index("tile"), lax.axis_index("band")
    counts, chunk_makers = find(slots[...], tile, band)
    count = counts[0, 0].astype(jnp.int32)

    @pl.when(count > PER_CHUNK)
    def _():
        picked, gathered = chunk_makers()
        factors = (y_factor, x_factor)
        chunks = (count + PER_CHUNK - 1) // PER_CHUNK
        rest_model[...] = jnp.zeros_like(rest_model)
        rest_parts[...] = jnp.zeros_like(rest_parts)

        def add(c, carry):
            render(gathered(c), conv, profiles, factors, c)
            for b in range(BANDS):
                rest_model[b] += model_of(factors, c, b)
            return carry

        lax.fori_loop(1, chunks, add, 0)
        render(gathered(0), conv, profiles, factors, 0)
        for b in range(BANDS):
            model = rest_model[b] + model_of(factors, 0, b)
            leave(observed, sky, model, residual, b)

        def take(c, carry):
            rest_parts[...] += pull(gathered(c), picked(c), back, profiles, factors, residual, stack, c)
            return carry

        lax.fori_loop(1, chunks, take, 0)


def to_parameters(pulled, data):
    lane = iota((SLOTS, LANES), 1)
    is_weight = (lane >= WEIGHT) & (lane < WEIGHT + COMPONENTS)
    is_spread = ((lane >= SPREAD_Y) & (lane < SPREAD_Y + COMPONENTS)) | (
        (lane >= SPREAD_X) & (lane < SPREAD_X + COMPONENTS)
    )
    weight = jnp.where(is_weight, data, 0.0)
    groups = jnp.concatenate(
        [jnp.where(is_weight, pulled, 0.0), jnp.where(is_spread, pulled * data, 0.0)], axis=0
    )
    sums = summed(dot(thirds_of(groups), jnp.ones((LANES, LANES), bf16)))
    slope = jnp.where(lane < HALVES, pltpu.roll(data, HALVES, 1), 0.0)
    by_lane = pulled * slope - weight * sums[:SLOTS]
    by_lane = jnp.where(lane == BANDS + 2, 0.25 * sums[SLOTS:], by_lane)
    return summed(dot(thirds_of(by_lane), parameter_columns()))


def return_kernel(
    slots,
    rest_model,
    rest_parts,
    sky,
    observed,
    conv,
    back,
    prior,
    out,
    profiles,
    y_factor,
    x_factor,
    residual,
    stack,
    parts,
    landed,
    send_sem,
    recv_sem,
):
    tile, band = lax.axis_index("tile"), lax.axis_index("band")
    barrier = pltpu.get_barrier_semaphore()
    greet(barrier, viewers(tile, band))
    factors = (y_factor, x_factor)
    count, chunk_makers = find(slots[...], tile, band)
    picked, gathered = chunk_makers()
    onehot, values = picked(0), gathered(0)
    more = count[:, 0:1] > PER_CHUNK
    render(values, conv, profiles, factors, 0)
    for b in range(BANDS):
        model = model_of(factors, 0, b) + jnp.where(more, rest_model[b], 0.0)
        leave(observed, sky, model, residual, b)
    pulled = pull(values, onehot, back, profiles, factors, residual, stack, 0)
    pulled = pulled + jnp.where(more, rest_parts[...], 0.0)
    parts[...] = to_parameters(pulled + pltpu.roll(pulled, HALVES, 1), slots[...])

    pl.semaphore_wait(barrier, how_many(owners(tile, band)))
    copies = []
    for i, (other_tile, other_band, block, answer, there) in enumerate(owners(tile, band)):
        copy = pltpu.make_async_remote_copy(
            src_ref=parts.at[pl.ds(pl.multiple_of(block * SRC, SRC), SRC), :],
            dst_ref=landed.at[answer],
            send_sem=send_sem.at[i],
            recv_sem=recv_sem.at[answer],
            device_id=(other_tile, other_band),
            device_id_type=MESH,
        )
        copies.append((copy, there))
        pl.when(there)(copy.start)
    for _, _, _, answer, there in viewers(tile, band):

        @pl.when(jnp.logical_not(there))
        def _():
            landed[answer] = jnp.zeros((SRC, LANES), f32)

    total = jnp.zeros((SRC, LANES), f32)
    for i, (other_tile, other_band, _, answer, there) in enumerate(reversed(viewers(tile, band))):
        copy = pltpu.make_async_remote_copy(
            src_ref=parts.at[0:SRC, :],
            dst_ref=landed.at[answer],
            send_sem=send_sem.at[i],
            recv_sem=recv_sem.at[answer],
            device_id=(other_tile, other_band),
            device_id_type=MESH,
        )
        pl.when(there)(copy.wait_recv)
        total = total + landed[answer]
    out[...] = total[:, :PARAMS] - prior[...]
    for copy, there in copies:
        pl.when(there)(copy.wait_send)


def vmem(count):
    return [pl.BlockSpec(memory_space=pltpu.VMEM)] * count


def hbm(count):
    return [pl.BlockSpec(memory_space=pltpu.HBM)] * count


def work_space(chunks):
    return [
        pltpu.VMEM((chunks, 2, SPAN, COLS), f32),
        pltpu.VMEM((chunks, BANDS, 2 * QUAD, COLS), bf16),
        pltpu.VMEM((chunks, BANDS, 2 * QUAD, COLS), bf16),
        pltpu.VMEM((2, BANDS, 2 * QUAD, QUAD), bf16),
        pltpu.VMEM((2, 2, BANDS * COLS, COLS), bf16),
    ]


def shape(*dims, kind=f32):
    return jax.ShapeDtypeStruct(dims, kind)


def body(params, offsets, counts, image, background, psf_y, psf_x):
    smem = pl.BlockSpec(memory_space=pltpu.SMEM)
    params, offsets, image, background, psf_y, psf_x = (
        pltpu.with_memory_space_constraint(x, pltpu.HBM)
        for x in (params, offsets.T, image, background, psf_y, psf_x)
    )
    partners = [pltpu.SemaphoreType.DMA((PARTNERS,))] * 2
    slots, conv, back, prior, sky, observed = pl.pallas_call(
        send_kernel,
        out_shape=[shape(SLOTS, LANES)]
        + [shape(2, BANDS * GROUP, COLS, kind=bf16), shape(2, 2, SPAN, BANDS * COLS, kind=bf16)]
        + [shape(SRC, PARAMS), shape(1, BANDS), shape(BANDS, QUAD, QUAD)],
        in_specs=hbm(2) + [smem] + hbm(4),
        out_specs=vmem(6),
        scratch_shapes=[
            pltpu.VMEM((SRC, PARAMS), f32),
            pltpu.VMEM((2, SRC), jnp.int32),
            pltpu.VMEM((2, BANDS, TAPS), f32),
            pltpu.VMEM((BANDS, QUAD, COLS), f32),
            pltpu.VMEM((SRC, LANES), f32),
            pltpu.VMEM((PARTNERS, SRC, LANES), f32),
            pltpu.SemaphoreType.DMA((6,)),
        ]
        + partners,
        compiler_params=pltpu.CompilerParams(
            collective_id=0, has_side_effects=True, vmem_limit_bytes=16 * 1024 * 1024
        ),
        name="send_slots",
    )(params, offsets, counts, psf_y, psf_x, background, image)
    rest_model, rest_parts = pl.pallas_call(
        more_kernel,
        out_shape=[shape(BANDS, QUAD, QUAD), shape(SLOTS, LANES)],
        in_specs=vmem(5),
        out_specs=vmem(2),
        scratch_shapes=work_space(CHUNKS),
        compiler_params=pltpu.CompilerParams(vmem_limit_bytes=40 * 1024 * 1024),
        name="more_sources",
    )(slots, sky, observed, conv, back)
    return pl.pallas_call(
        return_kernel,
        out_shape=shape(SRC, PARAMS),
        in_specs=vmem(8),
        out_specs=vmem(1)[0],
        scratch_shapes=work_space(1)
        + [
            pltpu.VMEM((SLOTS, LANES), f32),
            pltpu.VMEM((PARTNERS, SRC, LANES), f32),
        ]
        + partners,
        compiler_params=pltpu.CompilerParams(
            collective_id=1, has_side_effects=True, vmem_limit_bytes=24 * 1024 * 1024
        ),
        name="return_parts",
    )(
        slots, rest_model, rest_parts, sky, observed, conv, back, prior
    )


def solution(mesh):
    placed = (
        P(("tile", "band"), None),
        P(("tile", "band"), None),
        P(("tile", "band")),
        P("tile", None, None, None),
        P("tile", None),
        P(),
        P(),
    )
    return jax.shard_map(
        body, mesh=mesh, in_specs=placed, out_specs=P(("tile", "band"), None), check_vma=False
    )
```

```python
import functools

import jax
import jax.numpy as jnp
from jax import lax
from jax.experimental import pallas as pl
from jax.experimental.pallas import tpu as pltpu
from jax.sharding import PartitionSpec as P

BANDS = 5
COMPONENTS = 12
PARAMS = 44
PATCH = 64
TAPS = 25
HALF = TAPS // 2
TILE_COLS = 8
TILE_SIDE = 384
QUAD = TILE_SIDE // 2
SRC = 8
TILES = 64
N_BAND = 4
PARTNERS = 16
SLOTS = PARTNERS * SRC
LANES = 128

TOP, LEFT, LIVE = 8, 9, 10
WEIGHT, SPREAD_Y, SPREAD_X = 16, 32, 48
HALVES = 64

PER_CHUNK = 21
COLS = 256
CHUNKS = -(-SLOTS // PER_CHUNK)
SPAN = 224
GROUP = 48
STEP = 80
HALF_SPAN = SPAN // 2
BACK_START = QUAD - HALF_SPAN

flux_scale = 2.0
prior_weight = 0.1
highest = lax.Precision.HIGHEST
f32 = jnp.float32
bf16 = jnp.bfloat16
MESH = pl.DeviceIdType.MESH


def iota(shape, axis):
    return lax.broadcasted_iota(jnp.int32, shape, axis)


def dot(a, b, dims=((1,), (0,)), precision=None):
    return lax.dot_general(a, b, (dims, ((), ())), precision=precision, preferred_element_type=f32)


def halves(x):
    high = x.astype(bf16)
    return high, (x - high.astype(f32)).astype(bf16)


def dot3(a, b, dims=((1,), (0,))):
    rows = a.shape[0] // 2
    both = dot(a, b[0], dims)
    return both[:rows] + (both[rows:] + dot(a[:rows], b[1], dims))


def wrapped_tile(row, col):
    return lax.rem(row + TILE_COLS, TILE_COLS) * TILE_COLS + lax.rem(col + TILE_COLS, TILE_COLS)


def inside(row, col):
    return (row >= 0) & (row < TILE_COLS) & (col >= 0) & (col < TILE_COLS)


def viewers(tile, band):
    home = lax.rem(tile + TILES // 2, TILES)
    row, col = home // TILE_COLS, lax.rem(home, TILE_COLS)
    found = []
    for step_y, half_y in ((1, 0), (-1, 1), (0, 0), (0, 1)):
        for step_x, half_x in ((1, 0), (-1, 1), (0, 0), (0, 1)):
            far = 2 * abs(step_y) + abs(step_x)
            answer = (2 * abs(step_y) + half_y) * 4 + 2 * abs(step_x) + half_x
            to_row, to_col = row + step_y, col + step_x
            found.append(
                (
                    wrapped_tile(to_row, to_col),
                    2 * half_y + half_x,
                    far * N_BAND + band,
                    answer,
                    inside(to_row, to_col),
                )
            )
    return found


def owners(tile, band):
    row, col = tile // TILE_COLS, lax.rem(tile, TILE_COLS)
    half_y, half_x = band // 2, lax.rem(band, 2)
    found = []
    for far_y in (1, 0):
        for far_x in (1, 0):
            from_row, from_col = row + far_y * (2 * half_y - 1), col + far_x * (2 * half_x - 1)
            holder = lax.rem(wrapped_tile(from_row, from_col) + TILES // 2, TILES)
            answer = (2 * far_y + half_y) * 4 + 2 * far_x + half_x
            for other in range(N_BAND):
                block = (2 * far_y + far_x) * N_BAND + other
                found.append((holder, other, block, answer, inside(from_row, from_col)))
    return found


def greet(barrier, callers):
    for other_tile, other_band, _, _, there in callers:

        @pl.when(there)
        def _():
            pl.semaphore_signal(
                barrier, inc=1, device_id=(other_tile, other_band), device_id_type=MESH
            )


def how_many(partners):
    return sum(there.astype(jnp.int32) for _, _, _, _, there in partners)


def parameter_lanes():
    lane = iota((1, LANES), 1)
    source = jnp.where(lane < BANDS + 2, lane, -1)
    source = jnp.where(lane == BANDS + 2, PARAMS - 1, source)
    for j, base in enumerate((WEIGHT, SPREAD_Y, SPREAD_X)):
        here = (lane >= base) & (lane < base + COMPONENTS)
        source = jnp.where(here, BANDS + 2 + 3 * (lane - base) + j, source)
    return (iota((PARAMS, LANES), 0) == source).astype(bf16)


def parameter_columns():
    lane = iota((LANES, LANES), 0)
    target = jnp.where(lane < BANDS + 2, lane, -1)
    target = jnp.where(lane == BANDS + 2, PARAMS - 1, target)
    for j, base in enumerate((WEIGHT, SPREAD_Y, SPREAD_X)):
        here = (lane >= base) & (lane < base + COMPONENTS)
        target = jnp.where(here, BANDS + 2 + 3 * (lane - base) + j, target)
    return (iota((LANES, LANES), 1) == target).astype(bf16)


def thirds_of(x):
    high = x.astype(bf16).astype(f32)
    low = (x - high).astype(bf16).astype(f32)
    return jnp.concatenate([high, low, x - high - low], axis=0).astype(bf16)


def summed(x):
    rows = x.shape[0] // 3
    return x[:rows] + (x[rows : 2 * rows] + x[2 * rows :])


def derived(params):
    raw = summed(dot(thirds_of(params), parameter_lanes()))
    lane = iota(raw.shape, 1)
    is_flux = lane < BANDS
    is_shift = (lane >= BANDS) & (lane < BANDS + 2)
    is_weight = (lane >= WEIGHT) & (lane < WEIGHT + COMPONENTS)
    is_spread = ((lane >= SPREAD_Y) & (lane < SPREAD_Y + COMPONENTS)) | (
        (lane >= SPREAD_X) & (lane < SPREAD_X + COMPONENTS)
    )
    most = jnp.max(jnp.where(is_weight, raw, -jnp.inf), axis=1, keepdims=True)
    power = jnp.where(is_weight, jnp.exp(jnp.where(is_weight, raw - most, 0.0)), 0.0)
    weight = power / jnp.sum(power, axis=1, keepdims=True)
    decay = jnp.exp(-jnp.abs(raw))
    soft = jnp.maximum(raw, 0.0) + jnp.log1p(decay)
    sigmoid = jnp.where(raw >= 0.0, 1.0, decay) / (1.0 + decay)
    curve = jnp.tanh(raw)
    softness = jnp.exp(0.25 * raw[:, BANDS + 2 : BANDS + 3])
    scale = (PATCH / 32.0) * softness
    spread = (0.5 + soft) * scale
    return raw, is_flux, is_shift, is_weight, is_spread, weight, soft, sigmoid, curve, scale, spread


def start_copies(pairs, sems):
    copies = [pltpu.make_async_copy(src, dst, sems.at[i]) for i, (src, dst) in enumerate(pairs)]
    for copy in copies:
        copy.start()
    return copies


def build_tables(taps, conv, back):
    tap, spot = iota((TAPS, COLS), 0), iota((TAPS, COLS), 1)

    def spread_out(x, places):
        return dot(x, (places == spot).astype(bf16))

    def turned(row, rows, shift):
        wide = jnp.broadcast_to(row, (rows, COLS))
        return pltpu.roll(wide, shift, 1, stride=1, stride_axis=0)

    lane = iota((HALF_SPAN, COLS), 1)
    for side in range(2):
        high, low = halves(taps[side])
        ahead = spread_out(high, tap) + spread_out(high, tap + STEP) + spread_out(low, tap + 2 * STEP)
        behind = [spread_out(half, lax.rem(COLS - tap, COLS)) for half in (high, low)]
        for b in range(BANDS):
            conv[side, b * GROUP : (b + 1) * GROUP, :] = turned(ahead[b : b + 1], GROUP, 0).astype(bf16)
            for part in range(2):
                shift = (HALF_SPAN - BACK_START) * part
                near = turned(behind[0][b : b + 1], HALF_SPAN, shift)
                far = turned(behind[0][b : b + 1], HALF_SPAN, shift + HALF_SPAN)
                small = turned(behind[1][b : b + 1], HALF_SPAN, shift)
                both = jnp.where(lane < HALF_SPAN, near, jnp.where(lane < SPAN, far, 0.0))
                small = jnp.where(lane < HALF_SPAN, small, 0.0)
                cols = slice(b * COLS, (b + 1) * COLS)
                back[side, part, :HALF_SPAN, cols] = both.astype(bf16)
                back[side, part, HALF_SPAN:, cols] = small.astype(bf16)


def send_kernel(
    params,
    offsets,
    counts,
    psf_y,
    psf_x,
    background,
    image,
    out,
    conv,
    back,
    prior,
    sky,
    observed,
    theta,
    place,
    taps,
    pixels,
    mine,
    landed,
    load_sem,
    send_sem,
    recv_sem,
):
    tile, band = lax.axis_index("tile"), lax.axis_index("band")
    loads = start_copies(
        (
            (params, theta),
            (offsets, place),
            (psf_y, taps.at[0]),
            (psf_x, taps.at[1]),
            (background, sky),
        ),
        load_sem,
    )
    barrier = pltpu.get_barrier_semaphore()
    greet(barrier, owners(tile, band))
    for load in loads[:2]:
        load.wait()
    raw, is_flux, is_shift, is_weight, is_spread, weight, soft, sigmoid, curve, scale, spread = derived(
        theta[...]
    )
    slot, lane = iota((SRC, LANES), 0), iota((SRC, LANES), 1)
    live = (slot < counts[0]).astype(f32)
    row = jnp.where(is_flux, flux_scale * soft * live, 0.0)
    row = jnp.where(is_shift, (PATCH / 16.0) * curve, row)
    row = jnp.where(is_weight, weight, row)
    row = jnp.where(is_spread, spread, row)
    start = place[...].astype(f32)
    diagonal = iota((SRC, SRC), 0) == iota((SRC, SRC), 1)
    for side in range(2):
        start_side = jnp.sum(jnp.where(diagonal, start[side : side + 1, :], 0.0), axis=1, keepdims=True)
        row = jnp.where(lane == TOP + side, start_side, row)
    row = jnp.where(lane == LIVE, live, row)
    slope = jnp.where(is_flux, sigmoid / soft, 0.0)
    slope = jnp.where(is_shift, (PATCH / 16.0) * (1.0 - curve * curve), slope)
    slope = jnp.where(is_weight, 1.0, slope)
    slope = jnp.where(is_spread, scale * sigmoid, slope)
    mine[...] = row + pltpu.roll(slope, HALVES, 1)

    pl.semaphore_wait(barrier, how_many(viewers(tile, band)))
    copies = []
    for i, (other_tile, other_band, block, _, there) in enumerate(viewers(tile, band)):
        copy = pltpu.make_async_remote_copy(
            src_ref=mine,
            dst_ref=landed.at[block],
            send_sem=send_sem.at[i],
            recv_sem=recv_sem.at[block],
            device_id=(other_tile, other_band),
            device_id_type=MESH,
        )
        copies.append((copy, there))
        pl.when(there)(copy.start)
    for _, _, block, _, there in owners(tile, band):

        @pl.when(jnp.logical_not(there))
        def _():
            landed[block] = jnp.zeros((SRC, LANES), f32)

    picture = pltpu.make_async_copy(quadrant_of(image, tile, band), pixels, load_sem.at[5])
    picture.start()
    for load in loads[2:]:
        load.wait()
    build_tables(taps, conv, back)

    prior[...] = prior_weight * theta[...] * live[:, :PARAMS]
    picture.wait()
    turn = lax.rem(COLS - lax.rem(band, 2) * (QUAD - COLS // 2), COLS)
    for b in range(BANDS):
        observed[b] = pltpu.roll(pixels[b], turn, 1)[:, :QUAD]

    for i, (other_tile, other_band, block, _, there) in enumerate(reversed(owners(tile, band))):
        copy = pltpu.make_async_remote_copy(
            src_ref=mine,
            dst_ref=landed.at[block],
            send_sem=send_sem.at[i],
            recv_sem=recv_sem.at[block],
            device_id=(other_tile, other_band),
            device_id_type=MESH,
        )
        pl.when(there)(copy.wait_recv)
        out[block * SRC : (block + 1) * SRC, :] = landed[block]
    for copy, there in copies:
        pl.when(there)(copy.wait_send)


def quadrant_of(image, tile, band):
    half_y, half_x = band // 2, lax.rem(band, 2)
    rows = pl.ds(pl.multiple_of(half_y * QUAD, QUAD), QUAD)
    cols = pl.ds(pl.multiple_of(half_x * (COLS // 2), COLS // 2), COLS)
    return image.at[0, :, rows, cols]


def column_comps():
    column = iota((1, COLS), 1)
    place = (column * 5462) >> 16
    return place, iota((16, COLS), 0) == column - COMPONENTS * place


def one_of(values, base):
    mine = column_comps()[1]
    return jnp.sum(jnp.where(mine, values[base : base + 16], 0.0), axis=0, keepdims=True)


def geometry(values, side):
    spread = one_of(values, (SPREAD_Y, SPREAD_X)[side])
    inverse = 1.0 / jnp.where(spread > 0.0, spread, 1.0)
    shift = values[BANDS + side : BANDS + side + 1]
    start = values[TOP + side : TOP + side + 1]
    spot = iota((SPAN, COLS), 0).astype(f32) - (start + float(HALF))
    inside = (spot >= 0.0) & (spot < PATCH)
    ratio = (spot + (0.5 - PATCH / 2.0) - shift) * inverse
    spot = iota((QUAD, COLS), 0).astype(f32) - start
    window = ((spot >= 0.0) & (spot < PATCH)).astype(f32)
    return inverse, inside, ratio, window


def render(values, conv, profiles, factors, c):
    weight = one_of(values, WEIGHT)
    for side in range(2):
        _, inside, ratio, window = geometry(values, side)
        profile = jnp.where(inside, jnp.exp(-0.5 * ratio * ratio), 0.0)
        profiles[c, side] = profile
        high, low = halves(profile)
        for start in range(0, QUAD, GROUP):
            rows = slice(start, start + STEP)
            blank = jnp.zeros((COLS - 3 * STEP, COLS), bf16)
            stack = jnp.concatenate([high[rows], low[rows], high[rows], blank], axis=0)
            factor = dot(conv[side], stack)
            seen = window[start : start + GROUP]
            for b in range(BANDS):
                scale = seen * (weight * values[b : b + 1]) if side == 0 else seen
                high_low = halves(factor[b * GROUP : (b + 1) * GROUP] * scale)
                for half in range(2):
                    put = half * QUAD + start
                    factors[side][c, b, put : put + GROUP] = high_low[half]


def model_of(factors, c, b):
    y_factor, x_factor = factors
    x = (x_factor[c, b, :QUAD], x_factor[c, b, QUAD:])
    return dot3(y_factor[c, b], x, ((1,), (1,)))


def leave(observed, background, model, residual, b):
    left = observed[b] / (background[0:1, b : b + 1] + model) - 1.0
    left = left * (1.0 / (PATCH * PATCH))
    for way, r in enumerate((left, left.T)):
        high_low = halves(r)
        for half in range(2):
            residual[way, b, half * QUAD : (half + 1) * QUAD] = high_low[half]


def pull(values, onehot, back, profiles, factors, residual, stack, c):
    y_factor, x_factor = factors
    mine = column_comps()[1]
    weight = one_of(values, WEIGHT)
    rows = []
    inverse_y, _, ratio_y, window_y = geometry(values, 0)
    inverse_x, _, ratio_x, window_x = geometry(values, 1)
    blank = jnp.zeros((COLS - SPAN, COLS), bf16)
    for b in range(BANDS):
        y = (y_factor[c, b, :QUAD], y_factor[c, b, QUAD:])
        x = (x_factor[c, b, :QUAD], x_factor[c, b, QUAD:])
        along_y = dot3(residual[0, b], x)
        along_x = dot3(residual[1, b], y)
        factor = y[0].astype(f32) + y[1].astype(f32)
        rows.append(jnp.sum(along_y * factor, axis=0, keepdims=True))
        along_y = along_y * (window_y * (weight * values[b : b + 1]))
        along_x = along_x * window_x
        for side, along in enumerate((along_y, along_x)):
            high, low = halves(along)
            for part, start in enumerate((0, BACK_START)):
                here = slice(start, start + HALF_SPAN)
                put = b * COLS
                stack[side, part, put : put + HALF_SPAN] = high[here]
                stack[side, part, put + HALF_SPAN : put + SPAN] = low[here]
                stack[side, part, put + SPAN : put + COLS] = blank
    ds = []
    for side in range(2):
        d = []
        for part in range(2):
            both = dot(back[side, part], stack[side, part])
            d.append(both[:HALF_SPAN] + both[HALF_SPAN:])
        ds.append(jnp.concatenate(d, axis=0))
    by_comp = rows[0] + rows[1] + rows[2] + rows[3] + rows[4]
    spreads = []
    for side, (d, inverse, ratio) in enumerate(((ds[0], inverse_y, ratio_y), (ds[1], inverse_x, ratio_x))):
        first = d * profiles[c, side] * ratio
        rows.append(inverse * jnp.sum(first, axis=0, keepdims=True))
        spreads.append(inverse * jnp.sum(first * ratio, axis=0, keepdims=True))
    pieces = rows + [jnp.zeros((16 - len(rows), COLS), f32)]
    for by in (by_comp, spreads[0], spreads[1]):
        pieces.append(jnp.where(mine, by, 0.0))
    high_low = jnp.concatenate(halves(jnp.concatenate(pieces, axis=0)), axis=0)
    return dot(onehot, high_low, ((1,), (1,)))


def find(data, tile, band):
    row, col = tile // TILE_COLS, lax.rem(tile, TILE_COLS)
    half_y, half_x = band // 2, lax.rem(band, 2)
    slot = iota((SLOTS, LANES), 0)
    lane = iota((SLOTS, LANES), 1)
    far_y, far_x = slot // (SLOTS // 2), lax.rem(slot // (SLOTS // 4), 2)

    def moved(far, half, place):
        origin = jnp.where(far == 0, 0, TILE_SIDE * (2 * half - 1)) - QUAD * half
        beyond = place + 2 * half - 1
        there = (far == 0) | ((beyond >= 0) & (beyond < TILE_COLS))
        return origin.astype(f32), there

    origin_y, there_y = moved(far_y, half_y, row)
    origin_x, there_x = moved(far_x, half_x, col)
    data = data + jnp.where(lane == TOP, origin_y, jnp.where(lane == LEFT, origin_x, 0.0))
    is_place = (lane == TOP) | (lane == LEFT)
    reach = is_place & (data > -PATCH) & (data < QUAD) | (lane == LIVE) & (data > 0.0)
    met = jnp.where(reach & there_y & there_x, 1.0, 0.0).astype(bf16)
    active = jnp.where(dot(met, jnp.ones((LANES, LANES), bf16)) > 2.5, 1.0, 0.0)
    count = jnp.sum(active, axis=0, keepdims=True)

    def chunk_makers():
        before = jnp.where(lane < slot, 1.0, 0.0).astype(bf16)
        order = dot(before, active.astype(bf16))
        order = jnp.where(active > 0.0, order, -1.0)[:, 0:1].astype(jnp.int32)
        place = column_comps()[0]

        def picked(c):
            here = (place < PER_CHUNK) & (order - c * PER_CHUNK == place)
            return jnp.where(here, 1.0, 0.0).astype(bf16)

        thirds = thirds_of(data.T[:HALVES])

        def gathered(c):
            return summed(dot(thirds, picked(c)))

        return picked, gathered

    return count, chunk_makers


def more_kernel(
    slots,
    sky,
    observed,
    conv,
    back,
    rest_model,
    rest_parts,
    profiles,
    y_factor,
    x_factor,
    residual,
    stack,
):
    tile, band = lax.axis_index("tile"), lax.axis_index("band")
    counts, chunk_makers = find(slots[...], tile, band)
    count = counts[0, 0].astype(jnp.int32)

    @pl.when(count > PER_CHUNK)
    def _():
        picked, gathered = chunk_makers()
        factors = (y_factor, x_factor)
        chunks = (count + PER_CHUNK - 1) // PER_CHUNK
        rest_model[...] = jnp.zeros_like(rest_model)
        rest_parts[...] = jnp.zeros_like(rest_parts)

        def add(c, carry):
            render(gathered(c), conv, profiles, factors, c)
            for b in range(BANDS):
                rest_model[b] += model_of(factors, c, b)
            return carry

        lax.fori_loop(1, chunks, add, 0)
        render(gathered(0), conv, profiles, factors, 0)
        for b in range(BANDS):
            model = rest_model[b] + model_of(factors, 0, b)
            leave(observed, sky, model, residual, b)

        def take(c, carry):
            rest_parts[...] += pull(gathered(c), picked(c), back, profiles, factors, residual, stack, c)
            return carry

        lax.fori_loop(1, chunks, take, 0)


def to_parameters(pulled, data):
    lane = iota((SLOTS, LANES), 1)
    is_weight = (lane >= WEIGHT) & (lane < WEIGHT + COMPONENTS)
    is_spread = ((lane >= SPREAD_Y) & (lane < SPREAD_Y + COMPONENTS)) | (
        (lane >= SPREAD_X) & (lane < SPREAD_X + COMPONENTS)
    )
    weight = jnp.where(is_weight, data, 0.0)
    groups = jnp.concatenate(
        [jnp.where(is_weight, pulled, 0.0), jnp.where(is_spread, pulled * data, 0.0)], axis=0
    )
    sums = summed(dot(thirds_of(groups), jnp.ones((LANES, LANES), bf16)))
    slope = jnp.where(lane < HALVES, pltpu.roll(data, HALVES, 1), 0.0)
    by_lane = pulled * slope - weight * sums[:SLOTS]
    by_lane = jnp.where(lane == BANDS + 2, 0.25 * sums[SLOTS:], by_lane)
    return summed(dot(thirds_of(by_lane), parameter_columns()))


def return_kernel(
    slots,
    rest_model,
    rest_parts,
    sky,
    observed,
    conv,
    back,
    prior,
    out,
    profiles,
    y_factor,
    x_factor,
    residual,
    stack,
    parts,
    landed,
    send_sem,
    recv_sem,
):
    tile, band = lax.axis_index("tile"), lax.axis_index("band")
    barrier = pltpu.get_barrier_semaphore()
    greet(barrier, viewers(tile, band))
    factors = (y_factor, x_factor)
    count, chunk_makers = find(slots[...], tile, band)
    picked, gathered = chunk_makers()
    onehot, values = picked(0), gathered(0)
    more = count[:, 0:1] > PER_CHUNK
    render(values, conv, profiles, factors, 0)
    for b in range(BANDS):
        model = model_of(factors, 0, b) + jnp.where(more, rest_model[b], 0.0)
        leave(observed, sky, model, residual, b)
    pulled = pull(values, onehot, back, profiles, factors, residual, stack, 0)
    pulled = pulled + jnp.where(more, rest_parts[...], 0.0)
    parts[...] = to_parameters(pulled + pltpu.roll(pulled, HALVES, 1), slots[...])

    pl.semaphore_wait(barrier, how_many(owners(tile, band)))
    copies = []
    for i, (other_tile, other_band, block, answer, there) in enumerate(owners(tile, band)):
        copy = pltpu.make_async_remote_copy(
            src_ref=parts.at[block * SRC : (block + 1) * SRC, :],
            dst_ref=landed.at[answer],
            send_sem=send_sem.at[i],
            recv_sem=recv_sem.at[answer],
            device_id=(other_tile, other_band),
            device_id_type=MESH,
        )
        copies.append((copy, there))
        pl.when(there)(copy.start)
    for _, _, _, answer, there in viewers(tile, band):

        @pl.when(jnp.logical_not(there))
        def _():
            landed[answer] = jnp.zeros((SRC, LANES), f32)

    total = jnp.zeros((SRC, LANES), f32)
    for i, (other_tile, other_band, _, answer, there) in enumerate(reversed(viewers(tile, band))):
        copy = pltpu.make_async_remote_copy(
            src_ref=parts.at[0:SRC, :],
            dst_ref=landed.at[answer],
            send_sem=send_sem.at[i],
            recv_sem=recv_sem.at[answer],
            device_id=(other_tile, other_band),
            device_id_type=MESH,
        )
        pl.when(there)(copy.wait_recv)
        total = total + landed[answer]
    out[...] = total[:, :PARAMS] - prior[...]
    for copy, there in copies:
        pl.when(there)(copy.wait_send)


def vmem(count):
    return [pl.BlockSpec(memory_space=pltpu.VMEM)] * count


def hbm(count):
    return [pl.BlockSpec(memory_space=pltpu.HBM)] * count


def work_space(chunks):
    return [
        pltpu.VMEM((chunks, 2, SPAN, COLS), f32),
        pltpu.VMEM((chunks, BANDS, 2 * QUAD, COLS), bf16),
        pltpu.VMEM((chunks, BANDS, 2 * QUAD, COLS), bf16),
        pltpu.VMEM((2, BANDS, 2 * QUAD, QUAD), bf16),
        pltpu.VMEM((2, 2, BANDS * COLS, COLS), bf16),
    ]


def shape(*dims, kind=f32):
    return jax.ShapeDtypeStruct(dims, kind)


def body(params, offsets, counts, image, background, psf_y, psf_x):
    smem = pl.BlockSpec(memory_space=pltpu.SMEM)
    params, offsets, image, background, psf_y, psf_x = (
        pltpu.with_memory_space_constraint(x, pltpu.HBM)
        for x in (params, offsets.T, image, background, psf_y, psf_x)
    )
    partners = [pltpu.SemaphoreType.DMA((PARTNERS,))] * 2
    slots, conv, back, prior, sky, observed = pl.pallas_call(
        send_kernel,
        out_shape=[shape(SLOTS, LANES)]
        + [shape(2, BANDS * GROUP, COLS, kind=bf16), shape(2, 2, SPAN, BANDS * COLS, kind=bf16)]
        + [shape(SRC, PARAMS), shape(1, BANDS), shape(BANDS, QUAD, QUAD)],
        in_specs=hbm(2) + [smem] + hbm(4),
        out_specs=vmem(6),
        scratch_shapes=[
            pltpu.VMEM((SRC, PARAMS), f32),
            pltpu.VMEM((2, SRC), jnp.int32),
            pltpu.VMEM((2, BANDS, TAPS), f32),
            pltpu.VMEM((BANDS, QUAD, COLS), f32),
            pltpu.VMEM((SRC, LANES), f32),
            pltpu.VMEM((PARTNERS, SRC, LANES), f32),
            pltpu.SemaphoreType.DMA((6,)),
        ]
        + partners,
        compiler_params=pltpu.CompilerParams(
            collective_id=0, has_side_effects=True, vmem_limit_bytes=16 * 1024 * 1024
        ),
        name="send_slots",
    )(params, offsets, counts, psf_y, psf_x, background, image)
    rest_model, rest_parts = pl.pallas_call(
        more_kernel,
        out_shape=[shape(BANDS, QUAD, QUAD), shape(SLOTS, LANES)],
        in_specs=vmem(5),
        out_specs=vmem(2),
        scratch_shapes=work_space(CHUNKS),
        compiler_params=pltpu.CompilerParams(vmem_limit_bytes=40 * 1024 * 1024),
        name="more_sources",
    )(slots, sky, observed, conv, back)
    return pl.pallas_call(
        return_kernel,
        out_shape=shape(SRC, PARAMS),
        in_specs=vmem(8),
        out_specs=vmem(1)[0],
        scratch_shapes=work_space(1)
        + [
            pltpu.VMEM((SLOTS, LANES), f32),
            pltpu.VMEM((PARTNERS, SRC, LANES), f32),
        ]
        + partners,
        compiler_params=pltpu.CompilerParams(
            collective_id=1, has_side_effects=True, vmem_limit_bytes=24 * 1024 * 1024
        ),
        name="return_parts",
    )(
        slots, rest_model, rest_parts, sky, observed, conv, back, prior
    )


def solution(mesh):
    placed = (
        P(("tile", "band"), None),
        P(("tile", "band"), None),
        P(("tile", "band")),
        P("tile", None, None, None),
        P("tile", None),
        P(),
        P(),
    )
    return jax.shard_map(
        body, mesh=mesh, in_specs=placed, out_specs=P(("tile", "band"), None), check_vma=False
    )
```
